32 devices in a mesh: dp: 4 (over x, core), zero: 2 (over y), tensor: 4 (over z).
Axes of the slice: x: 2, y: 2, z: 4, core: 2. Of those that a mesh axis runs over, the one named last changes fastest.
Arguments:
- inputs: bfloat16 [7168, 2304], P(('dp', 'zero')), may hold values from -6 to 6
- cotangent: bfloat16 [7168, 2304], P(('dp', 'zero')), may hold values from -6 to 6
- segment: int32 [7168], P(('dp', 'zero')), may hold values from 0 to 7167, as said below
- query_weight: float32 [2304, 2048], P(('dp', 'zero'), 'tensor'), may hold values from -0.125 to 0.125
- key_weight: float32 [2304, 1024], P(('dp', 'zero'), 'tensor'), may hold values from -0.125 to 0.125
- value_weight: float32 [2304, 1024], P(('dp', 'zero'), 'tensor'), may hold values from -0.125 to 0.125
- out_weight: float32 [2048, 2304], P('tensor', ('dp', 'zero')), may hold values from -0.125 to 0.125
- gate_weight: float32 [2304, 9216], P(('dp', 'zero'), 'tensor'), may hold values from -0.125 to 0.125
- up_weight: float32 [2304, 9216], P(('dp', 'zero'), 'tensor'), may hold values from -0.125 to 0.125
- down_weight: float32 [9216, 2304], P('tensor', ('dp', 'zero')), may hold values from -0.0625 to 0.0625
- norm_gains: float32 [4, 2304], P(None, ('dp', 'zero')), may hold values from 0.25 to 1.75
- query_mean: float32 [2304, 2048], P(('dp', 'zero'), 'tensor')
- key_mean: float32 [2304, 1024], P(('dp', 'zero'), 'tensor')
- value_mean: float32 [2304, 1024], P(('dp', 'zero'), 'tensor')
- out_mean: float32 [2048, 2304], P('tensor', ('dp', 'zero'))
- gate_mean: float32 [2304, 9216], P(('dp', 'zero'), 'tensor')
- up_mean: float32 [2304, 9216], P(('dp', 'zero'), 'tensor')
- down_mean: float32 [9216, 2304], P('tensor', ('dp', 'zero'))
- gains_mean: float32 [4, 2304], P(None, ('dp', 'zero'))
- query_square: float32 [2304, 2048], P(('dp', 'zero'), 'tensor'), as said below
- key_square: float32 [2304, 1024], P(('dp', 'zero'), 'tensor'), as said below
- value_square: float32 [2304, 1024], P(('dp', 'zero'), 'tensor'), as said below
- out_square: float32 [2048, 2304], P('tensor', ('dp', 'zero')), as said below
- gate_square: float32 [2304, 9216], P(('dp', 'zero'), 'tensor'), as said below
- up_square: float32 [2304, 9216], P(('dp', 'zero'), 'tensor'), as said below
- down_square: float32 [9216, 2304], P('tensor', ('dp', 'zero')), as said below
- gains_square: float32 [4, 2304], P(None, ('dp', 'zero')), as said below
Outputs:
- block_out: bfloat16 [7168, 2304], P(('dp', 'zero'))
- input_grad: float32 [7168, 2304], P(('dp', 'zero'))
- query_moment: float32 [2304, 2048], P(('dp', 'zero'), 'tensor')
- key_moment: float32 [2304, 1024], P(('dp', 'zero'), 'tensor')
- value_moment: float32 [2304, 1024], P(('dp', 'zero'), 'tensor')
- out_moment: float32 [2048, 2304], P('tensor', ('dp', 'zero'))
- gate_moment: float32 [2304, 9216], P(('dp', 'zero'), 'tensor')
- up_moment: float32 [2304, 9216], P(('dp', 'zero'), 'tensor')
- down_moment: float32 [9216, 2304], P('tensor', ('dp', 'zero'))
- gains_moment: float32 [4, 2304], P(None, ('dp', 'zero'))
- query_second: float32 [2304, 2048], P(('dp', 'zero'), 'tensor')
- key_second: float32 [2304, 1024], P(('dp', 'zero'), 'tensor')
- value_second: float32 [2304, 1024], P(('dp', 'zero'), 'tensor')
- out_second: float32 [2048, 2304], P('tensor', ('dp', 'zero'))
- gate_second: float32 [2304, 9216], P(('dp', 'zero'), 'tensor')
- up_second: float32 [2304, 9216], P(('dp', 'zero'), 'tensor')
- down_second: float32 [9216, 2304], P('tensor', ('dp', 'zero'))
- gains_second: float32 [4, 2304], P(None, ('dp', 'zero'))
- query_master: float32 [2304, 2048], P(('dp', 'zero'), 'tensor')
- key_master: float32 [2304, 1024], P(('dp', 'zero'), 'tensor')
- value_master: float32 [2304, 1024], P(('dp', 'zero'), 'tensor')
- out_master: float32 [2048, 2304], P('tensor', ('dp', 'zero'))
- gate_master: float32 [2304, 9216], P(('dp', 'zero'), 'tensor')
- up_master: float32 [2304, 9216], P(('dp', 'zero'), 'tensor')
- down_master: float32 [9216, 2304], P('tensor', ('dp', 'zero'))
- gains_master: float32 [4, 2304], P(None, ('dp', 'zero'))
The draws below stay inside these ranges and needn't reach their ends.
Inputs may be any that keep to these rules, and one draw needn't show every extreme that they name: `segment`: token groups are aligned blocks of 896 tokens. Ids never fall, each sequence lies within one block, blocks share no id, each sequence holds 1 to 512 tokens, and every block holds a sequence of exactly 512. `query_square`: positive. `key_square`: positive. `value_square`: positive. `out_square`: positive. `gate_square`: positive. `up_square`: positive. `down_square`: positive. `gains_square`: positive.
All inputs are finite; a program needn't handle non-finite values.
Results may differ from the reference program's by a relative error of at most 0.025.
Values may be sent and summed in bfloat16 or wider, within the bound.
A program may use at most 320 MiB of HBM per device.

```python
import math
import jax
import jax.numpy as jnp
from jax import lax

MODEL_WIDTH = 2304
QUERY_HEADS = 8
KEY_VALUE_HEADS = 4
HEAD_SIZE = 256
FF = 9216
GROUP_TOKENS = 896
MAXLEN = 512
STEP = 10
QW = 2048
KW = 1024
TOKENS_TOTAL = 7168


def first_sample(key, shape, square):
    return jax.random.truncated_normal(key, -4.0, 4.0, shape, jnp.float32) * (0.111 * math.sqrt(square))


def second_sample(key, shape, square):
    lower = math.log(0.03 * square)
    upper = math.log(0.2 * square)
    return jnp.exp(jax.random.uniform(key, shape, jnp.float32, lower, upper))


def draw_segment(key, part):
    key = jax.random.fold_in(key, 3)
    token_groups = TOKENS_TOTAL // GROUP_TOKENS
    shortest = MAXLEN // 8
    count = GROUP_TOKENS // shortest + 2

    def one_group(group):
        sub = jax.random.fold_in(key, group)
        key_len, key_start = jax.random.split(sub)
        lengths = jax.random.randint(key_len, (count,), shortest, MAXLEN + 1)
        ends = jnp.cumsum(lengths)
        index = jnp.arange(GROUP_TOKENS, dtype=jnp.int32)
        cut = jnp.any(index[:, None] == ends[None, :], axis=1)
        start = jax.random.randint(key_start, (), 0, GROUP_TOKENS - MAXLEN + 1)
        inside = (index > start) & (index < start + MAXLEN)
        flag = cut & jnp.logical_not(inside) | (index == start) | (index == start + MAXLEN) | (index == 0)
        running = jnp.cumsum(flag.astype(jnp.int32))
        last = running == running[GROUP_TOKENS - 1]
        local = jnp.where(last, GROUP_TOKENS - 1, running - 1)
        return local + group * GROUP_TOKENS
    return jax.vmap(one_group)(jnp.arange(token_groups, dtype=jnp.int32)).reshape(-1)


def draw_query_mean(key, part):
    key = jax.random.fold_in(key, 11)
    return first_sample(key, (MODEL_WIDTH, QUERY_HEADS * HEAD_SIZE), TOKENS_TOTAL / 4.0)


def draw_key_mean(key, part):
    key = jax.random.fold_in(key, 12)
    return first_sample(key, (MODEL_WIDTH, KEY_VALUE_HEADS * HEAD_SIZE), TOKENS_TOTAL / 4.0)


def draw_value_mean(key, part):
    key = jax.random.fold_in(key, 13)
    return first_sample(key, (MODEL_WIDTH, KEY_VALUE_HEADS * HEAD_SIZE), TOKENS_TOTAL / 4.0)


def draw_out_mean(key, part):
    key = jax.random.fold_in(key, 14)
    return first_sample(key, (QUERY_HEADS * HEAD_SIZE, MODEL_WIDTH), TOKENS_TOTAL * 1.0)


def draw_gate_mean(key, part):
    key = jax.random.fold_in(key, 15)
    return first_sample(key, (MODEL_WIDTH, FF), TOKENS_TOTAL / 4.0)


def draw_up_mean(key, part):
    key = jax.random.fold_in(key, 16)
    return first_sample(key, (MODEL_WIDTH, FF), TOKENS_TOTAL / 4.0)


def draw_down_mean(key, part):
    key = jax.random.fold_in(key, 17)
    return first_sample(key, (FF, MODEL_WIDTH), TOKENS_TOTAL * 1.0)


def draw_gains_mean(key, part):
    key = jax.random.fold_in(key, 18)
    return first_sample(key, (4, MODEL_WIDTH), TOKENS_TOTAL * 1.0)


def draw_query_square(key, part):
    key = jax.random.fold_in(key, 21)
    return second_sample(key, (MODEL_WIDTH, QUERY_HEADS * HEAD_SIZE), TOKENS_TOTAL / 4.0)


def draw_key_square(key, part):
    key = jax.random.fold_in(key, 22)
    return second_sample(key, (MODEL_WIDTH, KEY_VALUE_HEADS * HEAD_SIZE), TOKENS_TOTAL / 4.0)


def draw_value_square(key, part):
    key = jax.random.fold_in(key, 23)
    return second_sample(key, (MODEL_WIDTH, KEY_VALUE_HEADS * HEAD_SIZE), TOKENS_TOTAL / 4.0)


def draw_out_square(key, part):
    key = jax.random.fold_in(key, 24)
    return second_sample(key, (QUERY_HEADS * HEAD_SIZE, MODEL_WIDTH), TOKENS_TOTAL * 1.0)


def draw_gate_square(key, part):
    key = jax.random.fold_in(key, 25)
    return second_sample(key, (MODEL_WIDTH, FF), TOKENS_TOTAL / 4.0)


def draw_up_square(key, part):
    key = jax.random.fold_in(key, 26)
    return second_sample(key, (MODEL_WIDTH, FF), TOKENS_TOTAL / 4.0)


def draw_down_square(key, part):
    key = jax.random.fold_in(key, 27)
    return second_sample(key, (FF, MODEL_WIDTH), TOKENS_TOTAL * 1.0)


def draw_gains_square(key, part):
    key = jax.random.fold_in(key, 28)
    return second_sample(key, (4, MODEL_WIDTH), TOKENS_TOTAL * 1.0)


def levels(stream_key, dims, pieces, low, largest):
    factor_of = 1.0
    for position, parts in pieces:
        draws = jax.random.uniform(jax.random.fold_in(jax.random.fold_in(stream_key, 6), position), (parts,), jnp.float32, low / len(pieces), largest / len(pieces))
        factor_of = factor_of * jnp.repeat(jnp.exp(draws), dims[position] // parts).reshape((-1,) + (1,) * (len(dims) - 1 - position))
    return factor_of


def centred(stream_key, extent, deviation, limit, cuts=(), kind=jnp.bfloat16):
    drawn = jax.random.normal(stream_key, extent, jnp.float32) * deviation
    if len(cuts) > 0:
        drawn = levels(stream_key, extent, cuts, -0.22, 0.18) * drawn
    return jnp.clip(drawn, min=-limit, max=limit).astype(kind)


def setup_inputs(seed: int = 0) -> dict:
    splits = jax.random.split(jax.random.key(seed), 28)
    return {
        "inputs": centred(splits[0], (TOKENS_TOTAL, MODEL_WIDTH), 1.0, 6.0, ((0, 8),)),
        "cotangent": centred(splits[1], (TOKENS_TOTAL, MODEL_WIDTH), 1.0, 6.0, ((0, 8),)),
        "segment": draw_segment(jax.random.fold_in(splits[27], 71), 0),
        "query_weight": centred(splits[3], (MODEL_WIDTH, QW), MODEL_WIDTH ** -0.5, 0.125, ((0, 8), (1, 4)), jnp.float32),
        "key_weight": centred(splits[4], (MODEL_WIDTH, KW), MODEL_WIDTH ** -0.5, 0.125, ((0, 8), (1, 4)), jnp.float32),
        "value_weight": centred(splits[5], (MODEL_WIDTH, KW), MODEL_WIDTH ** -0.5, 0.125, ((0, 8), (1, 4)), jnp.float32),
        "out_weight": centred(splits[6], (QW, MODEL_WIDTH), QW ** -0.5, 0.125, ((0, 4), (1, 8)), jnp.float32),
        "gate_weight": centred(splits[7], (MODEL_WIDTH, FF), MODEL_WIDTH ** -0.5, 0.125, ((0, 8), (1, 4)), jnp.float32),
        "up_weight": centred(splits[8], (MODEL_WIDTH, FF), MODEL_WIDTH ** -0.5, 0.125, ((0, 8), (1, 4)), jnp.float32),
        "down_weight": centred(splits[9], (FF, MODEL_WIDTH), FF ** -0.5, 0.0625, ((0, 4), (1, 8)), jnp.float32),
        "norm_gains": jnp.clip(1.0 + 0.15 * jax.random.normal(splits[10], (4, MODEL_WIDTH), jnp.float32), 0.25, 1.75),
        "query_mean": draw_query_mean(jax.random.fold_in(splits[27], 71), 0),
        "key_mean": draw_key_mean(jax.random.fold_in(splits[27], 71), 0),
        "value_mean": draw_value_mean(jax.random.fold_in(splits[27], 71), 0),
        "out_mean": draw_out_mean(jax.random.fold_in(splits[27], 71), 0),
        "gate_mean": draw_gate_mean(jax.random.fold_in(splits[27], 71), 0),
        "up_mean": draw_up_mean(jax.random.fold_in(splits[27], 71), 0),
        "down_mean": draw_down_mean(jax.random.fold_in(splits[27], 71), 0),
        "gains_mean": draw_gains_mean(jax.random.fold_in(splits[27], 71), 0),
        "query_square": draw_query_square(jax.random.fold_in(splits[27], 71), 0),
        "key_square": draw_key_square(jax.random.fold_in(splits[27], 71), 0),
        "value_square": draw_value_square(jax.random.fold_in(splits[27], 71), 0),
        "out_square": draw_out_square(jax.random.fold_in(splits[27], 71), 0),
        "gate_square": draw_gate_square(jax.random.fold_in(splits[27], 71), 0),
        "up_square": draw_up_square(jax.random.fold_in(splits[27], 71), 0),
        "down_square": draw_down_square(jax.random.fold_in(splits[27], 71), 0),
        "gains_square": draw_gains_square(jax.random.fold_in(splits[27], 71), 0),
    }


@jax.custom_vjp
def reduced_precision(v):
    return lax.optimization_barrier(v.astype(jnp.bfloat16)).astype(jnp.float32)

@jax.custom_vjp
def reduced_backward(v):
    return v

def low_keep(v):
    return (reduced_precision(v), None)

def low_pass(kept, grad):
    return (grad,)

def back_keep(v):
    return (v, None)

def back_low(kept, grad):
    return (reduced_precision(grad),)
reduced_precision.defvjp(low_keep, low_pass)
reduced_backward.defvjp(back_keep, back_low)
norm_eps = 1e-06
soft_cap = 50.0
rope_base = 10000.0
beta_one = 0.9
beta_two = 0.95
adam_eps = 1e-08
weight_decay = 0.1
gain_rate = 0.7

def matrix_product(left, right):
    return jnp.dot(left, right, precision=lax.Precision.HIGHEST, preferred_element_type=jnp.float32)

def rms_norm(value_rows, gain):
    factor = lax.rsqrt(lax.optimization_barrier(jnp.mean(value_rows * value_rows, axis=-1, keepdims=True)) + norm_eps)
    return value_rows * factor * gain

def rope_tables(segment):
    index = jnp.arange(segment.shape[0], dtype=jnp.int32)
    earlier = jnp.concatenate([jnp.full((1,), -1, jnp.int32), segment[:-1]])
    first = lax.cummax(jnp.where(segment != earlier, index, 0), axis=0)
    place = (index - first).astype(jnp.float32)
    inverse = rope_base ** (-jnp.arange(0, HEAD_SIZE, 2, dtype=jnp.float32) / HEAD_SIZE)
    angle = place[:, None] * inverse[None, :]
    return (jnp.cos(angle)[:, None, :], jnp.sin(angle)[:, None, :])

def rotate(value_rows, cosine, sine):
    half = value_rows.shape[-1] // 2
    first = value_rows[..., :half]
    second = value_rows[..., half:]
    return jnp.concatenate([first * cosine - second * sine, second * cosine + first * sine], axis=-1)

def attend_token_group(packed):
    query_rows, key_rows, value_rows, seg_ids = packed
    group_size = query_rows.shape[0]
    query_rows = query_rows.reshape(group_size, KEY_VALUE_HEADS, QUERY_HEADS // KEY_VALUE_HEADS, HEAD_SIZE)
    raw = jnp.einsum('qhgd,khd->hgqk', query_rows, key_rows, precision=lax.Precision.HIGHEST) * HEAD_SIZE ** (-0.5)
    raw = reduced_backward(raw)
    capped = soft_cap * jnp.tanh(raw / soft_cap)
    index = jnp.arange(group_size, dtype=jnp.int32)
    visible = (index[None, :] <= index[:, None]) & (seg_ids[:, None] == seg_ids[None, :])
    probs = jax.nn.softmax(jnp.where(visible, capped, -jnp.inf), axis=-1)
    mixed = jnp.einsum('hgqk,khd->qhgd', reduced_precision(probs), value_rows, precision=lax.Precision.HIGHEST)
    return reduced_precision(reduced_backward(mixed)).reshape(group_size, QUERY_HEADS * HEAD_SIZE)

def forward(resid_in, segment, weights):
    query_mat, key_matrix, value_matrix, out_mat, gate_mat, up_mat, down_mat, gains = [reduced_precision(w) for w in weights]
    cosine, sine = rope_tables(segment)
    token_rows = resid_in.shape[0]
    first_normed = reduced_precision(rms_norm(resid_in, gains[0]))
    query_rows = reduced_backward(matrix_product(first_normed, query_mat)).reshape(token_rows, QUERY_HEADS, HEAD_SIZE)
    key_rows = reduced_backward(matrix_product(first_normed, key_matrix)).reshape(token_rows, KEY_VALUE_HEADS, HEAD_SIZE)
    value_rows = reduced_precision(reduced_backward(matrix_product(first_normed, value_matrix))).reshape(token_rows, KEY_VALUE_HEADS, HEAD_SIZE)
    rotated_queries = reduced_precision(rotate(query_rows, cosine, sine))
    rotated_keys = reduced_precision(rotate(key_rows, cosine, sine))
    token_groups = token_rows // GROUP_TOKENS
    attention_output = lax.map(jax.checkpoint(attend_token_group), (rotated_queries.reshape(token_groups, GROUP_TOKENS, QUERY_HEADS, HEAD_SIZE), rotated_keys.reshape(token_groups, GROUP_TOKENS, KEY_VALUE_HEADS, HEAD_SIZE), value_rows.reshape(token_groups, GROUP_TOKENS, KEY_VALUE_HEADS, HEAD_SIZE), segment.reshape(token_groups, GROUP_TOKENS)))
    attention_output = attention_output.reshape(token_rows, QUERY_HEADS * HEAD_SIZE)
    attn_sum = reduced_backward(matrix_product(attention_output, out_mat))
    middle = resid_in + rms_norm(attn_sum, gains[1])
    normed_two = reduced_precision(rms_norm(middle, gains[2]))
    gate_val = reduced_backward(matrix_product(normed_two, gate_mat))
    up_val = reduced_backward(matrix_product(normed_two, up_mat))
    hidden = reduced_precision(jax.nn.gelu(gate_val, approximate=True) * up_val)
    mlp_sum = reduced_backward(matrix_product(hidden, down_mat))
    return middle + rms_norm(mlp_sum, gains[3])

def adam_update(master, mean, square, grad, rate, decay):
    moment = beta_one * mean + (1.0 - beta_one) * grad
    second = beta_two * square + (1.0 - beta_two) * grad * grad
    direction = moment / (1.0 - beta_one ** STEP) / (jnp.sqrt(second / (1.0 - beta_two ** STEP)) + adam_eps)
    return (moment, second, master - rate * (direction + decay * master))

def reference(inputs, cotangent, segment, query_weight, key_weight, value_weight, out_weight, gate_weight, up_weight, down_weight, norm_gains, query_mean, key_mean, value_mean, out_mean, gate_mean, up_mean, down_mean, gains_mean, query_square, key_square, value_square, out_square, gate_square, up_square, down_square, gains_square):
    masters = (query_weight, key_weight, value_weight, out_weight, gate_weight, up_weight, down_weight, norm_gains)
    means = (query_mean, key_mean, value_mean, out_mean, gate_mean, up_mean, down_mean, gains_mean)
    squares = (query_square, key_square, value_square, out_square, gate_square, up_square, down_square, gains_square)
    rates = (MODEL_WIDTH ** (-0.5), MODEL_WIDTH ** (-0.5), MODEL_WIDTH ** (-0.5), (QUERY_HEADS * HEAD_SIZE) ** (-0.5), MODEL_WIDTH ** (-0.5), MODEL_WIDTH ** (-0.5), FF ** (-0.5), gain_rate)
    decays = (weight_decay,) * 7 + (0.0,)

    def layer(resid_in, weights):
        return forward(resid_in, segment, weights)
    block_val, pullback = jax.vjp(layer, inputs.astype(jnp.float32), masters)
    input_grad, grads = pullback(cotangent.astype(jnp.float32))
    moments = []
    seconds = []
    updated = []
    for index in range(8):
        moment, second, master = adam_update(masters[index], means[index], squares[index], grads[index], rates[index], decays[index])
        moments.append(moment)
        seconds.append(second)
        updated.append(master)
    return (block_val.astype(jnp.bfloat16), input_grad, *moments, *seconds, *updated)
```

```python
import functools

import jax
import jax.numpy as jnp
from jax import lax
from jax.experimental import pallas as pl
from jax.experimental.pallas import tpu as pltpu
from jax.sharding import PartitionSpec as P

MESH = pl.DeviceIdType.MESH

MODEL_WIDTH = 2304
QUERY_HEADS = 8
HEAD_SIZE = 256
FF = 9216
STEP = 10
W = MODEL_WIDTH


norm_eps = 1e-06
soft_cap = 50.0
rope_base = 10000.0
beta_one = 0.9
beta_two = 0.95
adam_eps = 1e-08
weight_decay = 0.1
gain_rate = 0.7


def rms_forward(value_rows, gain):
    factor = lax.rsqrt(jnp.mean(value_rows * value_rows, axis=-1, keepdims=True) + norm_eps)
    normed = value_rows * factor
    return (normed * gain, normed, factor)


def rms_backward(grad, gain, normed, factor):
    scaled = grad * gain
    inner = jnp.mean(scaled * normed, axis=-1, keepdims=True)
    return (factor * (scaled - normed * inner), jnp.sum(grad * normed, axis=0))


def rope_tables(segment):
    index = jnp.arange(segment.shape[0], dtype=jnp.int32)
    earlier = jnp.concatenate([jnp.full((1,), -1, jnp.int32), segment[:-1]])
    first = lax.cummax(jnp.where(segment != earlier, index, 0), axis=0)
    place = (index - first).astype(jnp.float32)
    inverse = rope_base ** (-jnp.arange(0, HEAD_SIZE, 2, dtype=jnp.float32) / HEAD_SIZE)
    angle = place[:, None] * inverse[None, :]
    return (jnp.cos(angle)[:, None, :], jnp.sin(angle)[:, None, :])


def rotate(value_rows, cosine, sine):
    half = value_rows.shape[-1] // 2
    first = value_rows[..., :half]
    second = value_rows[..., half:]
    return jnp.concatenate(
        [first * cosine - second * sine, second * cosine + first * sine], axis=-1
    )


def unrotate(value_rows, cosine, sine):
    half = value_rows.shape[-1] // 2
    first = value_rows[..., :half]
    second = value_rows[..., half:]
    return jnp.concatenate(
        [first * cosine + second * sine, second * cosine - first * sine], axis=-1
    )


def gated(gate_val, up_val):
    return jax.nn.gelu(gate_val, approximate=True) * up_val


def score_block(query_blk, start, rotated_keys, segment):
    group_size = query_blk.shape[0]
    total = rotated_keys.shape[0]
    raw = jnp.einsum(
        "qhgd,khd->hgqk", query_blk, rotated_keys, preferred_element_type=jnp.float32
    ) * HEAD_SIZE ** (-0.5)
    bent = jnp.tanh(raw / soft_cap)
    rows_idx = start + jnp.arange(group_size, dtype=jnp.int32)
    cols_idx = jnp.arange(total, dtype=jnp.int32)
    visible = (cols_idx[None, :] <= rows_idx[:, None]) & (segment[:, None] == segment[None, :])
    return (jnp.where(visible, soft_cap * bent, -jnp.inf), bent)


def split_blocks(value_rows, heads_kv):
    total = value_rows.shape[0]
    count = total // total
    starts = jnp.arange(count, dtype=jnp.int32) * total
    return (value_rows.reshape(count, total, heads_kv, -1, HEAD_SIZE), starts)


def attend_forward(rotated_queries, rotated_keys, value_low, segment):
    total = rotated_queries.shape[0]
    blocks, starts = split_blocks(rotated_queries, rotated_keys.shape[1])

    def one_block(packed):
        query_blk, start = packed
        masked, bent = score_block(query_blk, start, rotated_keys, segment)
        top = jnp.max(masked, axis=-1, keepdims=True)
        expo = jnp.exp(masked - top)
        total_sum = jnp.sum(expo, axis=-1, keepdims=True)
        probs = expo / total_sum
        mixed = jnp.einsum(
            "hgqk,khd->qhgd",
            probs.astype(jnp.bfloat16),
            value_low,
            preferred_element_type=jnp.float32,
        )
        return (mixed.astype(jnp.bfloat16), top + jnp.log(total_sum))

    mixed, log_sums = lax.map(one_block, (blocks, starts))
    return (mixed.reshape(total, -1), log_sums)


def attend_backward(rotated_queries, rotated_keys, value_low, segment, log_sums, dout_low):
    total = rotated_queries.shape[0]
    heads_kv = rotated_keys.shape[1]
    blocks, starts = split_blocks(rotated_queries, heads_kv)
    dout_blocks, unused = split_blocks(dout_low, heads_kv)
    scale = HEAD_SIZE ** (-0.5)

    def one_block(carry, packed):
        key_grad, value_grad = carry
        query_blk, dout_blk, lse_blk, start = packed
        masked, bent = score_block(query_blk, start, rotated_keys, segment)
        probs = jnp.exp(masked - lse_blk)
        dprobs = jnp.einsum(
            "qhgd,khd->hgqk", dout_blk, value_low, preferred_element_type=jnp.float32
        )
        inner = jnp.sum(probs * dprobs, axis=-1, keepdims=True)
        dscore = (probs * (dprobs - inner) * (1.0 - bent * bent)).astype(jnp.bfloat16)
        query_grad = (
            jnp.einsum("hgqk,khd->qhgd", dscore, rotated_keys, preferred_element_type=jnp.float32)
            * scale
        )
        key_grad = (
            key_grad
            + jnp.einsum("hgqk,qhgd->khd", dscore, query_blk, preferred_element_type=jnp.float32)
            * scale
        )
        value_grad = value_grad + jnp.einsum(
            "hgqk,qhgd->khd",
            probs.astype(jnp.bfloat16),
            dout_blk,
            preferred_element_type=jnp.float32,
        )
        return ((key_grad, value_grad), query_grad)

    zeros = jnp.zeros(rotated_keys.shape, jnp.float32)
    (key_grad, value_grad), query_grads = lax.scan(
        one_block, (zeros, zeros), (blocks, dout_blocks, log_sums, starts)
    )
    return (query_grads.reshape(total, -1, HEAD_SIZE), key_grad, value_grad)


def adam_update(master, mean, square, grad, rate, decay):
    moment = beta_one * mean + (1.0 - beta_one) * grad
    second = beta_two * square + (1.0 - beta_two) * grad * grad
    direction = (
        moment / (1.0 - beta_one**STEP) / (jnp.sqrt(second / (1.0 - beta_two**STEP)) + adam_eps)
    )
    return (moment, second, master - rate * (direction + decay * master))


def remote(src,dst,ss,rs,dev):
    return pltpu.make_async_remote_copy(src_ref=src,dst_ref=dst,send_sem=ss,recv_sem=rs,device_id=dev,device_id_type=MESH)

class Chain:
    def __init__(self, half, ch, P, RE, RM, O, sp, so, ve, vm, vo, lags=(1,2,3,4)):
        self.p = lax.axis_index("tensor"); p=self.p
        self.reg=half//2; self.ch=ch; self.nt=self.reg//ch
        self.P,self.RE,self.RM,self.O=P,RE,RM,O
        self.sp,self.so,self.ve,self.vm,self.vo=sp,so,ve,vm,vo
        self.lags=lags
        self.end = (p==0)|(p==3)
        self.mid = (p==1)|(p==2)
        self.to_mid = {"tensor": jnp.where(p<2, 1, 2)}
        self.to_end = {"tensor": jnp.where(p<2, 0, 3)}
        self.to_oth = {"tensor": jnp.where(p<2, 2, 1)}
        self.own = jnp.where(p<2,0,1); self.oth=1-self.own
    def rows(self, part, t):
        return pl.ds(pl.multiple_of(part*self.reg+t*self.ch,16), self.ch)
    def trow(self,t): return pl.ds(pl.multiple_of(t*self.ch,16), self.ch)
    def r1(self,h,t):
        for part in (0,1):
            r=self.rows(part,t)
            remote(self.P.at[h,r],self.RE.at[h,r],self.sp.at[h,t,part],self.ve.at[h,t,part],self.to_mid).start()
    def r2(self,h,t):
        r=self.rows(self.oth,t)
        remote(self.P.at[h,r],self.RE.at[h,r],self.sp.at[h,t,0],self.ve.at[h,t,self.oth],self.to_end).wait_recv()
        self.P[h,r,:]=(self.P[h,r,:].astype(jnp.float32)+self.RE[h,r,:].astype(jnp.float32)).astype(jnp.bfloat16)
        remote(self.P.at[h,r],self.RM.at[h,self.trow(t)],self.sp.at[h,t,0],self.vm.at[h,t],self.to_oth).start()
    def r3(self,h,t):
        r=self.rows(self.own,t); q=self.trow(t)
        remote(self.P.at[h,r],self.RE.at[h,r],self.sp.at[h,t,0],self.ve.at[h,t,self.own],self.to_end).wait_recv()
        remote(self.P.at[h,r],self.RM.at[h,q],self.sp.at[h,t,0],self.vm.at[h,t],self.to_oth).wait_recv()
        self.O[h,r,:]=(self.P[h,r,:].astype(jnp.float32)+self.RE[h,r,:].astype(jnp.float32)+self.RM[h,q,:].astype(jnp.float32)).astype(jnp.bfloat16)
        remote(self.O.at[h,r],self.O.at[h,r],self.so.at[h,t,0],self.vo.at[h,t,self.own],self.to_end).start()
        remote(self.O.at[h,r],self.O.at[h,r],self.so.at[h,t,1],self.vo.at[h,t,self.own],self.to_oth).start()
    def b4(self,h,t):
        r=self.rows(self.oth,t)
        c=remote(self.O.at[h,r],self.O.at[h,r],self.so.at[h,t,2],self.vo.at[h,t,self.oth],self.to_end)
        c.wait_recv(); c.start()
    def b5_end(self,h,t):
        for part in (0,1):
            r=self.rows(part,t)
            remote(self.O.at[h,r],self.O.at[h,r],self.so.at[h,t,0],self.vo.at[h,t,part],self.to_mid).wait_recv()
            remote(self.P.at[h,r],self.RE.at[h,r],self.sp.at[h,t,part],self.ve.at[h,t,part],self.to_mid).wait_send()
    def b5_mid(self,h,t):
        r=self.rows(self.own,t)
        remote(self.P.at[h,r],self.RE.at[h,r],self.sp.at[h,t,0],self.ve.at[h,t,0],self.to_oth).wait_send()
        for i in range(3):
            remote(self.O.at[h,r],self.O.at[h,r],self.so.at[h,t,i],self.vo.at[h,t,0],self.to_end).wait_send()
    def tick(self, T, lo, hi):
        nt=self.nt
        def at(c, cond, fns):
            ok=(c>=lo)&(c<hi)
            j=c//nt; h=j%2; t=c%nt
            @pl.when(ok&cond)
            def _():
                for f in fns: f(h,t)
        l1,l2,l3,l4=self.lags
        at(T,self.end,[self.r1])
        at(T-l1,self.mid,[self.r2])
        at(T-l2,self.mid,[self.r3])
        at(T-l3,self.mid,[self.b4])
        at(T-l4,self.end,[self.b5_end])
        at(T-l4,self.mid,[self.b5_mid])

def chain_scratch(half,ch):
    nt=half//2//ch
    B=jnp.bfloat16; D=pltpu.SemaphoreType.DMA
    return [pltpu.VMEM((2,half,W),B),pltpu.VMEM((2,half,W),B),pltpu.VMEM((2,half//2,W),B),pltpu.VMEM((2,half,W),B),
            D((2,nt,2)),D((2,nt,3)),D((2,nt,2)),D((2,nt)),D((2,nt,2))]

def line_barrier():
    te=lax.axis_index("tensor")
    bar=pltpu.get_barrier_semaphore()
    @pl.when(te<3)
    def _(): pl.semaphore_signal(bar, inc=1, device_id={"tensor":te+1}, device_id_type=MESH)
    @pl.when(te>0)
    def _(): pl.semaphore_signal(bar, inc=1, device_id={"tensor":te-1}, device_id_type=MESH)
    pl.semaphore_wait(bar, (te<3).astype(jnp.int32)+(te>0).astype(jnp.int32))

def ar_kernel(half,ch,lags,a_ref,o_ref,P,RE,RM,O,sp,so,ve,vm,vo,isem,osem):
    ins=[pltpu.make_async_copy(a_ref.at[pl.ds(h*half,half)],P.at[h],isem.at[h]) for h in (0,1)]
    for c in ins: c.start()
    line_barrier()
    for c in ins: c.wait()
    C=Chain(half,ch,P,RE,RM,O,sp,so,ve,vm,vo,lags)
    n=2*C.nt
    def body(T,_):
        C.tick(T,0,n); return 0
    lax.fori_loop(0,n+lags[-1],body,0)
    outs=[pltpu.make_async_copy(O.at[h],o_ref.at[pl.ds(h*half,half)],osem.at[h]) for h in (0,1)]
    for c in outs: c.start()
    for c in outs: c.wait()

def all_reduce(a,ch=16,lags=(2,4,6,8),cid=1):
    rows=a.shape[0]; half=rows//2
    return pl.pallas_call(functools.partial(ar_kernel,half,ch,lags),
        out_shape=jax.ShapeDtypeStruct(a.shape,a.dtype),
        in_specs=[pl.BlockSpec(memory_space=pl.ANY)],out_specs=pl.BlockSpec(memory_space=pl.ANY),
        scratch_shapes=chain_scratch(half,ch)+[pltpu.SemaphoreType.DMA((2,)),pltpu.SemaphoreType.DMA((2,))],
        compiler_params=pltpu.CompilerParams(collective_id=cid,has_side_effects=True,vmem_limit_bytes=60*2**20))(a)

def coords():
    dp,ze=lax.axis_index("dp"),lax.axis_index("zero")
    x=dp//2; c=dp%2
    return x,c,ze
def sid(x,c,y): return (x*2+c)*2+y
class Plane:
    def __init__(self):
        x,c,y=coords()
        self.x,self.c,self.y=x,c,y
        self.toX={"dp":(1-x)*2+c}; self.toY={"zero":1-y}; self.toC={"dp":x*2+1-c}
        self.lane=[sid(x,c,y),sid(1-x,c,y),sid(x,c,1-y),sid(1-x,c,1-y)]
        d=1-c
        self.other=[sid(x,d,y),sid(1-x,d,y),sid(x,d,1-y),sid(1-x,d,1-y)]
        self.is0=c==0; self.is1=c==1
def plane_signal():
    x,c,y=coords()
    bar=pltpu.get_barrier_semaphore()
    for dev in ({"dp":(1-x)*2+c},{"zero":1-y},{"dp":x*2+1-c}):
        pl.semaphore_signal(bar, inc=1, device_id=dev, device_id_type=MESH)
def plane_barrier():
    plane_signal(); pl.semaphore_wait(pltpu.get_barrier_semaphore(),3)

class Gather:
    def __init__(self, units, ss, rs, ls):
        self.u=units; self.ss,self.rs,self.ls=ss,rs,ls; self.pl=Plane()
    def refs(self,i):
        S,F,r0,rr=self.u[i]; r=pl.ds(r0,rr)
        return S.at[r], (lambda s: F.at[s,r])
    def a(self,i):
        S,F=self.refs(i); q=self.pl; own=q.lane[0]
        remote(S,F(own),self.ss.at[i,0],self.rs.at[i,0],q.toX).start()
        remote(S,F(own),self.ss.at[i,1],self.rs.at[i,1],q.toY).start()
        remote(S,F(own),self.ss.at[i,2],self.rs.at[i,3],q.toC).start()
        pltpu.make_async_copy(S,F(own),self.ls.at[i]).start()
    def b(self,i):
        S,F=self.refs(i); q=self.pl; X,Y=q.lane[1],q.lane[2]
        remote(S,F(X),self.ss.at[i,0],self.rs.at[i,0],q.toX).wait_recv()
        @pl.when(q.is1)
        def _(): remote(F(X),F(X),self.ss.at[i,3],self.rs.at[i,2],q.toY).start()
        remote(F(X),F(X),self.ss.at[i,4],self.rs.at[i,4],q.toC).start()
        remote(S,F(Y),self.ss.at[i,1],self.rs.at[i,1],q.toY).wait_recv()
        @pl.when(q.is0)
        def _(): remote(F(Y),F(Y),self.ss.at[i,3],self.rs.at[i,2],q.toX).start()
        remote(F(Y),F(Y),self.ss.at[i,5],self.rs.at[i,5],q.toC).start()
    def d(self,i):
        S,F=self.refs(i); q=self.pl; D=q.lane[3]
        c=remote(F(D),F(D),self.ss.at[i,6],self.rs.at[i,6],q.toC)
        remote(S,F(D),self.ss.at[i,3],self.rs.at[i,2],q.toX).wait_recv()
        c.start()
    def e(self,i):
        S,F=self.refs(i); q=self.pl
        for j in range(4):
            remote(S,F(q.other[j]),self.ss.at[i,0],self.rs.at[i,3+j],q.toC).wait_recv()
        pltpu.make_async_copy(S,F(q.lane[0]),self.ls.at[i]).wait()
        for j in range(7):
            remote(S,S,self.ss.at[i,j],self.rs.at[i,0],q.toC).wait_send()
    def tick(self,T):
        n=len(self.u)
        if 0<=T<n: self.a(T)
        if 0<=T-1<n: self.b(T-1)
        if 0<=T-2<n: self.d(T-2)
        if 0<=T-3<n: self.e(T-3)
    @property
    def ticks(self): return len(self.u)+3
def gather_sems(n):
    D=pltpu.SemaphoreType.DMA
    return [D((n,7)),D((n,7)),D((n,))]

def ag_kernel(nw,rr,*refs):
    S=refs[:nw]; F=refs[nw:2*nw]; ss,rs,ls=refs[2*nw:]
    plane_barrier()
    units=[(S[k],F[k],r0,rr) for k in range(nw) for r0 in range(0,S[k].shape[0],rr)]
    G=Gather(units,ss,rs,ls)
    for T in range(G.ticks): G.tick(T)
def all_gather(shards,rr=96,cid=2):
    nw=len(shards); n=sum(s.shape[0]//rr for s in shards)
    out=pl.pallas_call(functools.partial(ag_kernel,nw,rr),
        out_shape=[jax.ShapeDtypeStruct((8,)+s.shape,s.dtype) for s in shards],
        in_specs=[pl.BlockSpec(memory_space=pl.ANY)]*nw,out_specs=[pl.BlockSpec(memory_space=pl.ANY)]*nw,
        scratch_shapes=gather_sems(n),
        compiler_params=pltpu.CompilerParams(collective_id=cid,has_side_effects=True,vmem_limit_bytes=60*2**20))(*shards)
    return [o.reshape(-1,s.shape[1]) for o,s in zip(out,shards)]

class Scatter:
    def __init__(self,units,LB,OB,depth,ss,rs,ls):
        self.u=units; self.LB,self.OB,self.depth=LB,OB,depth; self.ss,self.rs,self.ls=ss,rs,ls; self.pl=Plane()
    def get(self,i):
        G,O,CB,DB,XB,YB,r0,rr,C=self.u[i]; r=pl.ds(r0,rr); s=i%self.depth
        g=lambda k: G.at[k,r]
        lb=lambda j: self.LB.at[s,j,pl.ds(0,rr),pl.ds(0,C)]
        return g,lb,O.at[r],CB,DB,XB,YB,r,s,rr,C
    def p1(self,i):
        g,lb,O,CB,DB,XB,YB,r,s,rr,C=self.get(i); q=self.pl
        for j in (3,1,2,0):
            remote(g(q.other[j]),CB.at[j,r],self.ss.at[i,j],self.rs.at[i,j],q.toC).start()
            pltpu.make_async_copy(g(q.lane[j]),lb(j),self.ls.at[i,j]).start()
    def p2(self,i):
        g,lb,O,CB,DB,XB,YB,r,s,rr,C=self.get(i); q=self.pl
        for j in (3,1,2,0):
            pltpu.make_async_copy(g(q.lane[j]),lb(j),self.ls.at[i,j]).wait()
            remote(g(q.other[j]),CB.at[j,r],self.ss.at[i,j],self.rs.at[i,j],q.toC).wait_recv()
            v=self.LB[s,j,pl.ds(0,rr),pl.ds(0,C)].astype(jnp.float32)+CB[j,r].astype(jnp.float32)
            self.LB[s,j,pl.ds(0,rr),pl.ds(0,C)]=v.astype(jnp.bfloat16)
            if j==3:
                @pl.when(q.is0)
                def _(): remote(lb(3),DB.at[r],self.ss.at[i,4],self.rs.at[i,4],q.toX).start()
                @pl.when(q.is1)
                def _(): remote(lb(3),DB.at[r],self.ss.at[i,4],self.rs.at[i,4],q.toY).start()
            if j==1:
                @pl.when(q.is0)
                def _(): remote(lb(1),XB.at[r],self.ss.at[i,5],self.rs.at[i,5],q.toX).start()
            if j==2:
                @pl.when(q.is1)
                def _(): remote(lb(2),YB.at[r],self.ss.at[i,5],self.rs.at[i,6],q.toY).start()
    def p3(self,i):
        g,lb,O,CB,DB,XB,YB,r,s,rr,C=self.get(i); q=self.pl
        remote(lb(3),DB.at[r],self.ss.at[i,4],self.rs.at[i,4],q.toX).wait_recv()
        def relay(j,buf,sem,dev):
            v=self.LB[s,j,pl.ds(0,rr),pl.ds(0,C)].astype(jnp.float32)+DB[r].astype(jnp.float32)
            self.LB[s,j,pl.ds(0,rr),pl.ds(0,C)]=v.astype(jnp.bfloat16)
            remote(lb(j),buf.at[r],self.ss.at[i,6],self.rs.at[i,sem],dev).start()
        @pl.when(q.is0)
        def _(): relay(2,YB,6,q.toY)
        @pl.when(q.is1)
        def _(): relay(1,XB,5,q.toX)
    def p4(self,i):
        g,lb,O,CB,DB,XB,YB,r,s,rr,C=self.get(i); q=self.pl
        remote(lb(0),XB.at[r],self.ss.at[i,5],self.rs.at[i,5],q.toX).wait_recv()
        remote(lb(0),YB.at[r],self.ss.at[i,5],self.rs.at[i,6],q.toY).wait_recv()
        v=self.LB[s,0,pl.ds(0,rr),pl.ds(0,C)].astype(jnp.float32)+XB[r].astype(jnp.float32)+YB[r].astype(jnp.float32)
        ob=i%2
        self.OB[ob,pl.ds(0,rr),pl.ds(0,C)]=v.astype(self.OB.dtype)
        pltpu.make_async_copy(self.OB.at[ob,pl.ds(0,rr),pl.ds(0,C)],O,self.ls.at[i,4]).start()
        for j in range(7):
            remote(lb(0),XB.at[r],self.ss.at[i,j],self.rs.at[i,0],q.toX).wait_send()
    def p5(self,i):
        g,lb,O,CB,DB,XB,YB,r,s,rr,C=self.get(i)
        pltpu.make_async_copy(self.OB.at[i%2,pl.ds(0,rr),pl.ds(0,C)],O,self.ls.at[i,4]).wait()
    def tick(self,T):
        n=len(self.u)
        if 0<=T<n: self.p1(T)
        if 0<=T-1<n: self.p2(T-1)
        if 0<=T-2<n: self.p3(T-2)
        if 0<=T-4<n: self.p5(T-4)
        if 0<=T-3<n: self.p4(T-3)
    @property
    def ticks(self): return len(self.u)+4
def scatter_scratch(n,cols,rr,depth=4,rows=288):
    D=pltpu.SemaphoreType.DMA; B=jnp.bfloat16
    land=[]
    for C in cols: land+= [pltpu.VMEM((4,rows,C),B)]+[pltpu.VMEM((rows,C),B)]*3
    m=max(cols)
    return land+[pltpu.VMEM((depth,4,rr,m),B),pltpu.VMEM((2,rr,m),B),D((n,7)),D((n,7)),D((n,5))]
def rs_kernel(nw,rr,*refs):
    G=refs[:nw]; O=refs[nw:2*nw]; land=refs[2*nw:6*nw]; LB,OB,ss,rs,ls=refs[6*nw:]
    plane_barrier()
    units=[(G[k],O[k],*land[4*k:4*k+4],r0,rr,G[k].shape[2]) for k in range(nw) for r0 in range(0,G[k].shape[1],rr)]
    S=Scatter(units,LB,OB,LB.shape[0],ss,rs,ls)
    for T in range(S.ticks): S.tick(T)
def reduce_scatter(grads,rr=48,cid=3):
    nw=len(grads); g3=[g.reshape(8,g.shape[0]//8,g.shape[1]) for g in grads]
    n=sum(g.shape[1]//rr for g in g3)
    return pl.pallas_call(functools.partial(rs_kernel,nw,rr),
        out_shape=[jax.ShapeDtypeStruct(g.shape[1:],g.dtype) for g in g3],
        in_specs=[pl.BlockSpec(memory_space=pl.ANY)]*nw,out_specs=[pl.BlockSpec(memory_space=pl.ANY)]*nw,
        scratch_shapes=scatter_scratch(n,[g.shape[2] for g in g3],rr),
        compiler_params=pltpu.CompilerParams(collective_id=cid,has_side_effects=True,vmem_limit_bytes=62*2**20))(*g3)

def small_plane():
    return (lax.axis_size("dp"), lax.axis_size("zero")) == (4, 2)


def gather_rows(shards, cid):
    if small_plane():
        return all_gather(shards, cid=cid)
    return [lax.all_gather(s, ("dp", "zero"), axis=0, tiled=True) for s in shards]


def scatter_rows(grads, cid):
    if small_plane():
        return reduce_scatter(grads, cid=cid, rr=96)
    return [lax.psum_scatter(g, ("dp", "zero"), scatter_dimension=0, tiled=True) for g in grads]


def per_device(
    inputs,
    cotangent,
    segment,
    query_weight,
    key_weight,
    value_weight,
    out_weight,
    gate_weight,
    up_weight,
    down_weight,
    norm_gains,
    query_mean,
    key_mean,
    value_mean,
    out_mean,
    gate_mean,
    up_mean,
    down_mean,
    gains_mean,
    query_square,
    key_square,
    value_square,
    out_square,
    gate_square,
    up_square,
    down_square,
    gains_square,
):
    qkv_low = jnp.concatenate([query_weight, key_weight, value_weight], axis=1).astype(jnp.bfloat16)
    out_low = out_weight.T.astype(jnp.bfloat16)
    gate_low = gate_weight.astype(jnp.bfloat16)
    up_low = up_weight.astype(jnp.bfloat16)
    down_low = down_weight.T.astype(jnp.bfloat16)
    qkv_mat, out_mat = gather_rows([qkv_low, out_low], 2)
    gate_mat, up_mat, down_mat = gather_rows([gate_low, up_low, down_low], 3)
    gains_full = lax.all_gather(norm_gains.astype(jnp.bfloat16), ("dp", "zero"), axis=1, tiled=True)
    heads_q = query_weight.shape[1]
    heads_k = key_weight.shape[1]
    gains_val = gains_full.astype(jnp.float32)
    token_rows = inputs.shape[0]
    cosine, sine = rope_tables(segment)
    resid_in = inputs.astype(jnp.float32)
    first_normed, unit_one, factor_one = rms_forward(resid_in, gains_val[0])
    attn_in = first_normed.astype(jnp.bfloat16)
    qkv = jnp.dot(attn_in, qkv_mat, preferred_element_type=jnp.float32)
    query_raw = qkv[:, :heads_q].reshape(token_rows, -1, HEAD_SIZE)
    key_raw = qkv[:, heads_q : heads_q + heads_k].reshape(token_rows, -1, HEAD_SIZE)
    value_low = qkv[:, heads_q + heads_k :].astype(jnp.bfloat16).reshape(token_rows, -1, HEAD_SIZE)
    rotated_queries = rotate(query_raw, cosine, sine).astype(jnp.bfloat16)
    rotated_keys = rotate(key_raw, cosine, sine).astype(jnp.bfloat16)
    attention_output, log_sums = attend_forward(rotated_queries, rotated_keys, value_low, segment)
    attn_part = lax.dot_general(attention_output, out_mat, (((1,), (1,)), ((), ())), preferred_element_type=jnp.float32)
    attn_total = all_reduce(attn_part.astype(jnp.bfloat16), cid=4).astype(jnp.float32)
    post_attn, unit_two, factor_two = rms_forward(attn_total, gains_val[1])
    middle = resid_in + post_attn
    normed_two, unit_three, factor_three = rms_forward(middle, gains_val[2])
    mlp_in = normed_two.astype(jnp.bfloat16)
    gate_val = jnp.dot(mlp_in, gate_mat, preferred_element_type=jnp.float32)
    up_val = jnp.dot(mlp_in, up_mat, preferred_element_type=jnp.float32)
    hidden = gated(gate_val, up_val).astype(jnp.bfloat16)
    mlp_part = lax.dot_general(hidden, down_mat, (((1,), (1,)), ((), ())), preferred_element_type=jnp.float32)
    mlp_total = all_reduce(mlp_part.astype(jnp.bfloat16), cid=5).astype(jnp.float32)
    post_mlp, unit_four, factor_four = rms_forward(mlp_total, gains_val[3])
    block_out = (middle + post_mlp).astype(jnp.bfloat16)
    gains_back = gains_full.astype(jnp.float32)
    out_grad = cotangent.astype(jnp.float32)
    mlp_grad, gain_four = rms_backward(out_grad, gains_back[3], unit_four, factor_four)
    mlp_low = mlp_grad.astype(jnp.bfloat16)
    down_grad = jnp.einsum("td,tf->df", mlp_low, hidden, preferred_element_type=jnp.float32)
    hidden_grad = jnp.einsum("td,df->tf", mlp_low, down_mat, preferred_element_type=jnp.float32)
    unused_val, gelu_pull = jax.vjp(gated, gate_val, up_val)
    gate_dval, up_dval = gelu_pull(hidden_grad)
    gate_dlow = gate_dval.astype(jnp.bfloat16)
    up_dlow = up_dval.astype(jnp.bfloat16)
    gate_grad = jnp.einsum("td,tf->df", mlp_in, gate_dlow, preferred_element_type=jnp.float32)
    up_grad = jnp.einsum("td,tf->df", mlp_in, up_dlow, preferred_element_type=jnp.float32)
    normed_part = jnp.einsum(
        "tf,df->td", gate_dlow, gate_mat, preferred_element_type=jnp.float32
    ) + jnp.einsum("tf,df->td", up_dlow, up_mat, preferred_element_type=jnp.float32)
    normed_grad = all_reduce(normed_part.astype(jnp.bfloat16), cid=6).astype(jnp.float32)
    middle_part, gain_three = rms_backward(normed_grad, gains_back[2], unit_three, factor_three)
    middle_grad = out_grad + middle_part
    attn_grad, gain_two = rms_backward(middle_grad, gains_back[1], unit_two, factor_two)
    attn_low = attn_grad.astype(jnp.bfloat16)
    out_wgrad = jnp.einsum(
        "td,tc->dc", attn_low, attention_output, preferred_element_type=jnp.float32
    )
    attended_grad = (
        jnp.einsum("td,dc->tc", attn_low, out_mat, preferred_element_type=jnp.float32)
        .astype(jnp.bfloat16)
        .reshape(token_rows, -1, HEAD_SIZE)
    )
    query_rgrad, key_rgrad, value_rgrad = attend_backward(
        rotated_queries, rotated_keys, value_low, segment, log_sums, attended_grad
    )
    query_dlow = unrotate(query_rgrad, cosine, sine).astype(jnp.bfloat16).reshape(token_rows, -1)
    key_dlow = unrotate(key_rgrad, cosine, sine).astype(jnp.bfloat16).reshape(token_rows, -1)
    value_dlow = value_rgrad.astype(jnp.bfloat16).reshape(token_rows, -1)
    qkv_dlow = jnp.concatenate([query_dlow, key_dlow, value_dlow], axis=1)
    qkv_grad = jnp.einsum("td,tc->dc", attn_in, qkv_dlow, preferred_element_type=jnp.float32)
    first_part = lax.dot_general(qkv_dlow, qkv_mat, (((1,), (1,)), ((), ())), preferred_element_type=jnp.float32)
    first_grad = all_reduce(first_part.astype(jnp.bfloat16), cid=7).astype(jnp.float32)
    input_part, gain_one = rms_backward(first_grad, gains_back[0], unit_one, factor_one)
    input_grad = middle_grad + input_part
    gains_grad = jnp.stack([gain_one, gain_two, gain_three, gain_four])
    low_grads = [g.astype(jnp.bfloat16) for g in (qkv_grad, out_wgrad, gate_grad, up_grad, down_grad)]
    qkv_red, out_red, gate_red, up_red, down_red = [
        g.astype(jnp.float32) for g in scatter_rows(low_grads, 8)
    ]
    gains_red = lax.psum_scatter(
        gains_grad.astype(jnp.bfloat16), ("dp", "zero"), scatter_dimension=1, tiled=True
    ).astype(jnp.float32)
    reduced = (
        qkv_red[:, :heads_q],
        qkv_red[:, heads_q : heads_q + heads_k],
        qkv_red[:, heads_q + heads_k :],
        out_red.T,
        gate_red,
        up_red,
        down_red.T,
        gains_red,
    )
    masters = (
        query_weight,
        key_weight,
        value_weight,
        out_weight,
        gate_weight,
        up_weight,
        down_weight,
        norm_gains,
    )
    means = (query_mean, key_mean, value_mean, out_mean, gate_mean, up_mean, down_mean, gains_mean)
    squares = (
        query_square,
        key_square,
        value_square,
        out_square,
        gate_square,
        up_square,
        down_square,
        gains_square,
    )
    rates = (
        MODEL_WIDTH ** (-0.5),
        MODEL_WIDTH ** (-0.5),
        MODEL_WIDTH ** (-0.5),
        (QUERY_HEADS * HEAD_SIZE) ** (-0.5),
        MODEL_WIDTH ** (-0.5),
        MODEL_WIDTH ** (-0.5),
        FF ** (-0.5),
        gain_rate,
    )
    decays = (weight_decay,) * 7 + (0.0,)
    moments = []
    seconds = []
    updated = []
    for index in range(8):
        moment, second, master = adam_update(
            masters[index],
            means[index],
            squares[index],
            reduced[index],
            rates[index],
            decays[index],
        )
        moments.append(moment)
        seconds.append(second)
        updated.append(master)
    return (block_out, input_grad, *moments, *seconds, *updated)


def solution(mesh):
    in_specs = (
        P(("dp", "zero"), None),
        P(("dp", "zero"), None),
        P(("dp", "zero")),
        P(("dp", "zero"), "tensor"),
        P(("dp", "zero"), "tensor"),
        P(("dp", "zero"), "tensor"),
        P("tensor", ("dp", "zero")),
        P(("dp", "zero"), "tensor"),
        P(("dp", "zero"), "tensor"),
        P("tensor", ("dp", "zero")),
        P(None, ("dp", "zero")),
        P(("dp", "zero"), "tensor"),
        P(("dp", "zero"), "tensor"),
        P(("dp", "zero"), "tensor"),
        P("tensor", ("dp", "zero")),
        P(("dp", "zero"), "tensor"),
        P(("dp", "zero"), "tensor"),
        P("tensor", ("dp", "zero")),
        P(None, ("dp", "zero")),
        P(("dp", "zero"), "tensor"),
        P(("dp", "zero"), "tensor"),
        P(("dp", "zero"), "tensor"),
        P("tensor", ("dp", "zero")),
        P(("dp", "zero"), "tensor"),
        P(("dp", "zero"), "tensor"),
        P("tensor", ("dp", "zero")),
        P(None, ("dp", "zero")),
    )
    out_specs = (
        P(("dp", "zero"), None),
        P(("dp", "zero"), None),
        P(("dp", "zero"), "tensor"),
        P(("dp", "zero"), "tensor"),
        P(("dp", "zero"), "tensor"),
        P("tensor", ("dp", "zero")),
        P(("dp", "zero"), "tensor"),
        P(("dp", "zero"), "tensor"),
        P("tensor", ("dp", "zero")),
        P(None, ("dp", "zero")),
        P(("dp", "zero"), "tensor"),
        P(("dp", "zero"), "tensor"),
        P(("dp", "zero"), "tensor"),
        P("tensor", ("dp", "zero")),
        P(("dp", "zero"), "tensor"),
        P(("dp", "zero"), "tensor"),
        P("tensor", ("dp", "zero")),
        P(None, ("dp", "zero")),
        P(("dp", "zero"), "tensor"),
        P(("dp", "zero"), "tensor"),
        P(("dp", "zero"), "tensor"),
        P("tensor", ("dp", "zero")),
        P(("dp", "zero"), "tensor"),
        P(("dp", "zero"), "tensor"),
        P("tensor", ("dp", "zero")),
        P(None, ("dp", "zero")),
    )
    return jax.shard_map(
        per_device, mesh=mesh, in_specs=in_specs, out_specs=out_specs, check_vma=False
    )
```

```python
import functools

import jax
import jax.numpy as jnp
from jax import lax
from jax.experimental import pallas as pl
from jax.experimental.pallas import tpu as pltpu
from jax.sharding import PartitionSpec as P

MESH = pl.DeviceIdType.MESH

MODEL_WIDTH = 2304
QUERY_HEADS = 8
HEAD_SIZE = 256
FF = 9216
STEP = 10
W = MODEL_WIDTH


norm_eps = 1e-06
soft_cap = 50.0
rope_base = 10000.0
beta_one = 0.9
beta_two = 0.95
adam_eps = 1e-08
weight_decay = 0.1
gain_rate = 0.7


def rms_forward(value_rows, gain):
    factor = lax.rsqrt(jnp.mean(value_rows * value_rows, axis=-1, keepdims=True) + norm_eps)
    normed = value_rows * factor
    return (normed * gain, normed, factor)


def rms_backward(grad, gain, normed, factor):
    scaled = grad * gain
    inner = jnp.mean(scaled * normed, axis=-1, keepdims=True)
    return (factor * (scaled - normed * inner), jnp.sum(grad * normed, axis=0))


def rope_tables(segment):
    index = jnp.arange(segment.shape[0], dtype=jnp.int32)
    earlier = jnp.concatenate([jnp.full((1,), -1, jnp.int32), segment[:-1]])
    first = lax.cummax(jnp.where(segment != earlier, index, 0), axis=0)
    place = (index - first).astype(jnp.float32)
    inverse = rope_base ** (-jnp.arange(0, HEAD_SIZE, 2, dtype=jnp.float32) / HEAD_SIZE)
    angle = place[:, None] * inverse[None, :]
    return (jnp.cos(angle)[:, None, :], jnp.sin(angle)[:, None, :])


def rotate(value_rows, cosine, sine):
    half = value_rows.shape[-1] // 2
    first = value_rows[..., :half]
    second = value_rows[..., half:]
    return jnp.concatenate(
        [first * cosine - second * sine, second * cosine + first * sine], axis=-1
    )


def unrotate(value_rows, cosine, sine):
    half = value_rows.shape[-1] // 2
    first = value_rows[..., :half]
    second = value_rows[..., half:]
    return jnp.concatenate(
        [first * cosine + second * sine, second * cosine - first * sine], axis=-1
    )


def gated(gate_val, up_val):
    return jax.nn.gelu(gate_val, approximate=True) * up_val


def score_block(query_blk, start, rotated_keys, segment):
    group_size = query_blk.shape[0]
    total = rotated_keys.shape[0]
    raw = jnp.einsum(
        "qhgd,khd->hgqk", query_blk, rotated_keys, preferred_element_type=jnp.float32
    ) * HEAD_SIZE ** (-0.5)
    bent = jnp.tanh(raw / soft_cap)
    rows_idx = start + jnp.arange(group_size, dtype=jnp.int32)
    cols_idx = jnp.arange(total, dtype=jnp.int32)
    visible = (cols_idx[None, :] <= rows_idx[:, None]) & (segment[:, None] == segment[None, :])
    return (jnp.where(visible, soft_cap * bent, -jnp.inf), bent)


def split_blocks(value_rows, heads_kv):
    total = value_rows.shape[0]
    count = total // total
    starts = jnp.arange(count, dtype=jnp.int32) * total
    return (value_rows.reshape(count, total, heads_kv, -1, HEAD_SIZE), starts)


def attend_forward(rotated_queries, rotated_keys, value_low, segment):
    total = rotated_queries.shape[0]
    blocks, starts = split_blocks(rotated_queries, rotated_keys.shape[1])

    def one_block(packed):
        query_blk, start = packed
        masked, bent = score_block(query_blk, start, rotated_keys, segment)
        top = jnp.max(masked, axis=-1, keepdims=True)
        expo = jnp.exp(masked - top)
        total_sum = jnp.sum(expo, axis=-1, keepdims=True)
        probs = expo / total_sum
        mixed = jnp.einsum(
            "hgqk,khd->qhgd",
            probs.astype(jnp.bfloat16),
            value_low,
            preferred_element_type=jnp.float32,
        )
        return (mixed.astype(jnp.bfloat16), top + jnp.log(total_sum))

    mixed, log_sums = lax.map(one_block, (blocks, starts))
    return (mixed.reshape(total, -1), log_sums)


def attend_backward(rotated_queries, rotated_keys, value_low, segment, log_sums, dout_low):
    total = rotated_queries.shape[0]
    heads_kv = rotated_keys.shape[1]
    blocks, starts = split_blocks(rotated_queries, heads_kv)
    dout_blocks, unused = split_blocks(dout_low, heads_kv)
    scale = HEAD_SIZE ** (-0.5)

    def one_block(carry, packed):
        key_grad, value_grad = carry
        query_blk, dout_blk, lse_blk, start = packed
        masked, bent = score_block(query_blk, start, rotated_keys, segment)
        probs = jnp.exp(masked - lse_blk)
        dprobs = jnp.einsum(
            "qhgd,khd->hgqk", dout_blk, value_low, preferred_element_type=jnp.float32
        )
        inner = jnp.sum(probs * dprobs, axis=-1, keepdims=True)
        dscore = (probs * (dprobs - inner) * (1.0 - bent * bent)).astype(jnp.bfloat16)
        query_grad = (
            jnp.einsum("hgqk,khd->qhgd", dscore, rotated_keys, preferred_element_type=jnp.float32)
            * scale
        )
        key_grad = (
            key_grad
            + jnp.einsum("hgqk,qhgd->khd", dscore, query_blk, preferred_element_type=jnp.float32)
            * scale
        )
        value_grad = value_grad + jnp.einsum(
            "hgqk,qhgd->khd",
            probs.astype(jnp.bfloat16),
            dout_blk,
            preferred_element_type=jnp.float32,
        )
        return ((key_grad, value_grad), query_grad)

    zeros = jnp.zeros(rotated_keys.shape, jnp.float32)
    (key_grad, value_grad), query_grads = lax.scan(
        one_block, (zeros, zeros), (blocks, dout_blocks, log_sums, starts)
    )
    return (query_grads.reshape(total, -1, HEAD_SIZE), key_grad, value_grad)


def adam_update(master, mean, square, grad, rate, decay):
    moment = beta_one * mean + (1.0 - beta_one) * grad
    second = beta_two * square + (1.0 - beta_two) * grad * grad
    direction = (
        moment / (1.0 - beta_one**STEP) / (jnp.sqrt(second / (1.0 - beta_two**STEP)) + adam_eps)
    )
    return (moment, second, master - rate * (direction + decay * master))


def remote(src,dst,ss,rs,dev):
    return pltpu.make_async_remote_copy(src_ref=src,dst_ref=dst,send_sem=ss,recv_sem=rs,device_id=dev,device_id_type=MESH)

class Chain:
    def __init__(self, half, ch, P, RE, RM, O, sp, so, ve, vm, vo, lags=(1,2,3,4)):
        self.p = lax.axis_index("tensor"); p=self.p
        self.reg=half//2; self.ch=ch; self.nt=self.reg//ch
        self.P,self.RE,self.RM,self.O=P,RE,RM,O
        self.sp,self.so,self.ve,self.vm,self.vo=sp,so,ve,vm,vo
        self.lags=lags
        self.end = (p==0)|(p==3)
        self.mid = (p==1)|(p==2)
        self.to_mid = {"tensor": jnp.where(p<2, 1, 2)}
        self.to_end = {"tensor": jnp.where(p<2, 0, 3)}
        self.to_oth = {"tensor": jnp.where(p<2, 2, 1)}
        self.own = jnp.where(p<2,0,1); self.oth=1-self.own
    def rows(self, part, t):
        return pl.ds(pl.multiple_of(part*self.reg+t*self.ch,16), self.ch)
    def trow(self,t): return pl.ds(pl.multiple_of(t*self.ch,16), self.ch)
    def r1(self,h,t):
        for part in (0,1):
            r=self.rows(part,t)
            remote(self.P.at[h,r],self.RE.at[h,r],self.sp.at[h,t,part],self.ve.at[h,t,part],self.to_mid).start()
    def r2(self,h,t):
        r=self.rows(self.oth,t)
        remote(self.P.at[h,r],self.RE.at[h,r],self.sp.at[h,t,0],self.ve.at[h,t,self.oth],self.to_end).wait_recv()
        self.P[h,r,:]=(self.P[h,r,:].astype(jnp.float32)+self.RE[h,r,:].astype(jnp.float32)).astype(jnp.bfloat16)
        remote(self.P.at[h,r],self.RM.at[h,self.trow(t)],self.sp.at[h,t,0],self.vm.at[h,t],self.to_oth).start()
    def r3(self,h,t):
        r=self.rows(self.own,t); q=self.trow(t)
        remote(self.P.at[h,r],self.RE.at[h,r],self.sp.at[h,t,0],self.ve.at[h,t,self.own],self.to_end).wait_recv()
        remote(self.P.at[h,r],self.RM.at[h,q],self.sp.at[h,t,0],self.vm.at[h,t],self.to_oth).wait_recv()
        self.O[h,r,:]=(self.P[h,r,:].astype(jnp.float32)+self.RE[h,r,:].astype(jnp.float32)+self.RM[h,q,:].astype(jnp.float32)).astype(jnp.bfloat16)
        remote(self.O.at[h,r],self.O.at[h,r],self.so.at[h,t,0],self.vo.at[h,t,self.own],self.to_end).start()
        remote(self.O.at[h,r],self.O.at[h,r],self.so.at[h,t,1],self.vo.at[h,t,self.own],self.to_oth).start()
    def b4(self,h,t):
        r=self.rows(self.oth,t)
        c=remote(self.O.at[h,r],self.O.at[h,r],self.so.at[h,t,2],self.vo.at[h,t,self.oth],self.to_end)
        c.wait_recv(); c.start()
    def b5_end(self,h,t):
        for part in (0,1):
            r=self.rows(part,t)
            remote(self.O.at[h,r],self.O.at[h,r],self.so.at[h,t,0],self.vo.at[h,t,part],self.to_mid).wait_recv()
            remote(self.P.at[h,r],self.RE.at[h,r],self.sp.at[h,t,part],self.ve.at[h,t,part],self.to_mid).wait_send()
    def b5_mid(self,h,t):
        r=self.rows(self.own,t)
        remote(self.P.at[h,r],self.RE.at[h,r],self.sp.at[h,t,0],self.ve.at[h,t,0],self.to_oth).wait_send()
        for i in range(3):
            remote(self.O.at[h,r],self.O.at[h,r],self.so.at[h,t,i],self.vo.at[h,t,0],self.to_end).wait_send()
    def tick(self, T, lo, hi):
        nt=self.nt
        def at(c, cond, fns):
            ok=(c>=lo)&(c<hi)
            j=c//nt; h=j%2; t=c%nt
            @pl.when(ok&cond)
            def _():
                for f in fns: f(h,t)
        l1,l2,l3,l4=self.lags
        at(T,self.end,[self.r1])
        at(T-l1,self.mid,[self.r2])
        at(T-l2,self.mid,[self.r3])
        at(T-l3,self.mid,[self.b4])
        at(T-l4,self.end,[self.b5_end])
        at(T-l4,self.mid,[self.b5_mid])

def chain_scratch(half,ch):
    nt=half//2//ch
    B=jnp.bfloat16; D=pltpu.SemaphoreType.DMA
    return [pltpu.VMEM((2,half,W),B),pltpu.VMEM((2,half,W),B),pltpu.VMEM((2,half//2,W),B),pltpu.VMEM((2,half,W),B),
            D((2,nt,2)),D((2,nt,3)),D((2,nt,2)),D((2,nt)),D((2,nt,2))]

def line_barrier():
    te=lax.axis_index("tensor")
    bar=pltpu.get_barrier_semaphore()
    @pl.when(te<3)
    def _(): pl.semaphore_signal(bar, inc=1, device_id={"tensor":te+1}, device_id_type=MESH)
    @pl.when(te>0)
    def _(): pl.semaphore_signal(bar, inc=1, device_id={"tensor":te-1}, device_id_type=MESH)
    pl.semaphore_wait(bar, (te<3).astype(jnp.int32)+(te>0).astype(jnp.int32))

def ar_kernel(half,ch,lags,a_ref,o_ref,P,RE,RM,O,sp,so,ve,vm,vo,isem,osem):
    ins=[pltpu.make_async_copy(a_ref.at[pl.ds(h*half,half)],P.at[h],isem.at[h]) for h in (0,1)]
    for c in ins: c.start()
    line_barrier()
    for c in ins: c.wait()
    C=Chain(half,ch,P,RE,RM,O,sp,so,ve,vm,vo,lags)
    n=2*C.nt
    def body(T,_):
        C.tick(T,0,n); return 0
    lax.fori_loop(0,n+lags[-1],body,0)
    outs=[pltpu.make_async_copy(O.at[h],o_ref.at[pl.ds(h*half,half)],osem.at[h]) for h in (0,1)]
    for c in outs: c.start()
    for c in outs: c.wait()

def all_reduce(a,ch=16,lags=(2,4,6,8),cid=1):
    rows=a.shape[0]; half=rows//2
    return pl.pallas_call(functools.partial(ar_kernel,half,ch,lags),
        out_shape=jax.ShapeDtypeStruct(a.shape,a.dtype),
        in_specs=[pl.BlockSpec(memory_space=pl.ANY)],out_specs=pl.BlockSpec(memory_space=pl.ANY),
        scratch_shapes=chain_scratch(half,ch)+[pltpu.SemaphoreType.DMA((2,)),pltpu.SemaphoreType.DMA((2,))],
        compiler_params=pltpu.CompilerParams(collective_id=cid,has_side_effects=True,vmem_limit_bytes=60*2**20))(a)

def coords():
    dp,ze=lax.axis_index("dp"),lax.axis_index("zero")
    x=dp//2; c=dp%2
    return x,c,ze
def sid(x,c,y): return (x*2+c)*2+y
class Plane:
    def __init__(self):
        x,c,y=coords()
        self.x,self.c,self.y=x,c,y
        self.toX={"dp":(1-x)*2+c}; self.toY={"zero":1-y}; self.toC={"dp":x*2+1-c}
        self.lane=[sid(x,c,y),sid(1-x,c,y),sid(x,c,1-y),sid(1-x,c,1-y)]
        d=1-c
        self.other=[sid(x,d,y),sid(1-x,d,y),sid(x,d,1-y),sid(1-x,d,1-y)]
        self.is0=c==0; self.is1=c==1
def plane_signal():
    x,c,y=coords()
    bar=pltpu.get_barrier_semaphore()
    for dev in ({"dp":(1-x)*2+c},{"zero":1-y},{"dp":x*2+1-c}):
        pl.semaphore_signal(bar, inc=1, device_id=dev, device_id_type=MESH)
def plane_barrier():
    plane_signal(); pl.semaphore_wait(pltpu.get_barrier_semaphore(),3)

class Gather:
    def __init__(self, units, ss, rs, ls):
        self.u=units; self.ss,self.rs,self.ls=ss,rs,ls; self.pl=Plane()
    def refs(self,i):
        S,F,r0,rr=self.u[i]; r=pl.ds(r0,rr)
        return S.at[r], (lambda s: F.at[s,r])
    def a(self,i):
        S,F=self.refs(i); q=self.pl; own=q.lane[0]
        remote(S,F(own),self.ss.at[i,0],self.rs.at[i,0],q.toX).start()
        remote(S,F(own),self.ss.at[i,1],self.rs.at[i,1],q.toY).start()
        remote(S,F(own),self.ss.at[i,2],self.rs.at[i,3],q.toC).start()
        pltpu.make_async_copy(S,F(own),self.ls.at[i]).start()
    def b(self,i):
        S,F=self.refs(i); q=self.pl; X,Y=q.lane[1],q.lane[2]
        remote(S,F(X),self.ss.at[i,0],self.rs.at[i,0],q.toX).wait_recv()
        @pl.when(q.is1)
        def _(): remote(F(X),F(X),self.ss.at[i,3],self.rs.at[i,2],q.toY).start()
        remote(F(X),F(X),self.ss.at[i,4],self.rs.at[i,4],q.toC).start()
        remote(S,F(Y),self.ss.at[i,1],self.rs.at[i,1],q.toY).wait_recv()
        @pl.when(q.is0)
        def _(): remote(F(Y),F(Y),self.ss.at[i,3],self.rs.at[i,2],q.toX).start()
        remote(F(Y),F(Y),self.ss.at[i,5],self.rs.at[i,5],q.toC).start()
    def d(self,i):
        S,F=self.refs(i); q=self.pl; D=q.lane[3]
        c=remote(F(D),F(D),self.ss.at[i,6],self.rs.at[i,6],q.toC)
        remote(S,F(D),self.ss.at[i,3],self.rs.at[i,2],q.toX).wait_recv()
        c.start()
    def e(self,i):
        S,F=self.refs(i); q=self.pl
        for j in range(4):
            remote(S,F(q.other[j]),self.ss.at[i,0],self.rs.at[i,3+j],q.toC).wait_recv()
        pltpu.make_async_copy(S,F(q.lane[0]),self.ls.at[i]).wait()
        for j in range(7):
            remote(S,S,self.ss.at[i,j],self.rs.at[i,0],q.toC).wait_send()
    def tick(self,T):
        n=len(self.u)
        if 0<=T<n: self.a(T)
        if 0<=T-1<n: self.b(T-1)
        if 0<=T-2<n: self.d(T-2)
        if 0<=T-3<n: self.e(T-3)
    @property
    def ticks(self): return len(self.u)+3
def gather_sems(n):
    D=pltpu.SemaphoreType.DMA
    return [D((n,7)),D((n,7)),D((n,))]

def ag_kernel(nw,rr,*refs):
    S=refs[:nw]; F=refs[nw:2*nw]; ss,rs,ls=refs[2*nw:]
    plane_barrier()
    units=[(S[k],F[k],r0,rr) for k in range(nw) for r0 in range(0,S[k].shape[0],rr)]
    G=Gather(units,ss,rs,ls)
    for T in range(G.ticks): G.tick(T)
def all_gather(shards,rr=96,cid=2):
    nw=len(shards); n=sum(s.shape[0]//rr for s in shards)
    out=pl.pallas_call(functools.partial(ag_kernel,nw,rr),
        out_shape=[jax.ShapeDtypeStruct((8,)+s.shape,s.dtype) for s in shards],
        in_specs=[pl.BlockSpec(memory_space=pl.ANY)]*nw,out_specs=[pl.BlockSpec(memory_space=pl.ANY)]*nw,
        scratch_shapes=gather_sems(n),
        compiler_params=pltpu.CompilerParams(collective_id=cid,has_side_effects=True,vmem_limit_bytes=60*2**20))(*shards)
    return [o.reshape(-1,s.shape[1]) for o,s in zip(out,shards)]

class Scatter:
    def __init__(self,units,LB,OB,depth,ss,rs,ls):
        self.u=units; self.LB,self.OB,self.depth=LB,OB,depth; self.ss,self.rs,self.ls=ss,rs,ls; self.pl=Plane()
    def get(self,i):
        G,O,CB,DB,XB,YB,r0,rr,C=self.u[i]; r=pl.ds(r0,rr); s=i%self.depth
        g=lambda k: G.at[k,r]
        lb=lambda j: self.LB.at[s,j,pl.ds(0,rr),pl.ds(0,C)]
        return g,lb,O.at[r],CB,DB,XB,YB,r,s,rr,C
    def p1(self,i):
        g,lb,O,CB,DB,XB,YB,r,s,rr,C=self.get(i); q=self.pl
        for j in (3,1,2,0):
            remote(g(q.other[j]),CB.at[j,r],self.ss.at[i,j],self.rs.at[i,j],q.toC).start()
            pltpu.make_async_copy(g(q.lane[j]),lb(j),self.ls.at[i,j]).start()
    def p2(self,i):
        g,lb,O,CB,DB,XB,YB,r,s,rr,C=self.get(i); q=self.pl
        for j in (3,1,2,0):
            pltpu.make_async_copy(g(q.lane[j]),lb(j),self.ls.at[i,j]).wait()
            remote(g(q.other[j]),CB.at[j,r],self.ss.at[i,j],self.rs.at[i,j],q.toC).wait_recv()
            v=self.LB[s,j,pl.ds(0,rr),pl.ds(0,C)].astype(jnp.float32)+CB[j,r].astype(jnp.float32)
            self.LB[s,j,pl.ds(0,rr),pl.ds(0,C)]=v.astype(jnp.bfloat16)
            if j==3:
                @pl.when(q.is0)
                def _(): remote(lb(3),DB.at[r],self.ss.at[i,4],self.rs.at[i,4],q.toX).start()
                @pl.when(q.is1)
                def _(): remote(lb(3),DB.at[r],self.ss.at[i,4],self.rs.at[i,4],q.toY).start()
            if j==1:
                @pl.when(q.is0)
                def _(): remote(lb(1),XB.at[r],self.ss.at[i,5],self.rs.at[i,5],q.toX).start()
            if j==2:
                @pl.when(q.is1)
                def _(): remote(lb(2),YB.at[r],self.ss.at[i,5],self.rs.at[i,6],q.toY).start()
    def p3(self,i):
        g,lb,O,CB,DB,XB,YB,r,s,rr,C=self.get(i); q=self.pl
        remote(lb(3),DB.at[r],self.ss.at[i,4],self.rs.at[i,4],q.toX).wait_recv()
        def relay(j,buf,sem,dev):
            v=self.LB[s,j,pl.ds(0,rr),pl.ds(0,C)].astype(jnp.float32)+DB[r].astype(jnp.float32)
            self.LB[s,j,pl.ds(0,rr),pl.ds(0,C)]=v.astype(jnp.bfloat16)
            remote(lb(j),buf.at[r],self.ss.at[i,6],self.rs.at[i,sem],dev).start()
        @pl.when(q.is0)
        def _(): relay(2,YB,6,q.toY)
        @pl.when(q.is1)
        def _(): relay(1,XB,5,q.toX)
    def p4(self,i):
        g,lb,O,CB,DB,XB,YB,r,s,rr,C=self.get(i); q=self.pl
        remote(lb(0),XB.at[r],self.ss.at[i,5],self.rs.at[i,5],q.toX).wait_recv()
        remote(lb(0),YB.at[r],self.ss.at[i,5],self.rs.at[i,6],q.toY).wait_recv()
        v=self.LB[s,0,pl.ds(0,rr),pl.ds(0,C)].astype(jnp.float32)+XB[r].astype(jnp.float32)+YB[r].astype(jnp.float32)
        ob=i%2
        self.OB[ob,pl.ds(0,rr),pl.ds(0,C)]=v.astype(self.OB.dtype)
        pltpu.make_async_copy(self.OB.at[ob,pl.ds(0,rr),pl.ds(0,C)],O,self.ls.at[i,4]).start()
        for j in range(7):
            remote(lb(0),XB.at[r],self.ss.at[i,j],self.rs.at[i,0],q.toX).wait_send()
    def p5(self,i):
        g,lb,O,CB,DB,XB,YB,r,s,rr,C=self.get(i)
        pltpu.make_async_copy(self.OB.at[i%2,pl.ds(0,rr),pl.ds(0,C)],O,self.ls.at[i,4]).wait()
    def tick(self,T):
        n=len(self.u)
        if 0<=T<n: self.p1(T)
        if 0<=T-1<n: self.p2(T-1)
        if 0<=T-2<n: self.p3(T-2)
        if 0<=T-4<n: self.p5(T-4)
        if 0<=T-3<n: self.p4(T-3)
    @property
    def ticks(self): return len(self.u)+4
def scatter_scratch(n,cols,rr,depth=4,rows=288):
    D=pltpu.SemaphoreType.DMA; B=jnp.bfloat16
    land=[]
    for C in cols: land+= [pltpu.VMEM((4,rows,C),B)]+[pltpu.VMEM((rows,C),B)]*3
    m=max(cols)
    return land+[pltpu.VMEM((depth,4,rr,m),B),pltpu.VMEM((2,rr,m),B),D((n,7)),D((n,7)),D((n,5))]
F32=jnp.float32; BF=jnp.bfloat16
class GatherD(Gather):
    def __init__(self,S,F,rr,lags,ss,rs,ls):
        self.S,self.F,self.rr=S,F,rr; self.shard=S.shape[1]; self.per=self.shard//rr; self.n=S.shape[0]*self.per
        self.lags=lags; self.ss,self.rs,self.ls=ss,rs,ls; self.pl=Plane()
    def refs(self,i):
        k=i//self.per; r0=(i%self.per)*self.rr
        return (self.S.at[k,pl.ds(pl.multiple_of(r0,16),self.rr)],
                lambda s: self.F.at[k,pl.ds(pl.multiple_of(s*self.shard+r0,16),self.rr)])
    def tick(self,T):
        lb,ld,le=self.lags
        for lag,f in ((0,self.a),(lb,self.b),(ld,self.d),(le,self.e)):
            i=T-lag
            @pl.when((i>=0)&(i<self.n))
            def _(): f(i)
    def done(self,k): return (k+1)*self.per-1+self.lags[2]+1

def gelu_parts(g):
    k=0.7978845608028654; c=0.044715
    t=jnp.tanh(k*(g+c*g*g*g))
    act=0.5*g*(1.0+t)
    der=0.5*(1.0+t)+0.5*g*(1.0-t*t)*k*(1.0+3.0*c*g*g)
    return act,der
def nt_dot(a,b): return lax.dot_general(a,b,(((1,),(1,)),((),())),preferred_element_type=F32)
def rsq(v): return lax.rsqrt(jnp.mean(v*v,axis=-1,keepdims=True)+1e-6)

def m_kernel(gather,half,ch,lags,grr,glags,tn,*refs):
    (a_ref,x_ref,dy_ref,g_ref,s_ref,
     at_out,f_out,d_out,n2_out,hid_out,dg_out,du_out,df_out,
     Wt,GU,N2,HID,XS,P,RE,RM,O,sp,so,ve,vm,vo,gss,grs,gls,isem,osem)=refs
    C=Chain(half,ch,P,RE,RM,O,sp,so,ve,vm,vo,lags)
    L=lags[-1]; nt=C.nt; nj=Wt.shape[2]//tn
    def rows(h): return pl.ds(h*half,half)
    def cp(src,dst,sem): return pltpu.make_async_copy(src,dst,sem)
    ins=[cp(a_ref.at[rows(h)],P.at[h],isem.at[h]) for h in (0,1)]
    for c in ins: c.start()
    xin=lambda ref,h: cp(ref.at[rows(h)],XS,isem.at[2])
    xin(x_ref,0).start()
    line_signal()
    if gather:
        plane_signal()
        pl.semaphore_wait(pltpu.get_barrier_semaphore(),line_count()+3)
        Gt=GatherD(s_ref,Wt,grr,glags,gss,grs,gls)
    else:
        pl.semaphore_wait(pltpu.get_barrier_semaphore(),line_count())
        wc=[cp(s_ref.at[k],Wt.at[k],gls.at[k]) for k in range(3)]
        for c in wc: c.start()
        for c in wc: c.wait()
    for c in ins: c.wait()
    st={'g':0}
    def ag(upto):
        if not gather: return
        if upto>st['g']:
            lax.fori_loop(st['g'],upto,lambda T,_: (Gt.tick(T),0)[1],0); st['g']=upto
    def ticks(T0,T1,lo,hi,every_g=0):
        g0=st['g']
        def body(T,_):
            C.tick(T,lo,hi)
            if every_g and gather:
                @pl.when((T-T0)%every_g==0)
                def _(): Gt.tick(g0+(T-T0)//every_g)
            return 0
        if T1>T0: lax.fori_loop(T0,T1,body,0)
        if every_g and gather: st['g']=g0+(T1-T0+every_g-1)//every_g
    def units(n,fn,T0=0,every=0,lo=0,hi=0,limit=0):
        def body(i,_):
            fn(i)
            if every:
                @pl.when((i+1)%every==0)
                def _(): C.tick(T0+i//every,lo,hi)
            return 0
        lax.fori_loop(0,n,body,0)
        return T0+(n//every if every else 0)
    nr=32
    def rch(i): return pl.ds(pl.multiple_of(i*nr,nr),nr)
    g1=g_ref[1:2,:]; g2=g_ref[2:3,:]; g3=g_ref[3:4,:]
    def norm1(h):
        def f(i):
            r=rch(i)
            a=O[h,r,:].astype(F32)
            h1=XS[r,:].astype(F32)+a*rsq(a)*g1
            N2[r,:]=(h1*rsq(h1)*g2).astype(BF)
        return f
    def normf(h):
        def f(i):
            r=rch(i)
            v=O[h,r,:].astype(F32); q=rsq(v); z=v*q
            s=XS[r,:].astype(F32)*g3
            N2[r,:]=(q*(s-z*jnp.mean(s*z,axis=-1,keepdims=True))).astype(BF)
        return f
    def col(j): return pl.ds(pl.multiple_of(j*tn,tn),tn)
    def gate(h):
        def f(j): GU[0,h,:,col(j)]=jnp.dot(N2[...],Wt[0,:,col(j)],preferred_element_type=F32).astype(BF)
        return f
    def up(h):
        def f(j):
            u=jnp.dot(N2[...],Wt[1,:,col(j)],preferred_element_type=F32)
            g=GU[0,h,:,col(j)].astype(F32)
            act,_=gelu_parts(g)
            GU[1,h,:,col(j)]=u.astype(BF)
            HID[:,col(j)]=(act*u).astype(BF)
        return f
    def down(h):
        def f(j): P[h,:,col(j)]=nt_dot(HID[...],Wt[2,col(j),:]).astype(BF)
        return f
    def bwd1(h):
        def f(j):
            d=jnp.dot(N2[...],Wt[2,:,col(j)],preferred_element_type=F32)
            g=GU[0,h,:,col(j)].astype(F32); u=GU[1,h,:,col(j)].astype(F32)
            act,der=gelu_parts(g)
            GU[0,h,:,col(j)]=(d*u*der).astype(BF)
            GU[1,h,:,col(j)]=(d*act).astype(BF)
        return f
    def bwd2(h):
        def f(j):
            P[h,:,col(j)]=(nt_dot(GU[0,h],Wt[0,col(j),:])+nt_dot(GU[1,h],Wt[1,col(j),:])).astype(BF)
        return f
    nn=half//nr
    oc={}
    def out(name,src,dst,i):
        c=cp(src,dst,osem.at[i]); c.start(); oc[name]=c
    def fin(name): oc.pop(name).wait()
    ticks(0,nt+L,0,2*nt,2)
    out('at0',O.at[0],at_out.at[rows(0)],0)
    xin(x_ref,0).wait()
    if gather: ag(Gt.done(0))
    T=nt+L
    T=units(nn,norm1(0),T,7,0,2*nt)
    xin(x_ref,1).start()
    out('n2',N2,n2_out.at[rows(0)],1)
    T=units(nj,gate(0),T,3,0,2*nt)
    if gather:
        need=Gt.done(1)-st['g']; k=max(2*nt+L-T,0)
        while st['g']<Gt.done(1):
            ag(st['g']+1)
            T1=min(T+2,2*nt+L); ticks(T,T1,0,2*nt); T=T1
    T=units(nj,up(0),T,3,0,2*nt) if T+nj//3<=2*nt+L else (units(nj,up(0)),T)[1]
    out('hid',HID,hid_out.at[rows(0)],2)
    ticks(T,2*nt+L,0,2*nt)
    out('at1',O.at[1],at_out.at[rows(1)],3)
    xin(x_ref,1).wait()
    fin('n2')
    units(nn,norm1(1))
    xin(dy_ref,0).start()
    out('n2',N2,n2_out.at[rows(1)],1)
    units(nj,gate(1))
    if gather: ag(Gt.done(2))
    units(nj,down(0))
    fin('at0')
    T=2*nt
    fin('hid')
    T=units(nj,up(1),T,2,2*nt,3*nt)
    out('hid',HID,hid_out.at[rows(1)],2)
    T=units(nj,down(1),T,2,2*nt,3*nt)
    fin('at1')
    ticks(T,3*nt+L,2*nt,4*nt)
    T=3*nt+L
    out('f0',O.at[0],f_out.at[rows(0)],0)
    xin(dy_ref,0).wait()
    fin('n2')
    T=units(nn,normf(0),T,7,2*nt,4*nt)
    xin(dy_ref,1).start()
    out('df',N2,df_out.at[rows(0)],1)
    T=units(nj,bwd1(0),T,3,2*nt,4*nt)
    out('dg0',GU.at[0,0],dg_out.at[rows(0)],4); out('du0',GU.at[1,0],du_out.at[rows(0)],5)
    T=units(nj,bwd2(0),T,2,2*nt,4*nt)
    fin('f0')
    hi=5*nt
    ticks(T,4*nt+L,2*nt,hi)
    out('f1',O.at[1],f_out.at[rows(1)],3)
    T=4*nt+L
    xin(dy_ref,1).wait()
    fin('df')
    T=units(nn,normf(1),T,7,4*nt,hi)
    out('df',N2,df_out.at[rows(1)],1)
    T=units(nj,bwd1(1),T,3,4*nt,hi)
    out('dg1',GU.at[0,1],dg_out.at[rows(1)],6); out('du1',GU.at[1,1],du_out.at[rows(1)],7)
    T=units(nj,bwd2(1),T,2,4*nt,hi)
    fin('f1')
    ticks(T,5*nt+L,4*nt,6*nt)
    out('d0',O.at[0],d_out.at[rows(0)],0)
    ticks(5*nt+L,6*nt+L,4*nt,6*nt)
    out('d1',O.at[1],d_out.at[rows(1)],3)
    for k in list(oc): fin(k)

def line_signal():
    te=lax.axis_index("tensor")
    bar=pltpu.get_barrier_semaphore()
    @pl.when(te<3)
    def _(): pl.semaphore_signal(bar, inc=1, device_id={"tensor":te+1}, device_id_type=MESH)
    @pl.when(te>0)
    def _(): pl.semaphore_signal(bar, inc=1, device_id={"tensor":te-1}, device_id_type=MESH)
def line_count():
    te=lax.axis_index("tensor")
    return (te<3).astype(jnp.int32)+(te>0).astype(jnp.int32)

def mlp_both(part,x,dy,gains,shards,gather,cid=9,ch=16,lags=(1,2,3,4),grr=48,glags=(2,3,5),tn=256):
    rows=part.shape[0]; half=rows//2; D=pltpu.SemaphoreType.DMA; ff=shards.shape[2]
    ng=(shards.shape[0]*shards.shape[1]//grr) if gather else 3
    act=jax.ShapeDtypeStruct((rows,W),BF); wide=jax.ShapeDtypeStruct((rows,ff),BF)
    A=pl.BlockSpec(memory_space=pl.ANY)
    return pl.pallas_call(functools.partial(m_kernel,gather,half,ch,lags,grr,glags,tn),
        out_shape=[act,act,act,act,wide,wide,wide,act],
        in_specs=[A,A,A,pl.BlockSpec(memory_space=pltpu.VMEM),A],out_specs=[A]*8,
        scratch_shapes=[pltpu.VMEM((3,W,ff),BF),pltpu.VMEM((2,2,half,ff),BF),pltpu.VMEM((half,W),BF),pltpu.VMEM((half,ff),BF),pltpu.VMEM((half,W),BF)]
            +chain_scratch(half,ch)+gather_sems(ng)+[D((3,)),D((8,))],
        compiler_params=pltpu.CompilerParams(collective_id=cid,has_side_effects=True,vmem_limit_bytes=63*2**20))(part,x,dy,gains,shards)
def n_kernel(nw,half,ch,lags,rr,every,*refs):
    a_ref=refs[0]; G=refs[1:1+nw]; o_ref=refs[1+nw]; Og=refs[2+nw:2+2*nw]
    r=refs[2+2*nw:]
    land=r[:4*nw]; LB,OB,ss,rs,ls=r[4*nw:4*nw+5]
    P,RE,RM,O,sp,so,ve,vm,vo,isem,osem=r[4*nw+5:]
    ins=[pltpu.make_async_copy(a_ref.at[pl.ds(h*half,half)],P.at[h],isem.at[h]) for h in (0,1)]
    for c in ins: c.start()
    line_signal(); plane_signal()
    pl.semaphore_wait(pltpu.get_barrier_semaphore(),line_count()+3)
    for c in ins: c.wait()
    C=Chain(half,ch,P,RE,RM,O,sp,so,ve,vm,vo,lags)
    units=[(G[k],Og[k],*land[4*k:4*k+4],r0,rr,G[k].shape[2]) for k in range(nw) for r0 in range(0,G[k].shape[1],rr)]
    S=Scatter(units,LB,OB,LB.shape[0],ss,rs,ls)
    n=2*C.nt; total=n+lags[-1]; outs=[]
    def out(h):
        c=pltpu.make_async_copy(O.at[h],o_ref.at[pl.ds(h*half,half)],osem.at[h]); c.start(); outs.append(c)
    at=0
    for T in range(S.ticks):
        S.tick(T)
        to=min(total,at+every)
        lax.fori_loop(at,to,lambda t,_: (C.tick(t,0,n),0)[1],0); at=to
        if at==total and not outs: out(0); out(1)
    lax.fori_loop(at,total,lambda t,_: (C.tick(t,0,n),0)[1],0)
    if not outs: out(0); out(1)
    for c in outs: c.wait()

def sum_and_scatter(a,grads,cid=10,ch=16,lags=(1,2,3,4),rr=96,every=2):
    rows=a.shape[0]; half=rows//2; D=pltpu.SemaphoreType.DMA; A=pl.BlockSpec(memory_space=pl.ANY)
    nw=len(grads); g3=[g.reshape(8,g.shape[0]//8,g.shape[1]) for g in grads]
    n=sum(g.shape[1]//rr for g in g3)
    o=pl.pallas_call(functools.partial(n_kernel,nw,half,ch,lags,rr,every),
        out_shape=[jax.ShapeDtypeStruct(a.shape,BF)]+[jax.ShapeDtypeStruct(g.shape[1:],g.dtype) for g in g3],
        in_specs=[A]*(nw+1),out_specs=[A]*(nw+1),
        scratch_shapes=scatter_scratch(n,[g.shape[2] for g in g3],rr)+chain_scratch(half,ch)+[D((2,)),D((2,))],
        compiler_params=pltpu.CompilerParams(collective_id=cid,has_side_effects=True,vmem_limit_bytes=63*2**20))(a,*g3)
    return o[0],o[1:]

def small_plane():
    return (lax.axis_size("dp"), lax.axis_size("zero")) == (4, 2)


def gather_rows(shards, cid):
    if small_plane():
        return all_gather(shards, cid=cid)
    return [lax.all_gather(s, ("dp", "zero"), axis=0, tiled=True) for s in shards]


def finish(part, grads):
    if small_plane():
        return sum_and_scatter(part, grads, every=3)
    total = all_reduce(part, cid=10)
    return total, [lax.psum_scatter(g, ("dp", "zero"), scatter_dimension=0, tiled=True) for g in grads]


def per_device(
    inputs,
    cotangent,
    segment,
    query_weight,
    key_weight,
    value_weight,
    out_weight,
    gate_weight,
    up_weight,
    down_weight,
    norm_gains,
    query_mean,
    key_mean,
    value_mean,
    out_mean,
    gate_mean,
    up_mean,
    down_mean,
    gains_mean,
    query_square,
    key_square,
    value_square,
    out_square,
    gate_square,
    up_square,
    down_square,
    gains_square,
):
    qkv_low = jnp.concatenate([query_weight, key_weight, value_weight], axis=1).astype(jnp.bfloat16)
    out_low = out_weight.T.astype(jnp.bfloat16)
    gate_low = gate_weight.astype(jnp.bfloat16)
    up_low = up_weight.astype(jnp.bfloat16)
    down_low = down_weight.T.astype(jnp.bfloat16)
    qkv_mat, out_mat = gather_rows([qkv_low, out_low], 2)
    mlp_shards = jnp.stack([gate_low, up_low, down_low])
    if not small_plane():
        mlp_shards = lax.all_gather(mlp_shards, ("dp", "zero"), axis=1, tiled=True)
    gains_full = lax.all_gather(norm_gains.astype(jnp.bfloat16), ("dp", "zero"), axis=1, tiled=True)
    heads_q = query_weight.shape[1]
    heads_k = key_weight.shape[1]
    gains_val = gains_full.astype(jnp.float32)
    token_rows = inputs.shape[0]
    cosine, sine = rope_tables(segment)
    resid_in = inputs.astype(jnp.float32)
    first_normed, unit_one, factor_one = rms_forward(resid_in, gains_val[0])
    attn_in = first_normed.astype(jnp.bfloat16)
    qkv = jnp.dot(attn_in, qkv_mat, preferred_element_type=jnp.float32)
    query_raw = qkv[:, :heads_q].reshape(token_rows, -1, HEAD_SIZE)
    key_raw = qkv[:, heads_q : heads_q + heads_k].reshape(token_rows, -1, HEAD_SIZE)
    value_low = qkv[:, heads_q + heads_k :].astype(jnp.bfloat16).reshape(token_rows, -1, HEAD_SIZE)
    rotated_queries = rotate(query_raw, cosine, sine).astype(jnp.bfloat16)
    rotated_keys = rotate(key_raw, cosine, sine).astype(jnp.bfloat16)
    attention_output, log_sums = attend_forward(rotated_queries, rotated_keys, value_low, segment)
    attn_part = lax.dot_general(attention_output, out_mat, (((1,), (1,)), ((), ())), preferred_element_type=jnp.float32)
    attn_total, mlp_total, normed_grad, mlp_in, hidden, gate_dlow, up_dlow, mlp_low = mlp_both(
        attn_part.astype(jnp.bfloat16), inputs, cotangent, gains_val, mlp_shards, small_plane()
    )
    attn_total = attn_total.astype(jnp.float32)
    mlp_total = mlp_total.astype(jnp.float32)
    normed_grad = normed_grad.astype(jnp.float32)
    post_attn, unit_two, factor_two = rms_forward(attn_total, gains_val[1])
    middle = resid_in + post_attn
    normed_two, unit_three, factor_three = rms_forward(middle, gains_val[2])
    post_mlp, unit_four, factor_four = rms_forward(mlp_total, gains_val[3])
    block_out = (middle + post_mlp).astype(jnp.bfloat16)
    gains_back = gains_full.astype(jnp.float32)
    out_grad = cotangent.astype(jnp.float32)
    mlp_grad, gain_four = rms_backward(out_grad, gains_back[3], unit_four, factor_four)
    down_grad = jnp.einsum("td,tf->df", mlp_low, hidden, preferred_element_type=jnp.float32)
    gate_grad = jnp.einsum("td,tf->df", mlp_in, gate_dlow, preferred_element_type=jnp.float32)
    up_grad = jnp.einsum("td,tf->df", mlp_in, up_dlow, preferred_element_type=jnp.float32)
    middle_part, gain_three = rms_backward(normed_grad, gains_back[2], unit_three, factor_three)
    middle_grad = out_grad + middle_part
    attn_grad, gain_two = rms_backward(middle_grad, gains_back[1], unit_two, factor_two)
    attn_low = attn_grad.astype(jnp.bfloat16)
    out_wgrad = jnp.einsum(
        "td,tc->dc", attn_low, attention_output, preferred_element_type=jnp.float32
    )
    attended_grad = (
        jnp.einsum("td,dc->tc", attn_low, out_mat, preferred_element_type=jnp.float32)
        .astype(jnp.bfloat16)
        .reshape(token_rows, -1, HEAD_SIZE)
    )
    query_rgrad, key_rgrad, value_rgrad = attend_backward(
        rotated_queries, rotated_keys, value_low, segment, log_sums, attended_grad
    )
    query_dlow = unrotate(query_rgrad, cosine, sine).astype(jnp.bfloat16).reshape(token_rows, -1)
    key_dlow = unrotate(key_rgrad, cosine, sine).astype(jnp.bfloat16).reshape(token_rows, -1)
    value_dlow = value_rgrad.astype(jnp.bfloat16).reshape(token_rows, -1)
    qkv_dlow = jnp.concatenate([query_dlow, key_dlow, value_dlow], axis=1)
    qkv_grad = jnp.einsum("td,tc->dc", attn_in, qkv_dlow, preferred_element_type=jnp.float32)
    first_part = lax.dot_general(qkv_dlow, qkv_mat, (((1,), (1,)), ((), ())), preferred_element_type=jnp.float32)
    low_grads = [g.astype(jnp.bfloat16) for g in (gate_grad, up_grad, down_grad, qkv_grad, out_wgrad)]
    first_grad, red = finish(first_part.astype(jnp.bfloat16), low_grads)
    first_grad = first_grad.astype(jnp.float32)
    input_part, gain_one = rms_backward(first_grad, gains_back[0], unit_one, factor_one)
    input_grad = middle_grad + input_part
    gains_grad = jnp.stack([gain_one, gain_two, gain_three, gain_four])
    gate_red, up_red, down_red, qkv_red, out_red = [g.astype(jnp.float32) for g in red]
    gains_red = lax.psum_scatter(
        gains_grad.astype(jnp.bfloat16), ("dp", "zero"), scatter_dimension=1, tiled=True
    ).astype(jnp.float32)
    reduced = (
        qkv_red[:, :heads_q],
        qkv_red[:, heads_q : heads_q + heads_k],
        qkv_red[:, heads_q + heads_k :],
        out_red.T,
        gate_red,
        up_red,
        down_red.T,
        gains_red,
    )
    masters = (
        query_weight,
        key_weight,
        value_weight,
        out_weight,
        gate_weight,
        up_weight,
        down_weight,
        norm_gains,
    )
    means = (query_mean, key_mean, value_mean, out_mean, gate_mean, up_mean, down_mean, gains_mean)
    squares = (
        query_square,
        key_square,
        value_square,
        out_square,
        gate_square,
        up_square,
        down_square,
        gains_square,
    )
    rates = (
        MODEL_WIDTH ** (-0.5),
        MODEL_WIDTH ** (-0.5),
        MODEL_WIDTH ** (-0.5),
        (QUERY_HEADS * HEAD_SIZE) ** (-0.5),
        MODEL_WIDTH ** (-0.5),
        MODEL_WIDTH ** (-0.5),
        FF ** (-0.5),
        gain_rate,
    )
    decays = (weight_decay,) * 7 + (0.0,)
    moments = []
    seconds = []
    updated = []
    for index in range(8):
        moment, second, master = adam_update(
            masters[index],
            means[index],
            squares[index],
            reduced[index],
            rates[index],
            decays[index],
        )
        moments.append(moment)
        seconds.append(second)
        updated.append(master)
    return (block_out, input_grad, *moments, *seconds, *updated)


def solution(mesh):
    in_specs = (
        P(("dp", "zero"), None),
        P(("dp", "zero"), None),
        P(("dp", "zero")),
        P(("dp", "zero"), "tensor"),
        P(("dp", "zero"), "tensor"),
        P(("dp", "zero"), "tensor"),
        P("tensor", ("dp", "zero")),
        P(("dp", "zero"), "tensor"),
        P(("dp", "zero"), "tensor"),
        P("tensor", ("dp", "zero")),
        P(None, ("dp", "zero")),
        P(("dp", "zero"), "tensor"),
        P(("dp", "zero"), "tensor"),
        P(("dp", "zero"), "tensor"),
        P("tensor", ("dp", "zero")),
        P(("dp", "zero"), "tensor"),
        P(("dp", "zero"), "tensor"),
        P("tensor", ("dp", "zero")),
        P(None, ("dp", "zero")),
        P(("dp", "zero"), "tensor"),
        P(("dp", "zero"), "tensor"),
        P(("dp", "zero"), "tensor"),
        P("tensor", ("dp", "zero")),
        P(("dp", "zero"), "tensor"),
        P(("dp", "zero"), "tensor"),
        P("tensor", ("dp", "zero")),
        P(None, ("dp", "zero")),
    )
    out_specs = (
        P(("dp", "zero"), None),
        P(("dp", "zero"), None),
        P(("dp", "zero"), "tensor"),
        P(("dp", "zero"), "tensor"),
        P(("dp", "zero"), "tensor"),
        P("tensor", ("dp", "zero")),
        P(("dp", "zero"), "tensor"),
        P(("dp", "zero"), "tensor"),
        P("tensor", ("dp", "zero")),
        P(None, ("dp", "zero")),
        P(("dp", "zero"), "tensor"),
        P(("dp", "zero"), "tensor"),
        P(("dp", "zero"), "tensor"),
        P("tensor", ("dp", "zero")),
        P(("dp", "zero"), "tensor"),
        P(("dp", "zero"), "tensor"),
        P("tensor", ("dp", "zero")),
        P(None, ("dp", "zero")),
        P(("dp", "zero"), "tensor"),
        P(("dp", "zero"), "tensor"),
        P(("dp", "zero"), "tensor"),
        P("tensor", ("dp", "zero")),
        P(("dp", "zero"), "tensor"),
        P(("dp", "zero"), "tensor"),
        P("tensor", ("dp", "zero")),
        P(None, ("dp", "zero")),
    )
    return jax.shard_map(
        per_device, mesh=mesh, in_specs=in_specs, out_specs=out_specs, check_vma=False
    )
```

```python
import functools

import jax
import jax.numpy as jnp
from jax import lax
from jax.experimental import pallas as pl
from jax.experimental.pallas import tpu as pltpu
from jax.sharding import PartitionSpec as P

MESH = pl.DeviceIdType.MESH

MODEL_WIDTH = 2304
QUERY_HEADS = 8
HEAD_SIZE = 256
FF = 9216
STEP = 10
W = MODEL_WIDTH


norm_eps = 1e-06
soft_cap = 50.0
rope_base = 10000.0
beta_one = 0.9
beta_two = 0.95
adam_eps = 1e-08
weight_decay = 0.1
gain_rate = 0.7


def rms_forward(value_rows, gain):
    factor = lax.rsqrt(jnp.mean(value_rows * value_rows, axis=-1, keepdims=True) + norm_eps)
    normed = value_rows * factor
    return (normed * gain, normed, factor)


def rms_backward(grad, gain, normed, factor):
    scaled = grad * gain
    inner = jnp.mean(scaled * normed, axis=-1, keepdims=True)
    return (factor * (scaled - normed * inner), jnp.sum(grad * normed, axis=0))


def rope_tables(segment):
    index = jnp.arange(segment.shape[0], dtype=jnp.int32)
    earlier = jnp.concatenate([jnp.full((1,), -1, jnp.int32), segment[:-1]])
    first = lax.cummax(jnp.where(segment != earlier, index, 0), axis=0)
    place = (index - first).astype(jnp.float32)
    inverse = rope_base ** (-jnp.arange(0, HEAD_SIZE, 2, dtype=jnp.float32) / HEAD_SIZE)
    angle = place[:, None] * inverse[None, :]
    return (jnp.cos(angle)[:, None, :], jnp.sin(angle)[:, None, :])


def unrotate(value_rows, cosine, sine):
    half = value_rows.shape[-1] // 2
    first = value_rows[..., :half]
    second = value_rows[..., half:]
    return jnp.concatenate(
        [first * cosine + second * sine, second * cosine - first * sine], axis=-1
    )


def score_block(query_blk, start, rotated_keys, segment):
    group_size = query_blk.shape[0]
    total = rotated_keys.shape[0]
    raw = jnp.einsum(
        "qhgd,khd->hgqk", query_blk, rotated_keys, preferred_element_type=jnp.float32
    ) * HEAD_SIZE ** (-0.5)
    bent = jnp.tanh(raw / soft_cap)
    rows_idx = start + jnp.arange(group_size, dtype=jnp.int32)
    cols_idx = jnp.arange(total, dtype=jnp.int32)
    visible = (cols_idx[None, :] <= rows_idx[:, None]) & (segment[:, None] == segment[None, :])
    return (jnp.where(visible, soft_cap * bent, -jnp.inf), bent)


def attend_backward(queries, keys, values, segment, dout):
    masked, bent = score_block(queries[:, None], 0, keys[:, None], segment)
    probs = jax.nn.softmax(masked, axis=-1)
    dprobs = jnp.einsum("qgd,kd->gqk", dout, values, preferred_element_type=jnp.float32)[None]
    inner = jnp.sum(probs * dprobs, axis=-1, keepdims=True)
    dscore = (probs * (dprobs - inner) * (1.0 - bent * bent)).astype(jnp.bfloat16)[0]
    low = probs.astype(jnp.bfloat16)[0]
    scale = HEAD_SIZE ** (-0.5)
    dq = jnp.einsum("gqk,kd->qgd", dscore, keys, preferred_element_type=jnp.float32) * scale
    dk = jnp.einsum("gqk,qgd->kd", dscore, queries, preferred_element_type=jnp.float32) * scale
    dv = jnp.einsum("gqk,qgd->kd", low, dout, preferred_element_type=jnp.float32)
    return dq, dk, dv


def adam_update(master, mean, square, grad, rate, decay):
    moment = beta_one * mean + (1.0 - beta_one) * grad
    second = beta_two * square + (1.0 - beta_two) * grad * grad
    direction = (
        moment / (1.0 - beta_one**STEP) / (jnp.sqrt(second / (1.0 - beta_two**STEP)) + adam_eps)
    )
    return (moment, second, master - rate * (direction + decay * master))


def remote(src,dst,ss,rs,dev):
    return pltpu.make_async_remote_copy(src_ref=src,dst_ref=dst,send_sem=ss,recv_sem=rs,device_id=dev,device_id_type=MESH)

class Chain:
    def __init__(self, half, ch, P, RE, RM, O, sp, so, ve, vm, vo, lags=(1,2,3,4)):
        self.p = lax.axis_index("tensor"); p=self.p
        self.reg=half//2; self.ch=ch; self.nt=self.reg//ch
        self.P,self.RE,self.RM,self.O=P,RE,RM,O
        self.sp,self.so,self.ve,self.vm,self.vo=sp,so,ve,vm,vo
        self.lags=lags
        self.end = (p==0)|(p==3)
        self.mid = (p==1)|(p==2)
        self.to_mid = {"tensor": jnp.where(p<2, 1, 2)}
        self.to_end = {"tensor": jnp.where(p<2, 0, 3)}
        self.to_oth = {"tensor": jnp.where(p<2, 2, 1)}
        self.own = jnp.where(p<2,0,1); self.oth=1-self.own
    def rows(self, part, t):
        return pl.ds(pl.multiple_of(part*self.reg+t*self.ch,16), self.ch)
    def trow(self,t): return pl.ds(pl.multiple_of(t*self.ch,16), self.ch)
    def r1(self,h,t):
        for part in (0,1):
            r=self.rows(part,t)
            remote(self.P.at[h,r],self.RE.at[h,r],self.sp.at[h,t,part],self.ve.at[h,t,part],self.to_mid).start()
    def r2(self,h,t):
        r=self.rows(self.oth,t)
        remote(self.P.at[h,r],self.RE.at[h,r],self.sp.at[h,t,0],self.ve.at[h,t,self.oth],self.to_end).wait_recv()
        self.P[h,r,:]=(self.P[h,r,:].astype(jnp.float32)+self.RE[h,r,:].astype(jnp.float32)).astype(jnp.bfloat16)
        remote(self.P.at[h,r],self.RM.at[h,self.trow(t)],self.sp.at[h,t,0],self.vm.at[h,t],self.to_oth).start()
    def r3(self,h,t):
        r=self.rows(self.own,t); q=self.trow(t)
        remote(self.P.at[h,r],self.RE.at[h,r],self.sp.at[h,t,0],self.ve.at[h,t,self.own],self.to_end).wait_recv()
        remote(self.P.at[h,r],self.RM.at[h,q],self.sp.at[h,t,0],self.vm.at[h,t],self.to_oth).wait_recv()
        self.O[h,r,:]=(self.P[h,r,:].astype(jnp.float32)+self.RE[h,r,:].astype(jnp.float32)+self.RM[h,q,:].astype(jnp.float32)).astype(jnp.bfloat16)
        remote(self.O.at[h,r],self.O.at[h,r],self.so.at[h,t,0],self.vo.at[h,t,self.own],self.to_end).start()
        remote(self.O.at[h,r],self.O.at[h,r],self.so.at[h,t,1],self.vo.at[h,t,self.own],self.to_oth).start()
    def b4(self,h,t):
        r=self.rows(self.oth,t)
        c=remote(self.O.at[h,r],self.O.at[h,r],self.so.at[h,t,2],self.vo.at[h,t,self.oth],self.to_end)
        c.wait_recv(); c.start()
    def b5_end(self,h,t):
        for part in (0,1):
            r=self.rows(part,t)
            remote(self.O.at[h,r],self.O.at[h,r],self.so.at[h,t,0],self.vo.at[h,t,part],self.to_mid).wait_recv()
            remote(self.P.at[h,r],self.RE.at[h,r],self.sp.at[h,t,part],self.ve.at[h,t,part],self.to_mid).wait_send()
    def b5_mid(self,h,t):
        r=self.rows(self.own,t)
        remote(self.P.at[h,r],self.RE.at[h,r],self.sp.at[h,t,0],self.ve.at[h,t,0],self.to_oth).wait_send()
        for i in range(3):
            remote(self.O.at[h,r],self.O.at[h,r],self.so.at[h,t,i],self.vo.at[h,t,0],self.to_end).wait_send()
    def tick(self, T, base0, hi0, start, base, hi):
        nt=self.nt
        def at(t0, cond, fns):
            late=t0>=start
            c=jnp.where(late,t0-base,t0-base0)
            ok=(t0>=0)&(c<jnp.where(late,hi,hi0))
            j=c//nt; h=j%2; t=c%nt
            @pl.when(ok&cond)
            def _():
                for f in fns: f(h,t)
        l1,l2,l3,l4=self.lags
        at(T,self.end,[self.r1])
        at(T-l1,self.mid,[self.r2])
        at(T-l2,self.mid,[self.r3])
        at(T-l3,self.mid,[self.b4])
        at(T-l4,self.end,[self.b5_end])
        at(T-l4,self.mid,[self.b5_mid])

def chain_scratch(half,ch):
    nt=half//2//ch
    B=jnp.bfloat16; D=pltpu.SemaphoreType.DMA
    return [pltpu.VMEM((2,half,W),B),pltpu.VMEM((2,half,W),B),pltpu.VMEM((2,half//2,W),B),pltpu.VMEM((2,half,W),B),
            D((2,nt,2)),D((2,nt,3)),D((2,nt,2)),D((2,nt)),D((2,nt,2))]

def line_barrier():
    te=lax.axis_index("tensor")
    bar=pltpu.get_barrier_semaphore()
    @pl.when(te<3)
    def _(): pl.semaphore_signal(bar, inc=1, device_id={"tensor":te+1}, device_id_type=MESH)
    @pl.when(te>0)
    def _(): pl.semaphore_signal(bar, inc=1, device_id={"tensor":te-1}, device_id_type=MESH)
    pl.semaphore_wait(bar, (te<3).astype(jnp.int32)+(te>0).astype(jnp.int32))

def ar_kernel(half,ch,lags,a_ref,o_ref,P,RE,RM,O,sp,so,ve,vm,vo,isem,osem):
    ins=[pltpu.make_async_copy(a_ref.at[pl.ds(h*half,half)],P.at[h],isem.at[h]) for h in (0,1)]
    for c in ins: c.start()
    line_barrier()
    for c in ins: c.wait()
    C=Chain(half,ch,P,RE,RM,O,sp,so,ve,vm,vo,lags)
    n=2*C.nt
    def body(T,_):
        C.tick(T,0,0,0,0,n); return 0
    lax.fori_loop(0,n+lags[-1],body,0)
    outs=[pltpu.make_async_copy(O.at[h],o_ref.at[pl.ds(h*half,half)],osem.at[h]) for h in (0,1)]
    for c in outs: c.start()
    for c in outs: c.wait()

def all_reduce(a,ch=16,lags=(2,3,4,5),cid=1):
    rows=a.shape[0]; half=rows//2
    return pl.pallas_call(functools.partial(ar_kernel,half,ch,lags),
        out_shape=jax.ShapeDtypeStruct(a.shape,a.dtype),
        in_specs=[pl.BlockSpec(memory_space=pl.ANY)],out_specs=pl.BlockSpec(memory_space=pl.ANY),
        scratch_shapes=chain_scratch(half,ch)+[pltpu.SemaphoreType.DMA((2,)),pltpu.SemaphoreType.DMA((2,))],
        compiler_params=pltpu.CompilerParams(collective_id=cid,has_side_effects=True,vmem_limit_bytes=60*2**20))(a)

def coords():
    dp,ze=lax.axis_index("dp"),lax.axis_index("zero")
    x=dp//2; c=dp%2
    return x,c,ze
def sid(x,c,y): return (x*2+c)*2+y
class Plane:
    def __init__(self):
        x,c,y=coords()
        self.x,self.c,self.y=x,c,y
        self.toX={"dp":(1-x)*2+c}; self.toY={"zero":1-y}; self.toC={"dp":x*2+1-c}
        self.lane=[sid(x,c,y),sid(1-x,c,y),sid(x,c,1-y),sid(1-x,c,1-y)]
        d=1-c
        self.other=[sid(x,d,y),sid(1-x,d,y),sid(x,d,1-y),sid(1-x,d,1-y)]
        self.is0=c==0; self.is1=c==1
def plane_signal():
    x,c,y=coords()
    bar=pltpu.get_barrier_semaphore()
    for dev in ({"dp":(1-x)*2+c},{"zero":1-y},{"dp":x*2+1-c}):
        pl.semaphore_signal(bar, inc=1, device_id=dev, device_id_type=MESH)
def plane_barrier():
    plane_signal(); pl.semaphore_wait(pltpu.get_barrier_semaphore(),3)

class Gather:
    def __init__(self, units, ss, rs, ls):
        self.u=units; self.ss,self.rs,self.ls=ss,rs,ls; self.pl=Plane()
    def refs(self,i):
        S,F,r0,rr=self.u[i]; r=pl.ds(r0,rr)
        return S.at[r], (lambda s: F.at[s,r])
    def a(self,i):
        S,F=self.refs(i); q=self.pl; own=q.lane[0]
        remote(S,F(own),self.ss.at[i,0],self.rs.at[i,0],q.toX).start()
        remote(S,F(own),self.ss.at[i,1],self.rs.at[i,1],q.toY).start()
        remote(S,F(own),self.ss.at[i,2],self.rs.at[i,3],q.toC).start()
        pltpu.make_async_copy(S,F(own),self.ls.at[i]).start()
    def b(self,i):
        S,F=self.refs(i); q=self.pl; X,Y=q.lane[1],q.lane[2]
        remote(S,F(X),self.ss.at[i,0],self.rs.at[i,0],q.toX).wait_recv()
        @pl.when(q.is1)
        def _(): remote(F(X),F(X),self.ss.at[i,3],self.rs.at[i,2],q.toY).start()
        remote(F(X),F(X),self.ss.at[i,4],self.rs.at[i,4],q.toC).start()
        remote(S,F(Y),self.ss.at[i,1],self.rs.at[i,1],q.toY).wait_recv()
        @pl.when(q.is0)
        def _(): remote(F(Y),F(Y),self.ss.at[i,3],self.rs.at[i,2],q.toX).start()
        remote(F(Y),F(Y),self.ss.at[i,5],self.rs.at[i,5],q.toC).start()
    def d(self,i):
        S,F=self.refs(i); q=self.pl; D=q.lane[3]
        c=remote(F(D),F(D),self.ss.at[i,6],self.rs.at[i,6],q.toC)
        remote(S,F(D),self.ss.at[i,3],self.rs.at[i,2],q.toX).wait_recv()
        c.start()
    def e(self,i):
        S,F=self.refs(i); q=self.pl
        for j in range(4):
            remote(S,F(q.other[j]),self.ss.at[i,0],self.rs.at[i,3+j],q.toC).wait_recv()
        pltpu.make_async_copy(S,F(q.lane[0]),self.ls.at[i]).wait()
        for j in range(7):
            remote(S,S,self.ss.at[i,j],self.rs.at[i,0],q.toC).wait_send()
    def tick(self,T):
        n=len(self.u)
        if 0<=T<n: self.a(T)
        if 0<=T-1<n: self.b(T-1)
        if 0<=T-2<n: self.d(T-2)
        if 0<=T-3<n: self.e(T-3)
    @property
    def ticks(self): return len(self.u)+3
def gather_sems(n):
    D=pltpu.SemaphoreType.DMA
    return [D((n,7)),D((n,7)),D((n,))]

class Scatter:
    def __init__(self,units,LB,OB,depth,ss,rs,ls):
        self.u=units; self.LB,self.OB,self.depth=LB,OB,depth; self.ss,self.rs,self.ls=ss,rs,ls; self.pl=Plane()
    def get(self,i):
        G,O,CB,DB,XB,YB,r0,rr,C=self.u[i]; r=pl.ds(r0,rr); s=i%self.depth
        g=lambda k: G.at[k,r]
        lb=lambda j: self.LB.at[s,j,pl.ds(0,rr),pl.ds(0,C)]
        return g,lb,O.at[r],CB,DB,XB,YB,r,s,rr,C
    def p1(self,i):
        g,lb,O,CB,DB,XB,YB,r,s,rr,C=self.get(i); q=self.pl
        for j in (3,1,2,0):
            remote(g(q.other[j]),CB.at[j,r],self.ss.at[i,j],self.rs.at[i,j],q.toC).start()
            pltpu.make_async_copy(g(q.lane[j]),lb(j),self.ls.at[i,j]).start()
    def p2(self,i):
        g,lb,O,CB,DB,XB,YB,r,s,rr,C=self.get(i); q=self.pl
        for j in (3,1,2,0):
            pltpu.make_async_copy(g(q.lane[j]),lb(j),self.ls.at[i,j]).wait()
            remote(g(q.other[j]),CB.at[j,r],self.ss.at[i,j],self.rs.at[i,j],q.toC).wait_recv()
            v=self.LB[s,j,pl.ds(0,rr),pl.ds(0,C)].astype(jnp.float32)+CB[j,r].astype(jnp.float32)
            self.LB[s,j,pl.ds(0,rr),pl.ds(0,C)]=v.astype(jnp.bfloat16)
            if j==3:
                @pl.when(q.is0)
                def _(): remote(lb(3),DB.at[r],self.ss.at[i,4],self.rs.at[i,4],q.toX).start()
                @pl.when(q.is1)
                def _(): remote(lb(3),DB.at[r],self.ss.at[i,4],self.rs.at[i,4],q.toY).start()
            if j==1:
                @pl.when(q.is0)
                def _(): remote(lb(1),XB.at[r],self.ss.at[i,5],self.rs.at[i,5],q.toX).start()
            if j==2:
                @pl.when(q.is1)
                def _(): remote(lb(2),YB.at[r],self.ss.at[i,5],self.rs.at[i,6],q.toY).start()
    def p3(self,i):
        g,lb,O,CB,DB,XB,YB,r,s,rr,C=self.get(i); q=self.pl
        remote(lb(3),DB.at[r],self.ss.at[i,4],self.rs.at[i,4],q.toX).wait_recv()
        def relay(j,buf,sem,dev):
            v=self.LB[s,j,pl.ds(0,rr),pl.ds(0,C)].astype(jnp.float32)+DB[r].astype(jnp.float32)
            self.LB[s,j,pl.ds(0,rr),pl.ds(0,C)]=v.astype(jnp.bfloat16)
            remote(lb(j),buf.at[r],self.ss.at[i,6],self.rs.at[i,sem],dev).start()
        @pl.when(q.is0)
        def _(): relay(2,YB,6,q.toY)
        @pl.when(q.is1)
        def _(): relay(1,XB,5,q.toX)
    def p4(self,i):
        g,lb,O,CB,DB,XB,YB,r,s,rr,C=self.get(i); q=self.pl
        remote(lb(0),XB.at[r],self.ss.at[i,5],self.rs.at[i,5],q.toX).wait_recv()
        remote(lb(0),YB.at[r],self.ss.at[i,5],self.rs.at[i,6],q.toY).wait_recv()
        v=self.LB[s,0,pl.ds(0,rr),pl.ds(0,C)].astype(jnp.float32)+XB[r].astype(jnp.float32)+YB[r].astype(jnp.float32)
        ob=i%2
        self.OB[ob,pl.ds(0,rr),pl.ds(0,C)]=v.astype(self.OB.dtype)
        pltpu.make_async_copy(self.OB.at[ob,pl.ds(0,rr),pl.ds(0,C)],O,self.ls.at[i,4]).start()
        for j in range(7):
            remote(lb(0),XB.at[r],self.ss.at[i,j],self.rs.at[i,0],q.toX).wait_send()
    def p5(self,i):
        g,lb,O,CB,DB,XB,YB,r,s,rr,C=self.get(i)
        pltpu.make_async_copy(self.OB.at[i%2,pl.ds(0,rr),pl.ds(0,C)],O,self.ls.at[i,4]).wait()
    def tick(self,T):
        n=len(self.u)
        if 0<=T<n: self.p1(T)
        if 0<=T-1<n: self.p2(T-1)
        if 0<=T-2<n: self.p3(T-2)
        if 0<=T-4<n: self.p5(T-4)
        if 0<=T-3<n: self.p4(T-3)
    @property
    def ticks(self): return len(self.u)+4
def scatter_scratch(n,cols,rr,depth=4,rows=288):
    D=pltpu.SemaphoreType.DMA; B=jnp.bfloat16
    land=[]
    for C in cols: land+= [pltpu.VMEM((4,rows,C),B)]+[pltpu.VMEM((rows,C),B)]*3
    m=max(cols)
    return land+[pltpu.VMEM((depth,4,rr,m),B),pltpu.VMEM((2,rr,m),B),D((n,7)),D((n,7)),D((n,5))]
F32=jnp.float32; BF=jnp.bfloat16
class GatherD(Gather):
    def __init__(self,src,dst,n,lags,ss,rs,ls,base=0):
        self.src,self.dst,self.n,self.lags,self.base=src,dst,n,lags,base
        self.ss,self.rs,self.ls=ss,rs,ls; self.pl=Plane()
    def refs(self,i):
        i=i-self.base
        return self.src(i),(lambda s: self.dst(i,s))
    def tick(self,T):
        lb,ld,le=self.lags
        for lag,f in ((0,self.a),(lb,self.b),(ld,self.d),(le,self.e)):
            i=T-lag
            @pl.when((i>=0)&(i<self.n))
            def _(): f(i+self.base)
def gelu_parts(g):
    k=0.7978845608028654; c=0.044715
    t=jnp.tanh(k*(g+c*g*g*g))
    act=0.5*g*(1.0+t)
    der=0.5*(1.0+t)+0.5*g*(1.0-t*t)*k*(1.0+3.0*c*g*g)
    return act,der
def nt_dot(a,b): return lax.dot_general(a,b,(((1,),(1,)),((),())),preferred_element_type=F32)
def rsq(v): return lax.rsqrt(jnp.mean(v*v,axis=-1,keepdims=True)+1e-6)

def f_kernel(gather,half,ch,lags,grr,qrr,glags,tn,nheads,*refs):
    (x_ref,dy_ref,cos,sin,segc,segr,wq_ref,ga_ref,s_ref,
     at_out,f_out,d_out,n2_out,hid_out,dg_out,du_out,df_out,n1_out,q_out,k_out,v_out,o_out,w_out,g_out,gg_out,gu_out,gd_out,
     Wt,BIG,XS,GV,P,RE,RM,O,sp,so,ve,vm,vo,gss,grs,gls,isem,osem)=refs
    C=Chain(half,ch,P,RE,RM,O,sp,so,ve,vm,vo,lags)
    L=lags[-1]; nt=C.nt; ff=Wt.shape[2]; nj=ff//tn; nd=W//tn; total=2*half; HS=256
    qw=nheads*HS; wq=qw+2*HS+qw
    def rows(h): return pl.ds(h*half,half)
    def cp(src,dst,sem): return pltpu.make_async_copy(src,dst,sem)
    n2r=pl.ds(4*half,half); hidr=pl.ds(5*half,half)
    N2=BIG.at[n2r]; HID=BIG.at[hidr]
    def gu(k,h): return pl.ds((k*2+h)*half,half)
    WQ=BIG.at[pl.ds(0,W),pl.ds(0,wq)]
    GA=BIG.at[pl.ds(0,W),pl.ds(wq,128)]
    c0,c1=wq+128,wq+128+HS
    def qpart(hd): return (pl.ds(hd*total,total),pl.ds(c0,HS))
    kpart=(pl.ds(0,total),pl.ds(c1,HS)); vpart=(pl.ds(total,total),pl.ds(c1,HS))
    def opart(h): return (pl.ds(2*total+h*half,half),pl.ds(c0,qw))
    xin=lambda ref,h: cp(ref.at[rows(h)],XS,isem.at[0])
    xin(x_ref,0).start()
    line_signal()
    oc={}
    def out(name,src,dst,i):
        c=cp(src,dst,osem.at[i]); c.start(); oc[name]=c
    def fin(name): oc.pop(name).wait()
    shard=W//8 if gather else 0
    nq=0; st={'q':0,'g':0}
    if gather:
        plane_signal()
        pl.semaphore_wait(pltpu.get_barrier_semaphore(),line_count()+3)
        def al(v): return pl.ds(pl.multiple_of(v,16),qrr)
        per=shard//grr; nq=shard//qrr; ng=s_ref.shape[0]*per
        Gg=GatherD(lambda i: ga_ref,lambda i,s: BIG.at[pl.ds(pl.multiple_of(s*shard,16),shard),pl.ds(wq,128)],1,(0,0,0),gss,grs,gls)
        Gq=GatherD(lambda i: wq_ref.at[al(i*qrr)],lambda i,s: BIG.at[al(s*shard+i*qrr),pl.ds(0,wq)],nq,(1,2,3),gss,grs,gls,1)
        Gt=GatherD(lambda i: s_ref.at[i//per,pl.ds(pl.multiple_of((i%per)*grr,16),grr)],
                   lambda i,s: Wt.at[i//per,pl.ds(pl.multiple_of(s*shard+(i%per)*grr,16),grr)],ng,glags,gss,grs,gls,1+nq)
        def done(k): return (k+1)*per-1+glags[2]+1
        Gg.a(0); Gq.tick(0); Gg.b(0); Gg.d(0); Gq.tick(1); Gg.e(0); st['q']=2
    else:
        pl.semaphore_wait(pltpu.get_barrier_semaphore(),line_count())
        wc=[cp(s_ref.at[k],Wt.at[k],gls.at[k]) for k in range(3)]+[cp(wq_ref,WQ,gls.at[3]),cp(ga_ref,GA,gls.at[4])]
        for c in wc: c.start()
        for c in wc: c.wait()
        def done(k): return 0
    def qg(upto):
        if gather:
            while st['q']<upto: Gq.tick(st['q']); st['q']+=1
    def ag(upto):
        if gather and upto>st['g']:
            lax.fori_loop(st['g'],upto,lambda T,_: (Gt.tick(T),0)[1],0); st['g']=upto
    S={'T':0,'base0':0,'hi0':0,'start':0,'base':0,'hi':0}
    def tick(T,s): C.tick(T,s['base0'],s['hi0'],s['start'],s['base'],s['hi'])
    def top(): return S['base']+S['hi']+L
    def ticks(until,every_g=0):
        s=dict(S); T0,g0=s['T'],st['g']; until=min(until,top())
        if until<=T0: return
        def body(T,_):
            tick(T,s)
            if every_g and gather:
                @pl.when((T-T0)%every_g==0)
                def _(): Gt.tick(g0+(T-T0)//every_g)
            return 0
        lax.fori_loop(T0,until,body,0)
        S['T']=until
        if every_g and gather: st['g']=g0+(until-T0+every_g-1)//every_g
    def finish(c,every_g=0):
        base=S['base'] if c>S['hi0'] else S['base0']
        ticks(base+c+L,every_g)
    def ready(c):
        if S['T']>S['base']+S['hi']:
            ticks(S['start']+L)
            S.update(base0=S['base'],hi0=S['hi'],start=S['T'],base=S['T']-S['hi'])
        S['hi']=c
    def units(n,fn,every=0,eg=0):
        s=dict(S); T0,g0=s['T'],st['g']
        def body(i,_):
            fn(i)
            if every:
                @pl.when((i+1)%every==0)
                def _(): tick(T0+i//every,s)
            if eg and gather:
                @pl.when((i+1)%eg==0)
                def _(): Gt.tick(g0+i//eg)
            return 0
        lax.fori_loop(0,n,body,0)
        if eg and gather: st['g']=g0+n//eg
        if every: S['T']=min(T0+n//every,max(top(),T0))
    def wait_w(k):
        while gather and st['g']<done(k):
            ag(st['g']+1); ticks(S['T']+2)
    nr=32; nn=half//nr
    def rch(i): return pl.ds(pl.multiple_of(i*nr,nr),nr)
    def gain(k): return GV[k:k+1,:]
    def norm0(h):
        def f(i):
            r=rch(i)
            v=XS[r,:].astype(F32)
            P[h,r,:]=(v*rsq(v)*gain(0)).astype(BF)
        return f
    def norm1(h):
        def f(i):
            r=rch(i)
            a=O[h,r,:].astype(F32)
            h1=XS[r,:].astype(F32)+a*rsq(a)*gain(1)
            BIG[pl.ds(pl.multiple_of(4*half+i*nr,nr),nr),:]=(h1*rsq(h1)*gain(2)).astype(BF)
        return f
    def normf(h):
        def f(i):
            r=rch(i)
            v=O[h,r,:].astype(F32); q=rsq(v); z=v*q
            s=XS[r,:].astype(F32)*gain(3)
            BIG[pl.ds(pl.multiple_of(4*half+i*nr,nr),nr),:]=(q*(s-z*jnp.mean(s*z,axis=-1,keepdims=True))).astype(BF)
        return f
    def qkv(h):
        def f(j):
            t=jnp.dot(P[h],BIG[pl.ds(0,W),pl.ds(pl.multiple_of(j*HS,HS),HS)],preferred_element_type=F32)
            return t
        cs=cos[rows(h),:]; sn=sin[rows(h),:]
        def rot(t):
            a,b=t[:,:HS//2],t[:,HS//2:]
            return jnp.concatenate([a*cs-b*sn,b*cs+a*sn],axis=1).astype(BF)
        for hd in range(nheads): BIG[pl.ds(hd*total+h*half,half),pl.ds(c0,HS)]=rot(f(hd))
        BIG[pl.ds(h*half,half),pl.ds(c1,HS)]=rot(f(nheads))
        BIG[pl.ds(total+h*half,half),pl.ds(c1,HS)]=f(nheads+1).astype(BF)
    qb=half//2
    def attend(h):
        def f(i):
            hd=i%nheads; r0=h*half+(i//nheads)*qb
            rr=pl.ds(pl.multiple_of(r0,16),qb)
            q=BIG[pl.ds(pl.multiple_of(hd*total+r0,16),qb),pl.ds(c0,HS)]
            s=nt_dot(q,BIG[kpart])*(HS**-0.5)
            cc=50.0*jnp.tanh(s*(1.0/50.0))
            ri=r0+lax.broadcasted_iota(jnp.int32,(qb,total),0); ci=lax.broadcasted_iota(jnp.int32,(qb,total),1)
            vis=(ci<=ri)&(segc[rr,:]==segr[...])
            cc=jnp.where(vis,cc,-jnp.inf)
            e=jnp.exp(cc-jnp.max(cc,axis=-1,keepdims=True))
            p=(e/jnp.sum(e,axis=-1,keepdims=True)).astype(BF)
            o=jnp.dot(p,BIG[vpart],preferred_element_type=F32).astype(BF)
            BIG[pl.ds(pl.multiple_of(2*total+r0,16),qb),pl.ds(pl.multiple_of(c0+hd*HS,128),HS)]=o
        return f
    def col(j): return pl.ds(pl.multiple_of(j*tn,tn),tn)
    def outp(h):
        def f(j): P[h,:,col(j)]=nt_dot(BIG[opart(h)],BIG[col(j),pl.ds(qw+2*HS,qw)]).astype(BF)
        return f
    def gate(h):
        def f(j): BIG[gu(0,h),col(j)]=jnp.dot(N2[...],Wt[0,:,col(j)],preferred_element_type=F32).astype(BF)
        return f
    def up(h):
        def f(j):
            u=jnp.dot(N2[...],Wt[1,:,col(j)],preferred_element_type=F32)
            g=BIG[gu(0,h),col(j)].astype(F32)
            act,_=gelu_parts(g)
            BIG[gu(1,h),col(j)]=u.astype(BF)
            BIG[hidr,col(j)]=(act*u).astype(BF)
        return f
    def down(h):
        def f(j): P[h,:,col(j)]=nt_dot(HID[...],Wt[2,col(j),:]).astype(BF)
        return f
    def bwd1(h):
        def f(j):
            d=jnp.dot(N2[...],Wt[2,:,col(j)],preferred_element_type=F32)
            g=BIG[gu(0,h),col(j)].astype(F32); u=BIG[gu(1,h),col(j)].astype(F32)
            act,der=gelu_parts(g)
            BIG[gu(0,h),col(j)]=(d*u*der).astype(BF)
            BIG[gu(1,h),col(j)]=(d*act).astype(BF)
        return f
    def bwd2(h):
        def f(j):
            P[h,:,col(j)]=(nt_dot(BIG[gu(0,h),:],Wt[0,col(j),:])+nt_dot(BIG[gu(1,h),:],Wt[1,col(j),:])).astype(BF)
        return f
    GV[...]=jnp.transpose(GA[...].astype(F32))[:8,:]
    xin(x_ref,0).wait()
    units(nn,norm0(0))
    xin(x_ref,1).start()
    out('g',GV,g_out,7)
    out('n1a',P.at[0],n1_out.at[rows(0)],4)
    qg(nq)
    ag(1)
    xin(x_ref,1).wait()
    units(nn,norm0(1))
    xin(x_ref,0).start()
    out('n1b',P.at[1],n1_out.at[rows(1)],5)
    qg(nq+3)
    ag(2)
    out('w',WQ,w_out,6)
    qkv(0)
    ag(3)
    qkv(1)
    out('q0',BIG.at[qpart(0)],q_out.at[0],0)
    if nheads>1: out('q1',BIG.at[qpart(1)],q_out.at[1],1)
    out('k',BIG.at[kpart],k_out,2)
    out('v',BIG.at[vpart],v_out,3)
    ag(4)
    fin('n1a'); fin('n1b')
    units(2*nheads,attend(0),eg=4)
    units(nd,outp(0))
    ready(nt)
    units(2*nheads,attend(1),1,eg=4)
    units(nd,outp(1),3)
    ready(2*nt)
    out('o0',BIG.at[opart(0)],o_out.at[rows(0)],8)
    out('o1',BIG.at[opart(1)],o_out.at[rows(1)],9)
    finish(nt,2)
    out('at0',O.at[0],at_out.at[rows(0)],10)
    xin(x_ref,0).wait()
    for k in ('q0','q1','k','v','o0','o1','w','g'):
        if k in oc: fin(k)
    units(nn,norm1(0),7)
    xin(x_ref,1).start()
    out('n2',N2,n2_out.at[rows(0)],0)
    wait_w(0)
    units(nj,gate(0),3)
    wait_w(1)
    units(nj,up(0),4)
    out('hid',HID,hid_out.at[rows(0)],1)
    wait_w(2)
    fin('at0')
    units(nd,down(0),3)
    ready(3*nt)
    finish(2*nt)
    out('at1',O.at[1],at_out.at[rows(1)],11)
    xin(x_ref,1).wait()
    fin('n2')
    units(nn,norm1(1),7)
    xin(dy_ref,0).start()
    out('n2',N2,n2_out.at[rows(1)],0)
    units(nj,gate(1),3)
    fin('hid')
    units(nj,up(1),4)
    out('hid',HID,hid_out.at[rows(1)],1)
    fin('at1')
    units(nd,down(1),3)
    ready(4*nt)
    finish(3*nt)
    out('f0',O.at[0],f_out.at[rows(0)],10)
    xin(dy_ref,0).wait()
    fin('n2')
    units(nn,normf(0),7)
    xin(dy_ref,1).start()
    out('df',N2,df_out.at[rows(0)],0)
    units(nj,bwd1(0),3)
    out('dg0',BIG.at[gu(0,0)],dg_out.at[rows(0)],2); out('du0',BIG.at[gu(1,0)],du_out.at[rows(0)],3)
    fin('f0')
    units(nd,bwd2(0),2)
    ready(5*nt)
    finish(4*nt)
    out('f1',O.at[1],f_out.at[rows(1)],11)
    xin(dy_ref,1).wait()
    fin('df')
    units(nn,normf(1),7)
    out('df',N2,df_out.at[rows(1)],0)
    units(nj,bwd1(1),3)
    out('dg1',BIG.at[gu(0,1)],dg_out.at[rows(1)],4); out('du1',BIG.at[gu(1,1)],du_out.at[rows(1)],5)
    fin('f1'); fin('df'); fin('hid')
    n2f=pl.ds(2*total,total); dff=pl.ds(0,total); hidf=pl.ds(total,total)
    back=[cp(n2_out,BIG.at[n2f],isem.at[1]),cp(df_out,Wt.at[2,dff],isem.at[2]),cp(hid_out,Wt.at[2,hidf],isem.at[3])]
    for c in back: c.start()
    units(nd,bwd2(1),2)
    ready(6*nt)
    for c in back: c.wait()
    def wgrad(lhs,rhs,k):
        def f(j):
            lt=lhs(col(j))
            for n in range(0,ff,768):
                t=lax.dot_general(lt,rhs(pl.ds(n,768)),(((0,),(0,)),((),())),preferred_element_type=F32)
                Wt[k,col(j),pl.ds(n,768)]=t.astype(BF)
        return f
    units(nd,wgrad(lambda c: Wt[2,dff,c],lambda c: Wt[2,hidf,c],0),1)
    out('gd',Wt.at[0],gd_out,6)
    units(nd,wgrad(lambda c: BIG[n2f,c],lambda c: BIG[pl.ds(0,total),c],1),1)
    out('gg',Wt.at[1],gg_out,7)
    finish(5*nt)
    out('d0',O.at[0],d_out.at[rows(0)],10)
    units(nd,wgrad(lambda c: BIG[n2f,c],lambda c: BIG[pl.ds(total,total),c],2),1)
    out('gu',Wt.at[2],gu_out,8)
    finish(6*nt)
    out('d1',O.at[1],d_out.at[rows(1)],11)
    for k in list(oc): fin(k)

def line_signal():
    te=lax.axis_index("tensor")
    bar=pltpu.get_barrier_semaphore()
    @pl.when(te<3)
    def _(): pl.semaphore_signal(bar, inc=1, device_id={"tensor":te+1}, device_id_type=MESH)
    @pl.when(te>0)
    def _(): pl.semaphore_signal(bar, inc=1, device_id={"tensor":te-1}, device_id_type=MESH)
def line_count():
    te=lax.axis_index("tensor")
    return (te<3).astype(jnp.int32)+(te>0).astype(jnp.int32)

def forward_both(x,dy,cos,sin,seg,qkvo,gains,shards,nheads,gather,cid=9,ch=16,lags=(2,3,4,5),grr=48,qrr=48,glags=(3,4,6),tn=256):
    total=x.shape[0]; half=total//2; D=pltpu.SemaphoreType.DMA; ff=shards.shape[2]; w3=qkvo.shape[1]
    ng=(1+qkvo.shape[0]//qrr+shards.shape[0]*shards.shape[1]//grr) if gather else 5
    sds=jax.ShapeDtypeStruct
    act=sds((total,W),BF); wide=sds((total,ff),BF); hd=sds((total,256),BF)
    A=pl.BlockSpec(memory_space=pl.ANY); V=pl.BlockSpec(memory_space=pltpu.VMEM)
    return pl.pallas_call(functools.partial(f_kernel,gather,half,ch,lags,grr,qrr,glags,tn,nheads),
        out_shape=[act,act,act,act,wide,wide,wide,act,act,sds((nheads,total,256),BF),hd,hd,sds((total,nheads*256),BF),sds((W,w3),BF),sds((8,W),F32)]+[sds((W,ff),BF)]*3,
        in_specs=[A,A,V,V,V,V,A,A,A],out_specs=[A]*18,
        scratch_shapes=[pltpu.VMEM((3,W,ff),BF),pltpu.VMEM((6*half,W),BF),pltpu.VMEM((half,W),BF),pltpu.VMEM((8,W),F32)]
            +chain_scratch(half,ch)+gather_sems(ng)+[D((4,)),D((12,))],
        compiler_params=pltpu.CompilerParams(collective_id=cid,has_side_effects=True,vmem_limit_bytes=64*2**20))(
            x,dy,cos,sin,seg.reshape(-1,1),seg.reshape(1,-1),qkvo,gains,shards)
def n_kernel(nw,half,ch,lags,rr,every,*refs):
    a_ref=refs[0]; G=refs[1:1+nw]; o_ref=refs[1+nw]; Og=refs[2+nw:2+2*nw]
    r=refs[2+2*nw:]
    land=r[:4*nw]; LB,OB,ss,rs,ls=r[4*nw:4*nw+5]
    P,RE,RM,O,sp,so,ve,vm,vo,isem,osem=r[4*nw+5:]
    ins=[pltpu.make_async_copy(a_ref.at[pl.ds(h*half,half)],P.at[h],isem.at[h]) for h in (0,1)]
    for c in ins: c.start()
    line_signal(); plane_signal()
    pl.semaphore_wait(pltpu.get_barrier_semaphore(),line_count()+3)
    for c in ins: c.wait()
    C=Chain(half,ch,P,RE,RM,O,sp,so,ve,vm,vo,lags)
    units=[(G[k],Og[k],*land[4*k:4*k+4],r0,rr,G[k].shape[2]) for k in range(nw) for r0 in range(0,G[k].shape[1],rr)]
    S=Scatter(units,LB,OB,LB.shape[0],ss,rs,ls)
    n=2*C.nt; total=n+lags[-1]; outs=[]
    def out(h):
        c=pltpu.make_async_copy(O.at[h],o_ref.at[pl.ds(h*half,half)],osem.at[h]); c.start(); outs.append(c)
    at=0
    for T in range(S.ticks):
        S.tick(T)
        to=min(total,at+every)
        lax.fori_loop(at,to,lambda t,_: (C.tick(t,0,0,0,0,n),0)[1],0); at=to
        if at==total and not outs: out(0); out(1)
    lax.fori_loop(at,total,lambda t,_: (C.tick(t,0,0,0,0,n),0)[1],0)
    if not outs: out(0); out(1)
    for c in outs: c.wait()

def sum_and_scatter(a,grads,cid=10,ch=16,lags=(2,3,4,5),rr=96,every=2):
    rows=a.shape[0]; half=rows//2; D=pltpu.SemaphoreType.DMA; A=pl.BlockSpec(memory_space=pl.ANY)
    nw=len(grads); g3=[g.reshape(8,g.shape[0]//8,g.shape[1]) for g in grads]
    n=sum(g.shape[1]//rr for g in g3)
    o=pl.pallas_call(functools.partial(n_kernel,nw,half,ch,lags,rr,every),
        out_shape=[jax.ShapeDtypeStruct(a.shape,BF)]+[jax.ShapeDtypeStruct(g.shape[1:],g.dtype) for g in g3],
        in_specs=[A]*(nw+1),out_specs=[A]*(nw+1),
        scratch_shapes=scatter_scratch(n,[g.shape[2] for g in g3],rr)+chain_scratch(half,ch)+[D((2,)),D((2,))],
        compiler_params=pltpu.CompilerParams(collective_id=cid,has_side_effects=True,vmem_limit_bytes=63*2**20))(a,*g3)
    return o[0],o[1:]

def small_plane():
    return (lax.axis_size("dp"), lax.axis_size("zero")) == (4, 2)


def finish(part, grads):
    if small_plane():
        return sum_and_scatter(part, grads, every=3)
    total = all_reduce(part, cid=10)
    return total, [lax.psum_scatter(g, ("dp", "zero"), scatter_dimension=0, tiled=True) for g in grads]


def per_device(
    inputs,
    cotangent,
    segment,
    query_weight,
    key_weight,
    value_weight,
    out_weight,
    gate_weight,
    up_weight,
    down_weight,
    norm_gains,
    query_mean,
    key_mean,
    value_mean,
    out_mean,
    gate_mean,
    up_mean,
    down_mean,
    gains_mean,
    query_square,
    key_square,
    value_square,
    out_square,
    gate_square,
    up_square,
    down_square,
    gains_square,
):
    qkvo_low = jnp.concatenate(
        [query_weight, key_weight, value_weight, out_weight.T], axis=1
    ).astype(jnp.bfloat16)
    mlp_shards = jnp.stack([gate_weight, up_weight, down_weight.T]).astype(jnp.bfloat16)
    gains_low = jnp.pad(norm_gains.T.astype(jnp.bfloat16), ((0, 0), (0, 124)))
    if not small_plane():
        both = ("dp", "zero")
        qkvo_low = lax.all_gather(qkvo_low, both, axis=0, tiled=True)
        gains_low = lax.all_gather(gains_low, both, axis=0, tiled=True)
        mlp_shards = lax.all_gather(mlp_shards, both, axis=1, tiled=True)
    heads_q = query_weight.shape[1]
    heads_k = key_weight.shape[1]
    wide = heads_q + 2 * heads_k
    token_rows = inputs.shape[0]
    cosine, sine = rope_tables(segment)
    (
        attn_total,
        mlp_total,
        normed_grad,
        mlp_in,
        hidden,
        gate_dlow,
        up_dlow,
        mlp_low,
        attn_in,
        rotated_queries,
        rotated_keys,
        value_low,
        attention_output,
        qkvo_mat,
        gains_val,
        gate_grad,
        up_grad,
        down_grad,
    ) = forward_both(
        inputs,
        cotangent,
        cosine[:, 0],
        sine[:, 0],
        segment,
        qkvo_low,
        gains_low,
        mlp_shards,
        heads_q // HEAD_SIZE,
        small_plane(),
    )
    gains_back = gains_val
    out_mat = qkvo_mat[:, wide:]
    resid_in = inputs.astype(jnp.float32)
    unused, unit_one, factor_one = rms_forward(resid_in, gains_val[0])
    attn_total = attn_total.astype(jnp.float32)
    mlp_total = mlp_total.astype(jnp.float32)
    normed_grad = normed_grad.astype(jnp.float32)
    post_attn, unit_two, factor_two = rms_forward(attn_total, gains_val[1])
    middle = resid_in + post_attn
    unused, unit_three, factor_three = rms_forward(middle, gains_val[2])
    post_mlp, unit_four, factor_four = rms_forward(mlp_total, gains_val[3])
    block_out = (middle + post_mlp).astype(jnp.bfloat16)
    out_grad = cotangent.astype(jnp.float32)
    mlp_grad, gain_four = rms_backward(out_grad, gains_back[3], unit_four, factor_four)
    mlp_low = mlp_grad.astype(jnp.bfloat16)
    middle_part, gain_three = rms_backward(normed_grad, gains_back[2], unit_three, factor_three)
    middle_grad = out_grad + middle_part
    attn_grad, gain_two = rms_backward(middle_grad, gains_back[1], unit_two, factor_two)
    attn_low = attn_grad.astype(jnp.bfloat16)
    out_wgrad = jnp.einsum(
        "td,tc->dc", attn_low, attention_output, preferred_element_type=jnp.float32
    )
    attended_grad = (
        jnp.einsum("td,dc->tc", attn_low, out_mat, preferred_element_type=jnp.float32)
        .astype(jnp.bfloat16)
        .reshape(token_rows, -1, HEAD_SIZE)
    )
    query_rgrad, key_rgrad, value_rgrad = attend_backward(
        rotated_queries.transpose(1, 0, 2), rotated_keys, value_low, segment, attended_grad
    )
    key_rgrad = key_rgrad[:, None]
    query_dlow = unrotate(query_rgrad, cosine, sine).astype(jnp.bfloat16).reshape(token_rows, -1)
    key_dlow = unrotate(key_rgrad, cosine, sine).astype(jnp.bfloat16).reshape(token_rows, -1)
    value_dlow = value_rgrad.astype(jnp.bfloat16).reshape(token_rows, -1)
    qkv_dlow = jnp.concatenate([query_dlow, key_dlow, value_dlow], axis=1)
    qkv_grad = jnp.einsum("td,tc->dc", attn_in, qkv_dlow, preferred_element_type=jnp.float32)
    first_part = nt_dot(qkv_dlow, qkvo_mat[:, :wide])
    low_grads = [gate_grad, up_grad, down_grad, qkv_grad.astype(jnp.bfloat16), out_wgrad.astype(jnp.bfloat16)]
    first_grad, red = finish(first_part.astype(jnp.bfloat16), low_grads)
    first_grad = first_grad.astype(jnp.float32)
    input_part, gain_one = rms_backward(first_grad, gains_back[0], unit_one, factor_one)
    input_grad = middle_grad + input_part
    gains_grad = jnp.stack([gain_one, gain_two, gain_three, gain_four])
    gate_red, up_red, down_red, qkv_red, out_red = [g.astype(jnp.float32) for g in red]
    gains_red = lax.psum_scatter(
        gains_grad.astype(jnp.bfloat16), ("dp", "zero"), scatter_dimension=1, tiled=True
    ).astype(jnp.float32)
    reduced = (
        qkv_red[:, :heads_q],
        qkv_red[:, heads_q : heads_q + heads_k],
        qkv_red[:, heads_q + heads_k :],
        out_red.T,
        gate_red,
        up_red,
        down_red.T,
        gains_red,
    )
    masters = (
        query_weight,
        key_weight,
        value_weight,
        out_weight,
        gate_weight,
        up_weight,
        down_weight,
        norm_gains,
    )
    means = (query_mean, key_mean, value_mean, out_mean, gate_mean, up_mean, down_mean, gains_mean)
    squares = (
        query_square,
        key_square,
        value_square,
        out_square,
        gate_square,
        up_square,
        down_square,
        gains_square,
    )
    rates = (
        MODEL_WIDTH ** (-0.5),
        MODEL_WIDTH ** (-0.5),
        MODEL_WIDTH ** (-0.5),
        (QUERY_HEADS * HEAD_SIZE) ** (-0.5),
        MODEL_WIDTH ** (-0.5),
        MODEL_WIDTH ** (-0.5),
        FF ** (-0.5),
        gain_rate,
    )
    decays = (weight_decay,) * 7 + (0.0,)
    moments = []
    seconds = []
    updated = []
    for index in range(8):
        moment, second, master = adam_update(
            masters[index],
            means[index],
            squares[index],
            reduced[index],
            rates[index],
            decays[index],
        )
        moments.append(moment)
        seconds.append(second)
        updated.append(master)
    return (block_out, input_grad, *moments, *seconds, *updated)


def solution(mesh):
    in_specs = (
        P(("dp", "zero"), None),
        P(("dp", "zero"), None),
        P(("dp", "zero")),
        P(("dp", "zero"), "tensor"),
        P(("dp", "zero"), "tensor"),
        P(("dp", "zero"), "tensor"),
        P("tensor", ("dp", "zero")),
        P(("dp", "zero"), "tensor"),
        P(("dp", "zero"), "tensor"),
        P("tensor", ("dp", "zero")),
        P(None, ("dp", "zero")),
        P(("dp", "zero"), "tensor"),
        P(("dp", "zero"), "tensor"),
        P(("dp", "zero"), "tensor"),
        P("tensor", ("dp", "zero")),
        P(("dp", "zero"), "tensor"),
        P(("dp", "zero"), "tensor"),
        P("tensor", ("dp", "zero")),
        P(None, ("dp", "zero")),
        P(("dp", "zero"), "tensor"),
        P(("dp", "zero"), "tensor"),
        P(("dp", "zero"), "tensor"),
        P("tensor", ("dp", "zero")),
        P(("dp", "zero"), "tensor"),
        P(("dp", "zero"), "tensor"),
        P("tensor", ("dp", "zero")),
        P(None, ("dp", "zero")),
    )
    out_specs = (
        P(("dp", "zero"), None),
        P(("dp", "zero"), None),
        P(("dp", "zero"), "tensor"),
        P(("dp", "zero"), "tensor"),
        P(("dp", "zero"), "tensor"),
        P("tensor", ("dp", "zero")),
        P(("dp", "zero"), "tensor"),
        P(("dp", "zero"), "tensor"),
        P("tensor", ("dp", "zero")),
        P(None, ("dp", "zero")),
        P(("dp", "zero"), "tensor"),
        P(("dp", "zero"), "tensor"),
        P(("dp", "zero"), "tensor"),
        P("tensor", ("dp", "zero")),
        P(("dp", "zero"), "tensor"),
        P(("dp", "zero"), "tensor"),
        P("tensor", ("dp", "zero")),
        P(None, ("dp", "zero")),
        P(("dp", "zero"), "tensor"),
        P(("dp", "zero"), "tensor"),
        P(("dp", "zero"), "tensor"),
        P("tensor", ("dp", "zero")),
        P(("dp", "zero"), "tensor"),
        P(("dp", "zero"), "tensor"),
        P("tensor", ("dp", "zero")),
        P(None, ("dp", "zero")),
    )
    return jax.shard_map(
        per_device, mesh=mesh, in_specs=in_specs, out_specs=out_specs, check_vma=False
    )
```

```python
import functools

import jax
import jax.numpy as jnp
from jax import lax
from jax.experimental import pallas as pl
from jax.experimental.pallas import tpu as pltpu
from jax.sharding import PartitionSpec as P

MESH = pl.DeviceIdType.MESH

MODEL_WIDTH = 2304
QUERY_HEADS = 8
HEAD_SIZE = 256
FF = 9216
STEP = 10
W = MODEL_WIDTH


norm_eps = 1e-06
soft_cap = 50.0
rope_base = 10000.0
beta_one = 0.9
beta_two = 0.95
adam_eps = 1e-08
weight_decay = 0.1
gain_rate = 0.7


def rms_forward(value_rows, gain):
    factor = lax.rsqrt(jnp.mean(value_rows * value_rows, axis=-1, keepdims=True) + norm_eps)
    normed = value_rows * factor
    return (normed * gain, normed, factor)


def rms_backward(grad, gain, normed, factor):
    scaled = grad * gain
    inner = jnp.mean(scaled * normed, axis=-1, keepdims=True)
    return (factor * (scaled - normed * inner), jnp.sum(grad * normed, axis=0))


def rope_tables(segment):
    index = jnp.arange(segment.shape[0], dtype=jnp.int32)
    earlier = jnp.concatenate([jnp.full((1,), -1, jnp.int32), segment[:-1]])
    first = lax.cummax(jnp.where(segment != earlier, index, 0), axis=0)
    place = (index - first).astype(jnp.float32)
    inverse = rope_base ** (-jnp.arange(0, HEAD_SIZE, 2, dtype=jnp.float32) / HEAD_SIZE)
    angle = place[:, None] * inverse[None, :]
    return (jnp.cos(angle)[:, None, :], jnp.sin(angle)[:, None, :])


def adam_update(master, mean, square, grad, rate, decay):
    moment = beta_one * mean + (1.0 - beta_one) * grad
    second = beta_two * square + (1.0 - beta_two) * grad * grad
    direction = (
        moment / (1.0 - beta_one**STEP) / (jnp.sqrt(second / (1.0 - beta_two**STEP)) + adam_eps)
    )
    return (moment, second, master - rate * (direction + decay * master))


def remote(src,dst,ss,rs,dev):
    return pltpu.make_async_remote_copy(src_ref=src,dst_ref=dst,send_sem=ss,recv_sem=rs,device_id=dev,device_id_type=MESH)

class Chain:
    def __init__(self, half, ch, P, RE, RM, O, sp, so, ve, vm, vo, lags=(1,2,3,4)):
        self.p = lax.axis_index("tensor"); p=self.p
        self.reg=half//2; self.ch=ch; self.nt=self.reg//ch
        self.P,self.RE,self.RM,self.O=P,RE,RM,O
        self.sp,self.so,self.ve,self.vm,self.vo=sp,so,ve,vm,vo
        self.lags=lags
        self.end = (p==0)|(p==3)
        self.mid = (p==1)|(p==2)
        self.to_mid = {"tensor": jnp.where(p<2, 1, 2)}
        self.to_end = {"tensor": jnp.where(p<2, 0, 3)}
        self.to_oth = {"tensor": jnp.where(p<2, 2, 1)}
        self.own = jnp.where(p<2,0,1); self.oth=1-self.own
    def rows(self, part, t):
        return pl.ds(pl.multiple_of(part*self.reg+t*self.ch,16), self.ch)
    def trow(self,t): return pl.ds(pl.multiple_of(t*self.ch,16), self.ch)
    def r1(self,h,t):
        for part in (0,1):
            r=self.rows(part,t)
            remote(self.P.at[h,r],self.RE.at[h,r],self.sp.at[h,t,part],self.ve.at[h,t,part],self.to_mid).start()
    def r2(self,h,t):
        r=self.rows(self.oth,t)
        remote(self.P.at[h,r],self.RE.at[h,r],self.sp.at[h,t,0],self.ve.at[h,t,self.oth],self.to_end).wait_recv()
        self.P[h,r,:]=self.P[h,r,:]+self.RE[h,r,:]
        remote(self.P.at[h,r],self.RM.at[h,self.trow(t)],self.sp.at[h,t,0],self.vm.at[h,t],self.to_oth).start()
    def r3(self,h,t):
        r=self.rows(self.own,t); q=self.trow(t)
        remote(self.P.at[h,r],self.RE.at[h,r],self.sp.at[h,t,0],self.ve.at[h,t,self.own],self.to_end).wait_recv()
        remote(self.P.at[h,r],self.RM.at[h,q],self.sp.at[h,t,0],self.vm.at[h,t],self.to_oth).wait_recv()
        self.O[h,r,:]=(self.P[h,r,:].astype(jnp.float32)+self.RE[h,r,:].astype(jnp.float32)+self.RM[h,q,:].astype(jnp.float32)).astype(jnp.bfloat16)
        remote(self.O.at[h,r],self.O.at[h,r],self.so.at[h,t,0],self.vo.at[h,t,self.own],self.to_end).start()
        remote(self.O.at[h,r],self.O.at[h,r],self.so.at[h,t,1],self.vo.at[h,t,self.own],self.to_oth).start()
    def b4(self,h,t):
        r=self.rows(self.oth,t)
        c=remote(self.O.at[h,r],self.O.at[h,r],self.so.at[h,t,2],self.vo.at[h,t,self.oth],self.to_end)
        c.wait_recv(); c.start()
    def b5_end(self,h,t):
        for part in (0,1):
            r=self.rows(part,t)
            remote(self.O.at[h,r],self.O.at[h,r],self.so.at[h,t,0],self.vo.at[h,t,part],self.to_mid).wait_recv()
            remote(self.P.at[h,r],self.RE.at[h,r],self.sp.at[h,t,part],self.ve.at[h,t,part],self.to_mid).wait_send()
    def b5_mid(self,h,t):
        r=self.rows(self.own,t)
        remote(self.P.at[h,r],self.RE.at[h,r],self.sp.at[h,t,0],self.ve.at[h,t,0],self.to_oth).wait_send()
        for i in range(3):
            remote(self.O.at[h,r],self.O.at[h,r],self.so.at[h,t,i],self.vo.at[h,t,0],self.to_end).wait_send()
    def tick(self, T, base0, hi0, start, base, hi):
        nt=self.nt
        def at(t0, cond, fns):
            late=t0>=start
            c=jnp.where(late,t0-base,t0-base0)
            ok=(t0>=0)&(c<jnp.where(late,hi,hi0))
            j=c//nt; h=j%2; t=c%nt
            @pl.when(ok&cond)
            def _():
                for f in fns: f(h,t)
        l1,l2,l3,l4=self.lags
        at(T,self.end,[self.r1])
        at(T-l1,self.mid,[self.r2])
        at(T-l2,self.mid,[self.r3])
        at(T-l3,self.mid,[self.b4])
        at(T-l4,self.end,[self.b5_end])
        at(T-l4,self.mid,[self.b5_mid])

def chain_scratch(half,ch):
    nt=half//2//ch
    B=jnp.bfloat16; D=pltpu.SemaphoreType.DMA
    return [pltpu.VMEM((2,half,W),B),pltpu.VMEM((2,half,W),B),pltpu.VMEM((2,half//2,W),B),pltpu.VMEM((2,half,W),B),
            D((2,nt,2)),D((2,nt,3)),D((2,nt,2)),D((2,nt)),D((2,nt,2))]


def coords():
    dp,ze=lax.axis_index("dp"),lax.axis_index("zero")
    x=dp//2; c=dp%2
    return x,c,ze
def sid(x,c,y): return (x*2+c)*2+y
class Plane:
    def __init__(self):
        x,c,y=coords()
        self.x,self.c,self.y=x,c,y
        self.toX={"dp":(1-x)*2+c}; self.toY={"zero":1-y}; self.toC={"dp":x*2+1-c}
        self.lane=[sid(x,c,y),sid(1-x,c,y),sid(x,c,1-y),sid(1-x,c,1-y)]
        d=1-c
        self.other=[sid(x,d,y),sid(1-x,d,y),sid(x,d,1-y),sid(1-x,d,1-y)]
        self.is0=c==0; self.is1=c==1
def plane_signal():
    x,c,y=coords()
    bar=pltpu.get_barrier_semaphore()
    for dev in ({"dp":(1-x)*2+c},{"zero":1-y},{"dp":x*2+1-c}):
        pl.semaphore_signal(bar, inc=1, device_id=dev, device_id_type=MESH)
def plane_barrier():
    plane_signal(); pl.semaphore_wait(pltpu.get_barrier_semaphore(),3)

class Gather:
    def __init__(self, units, ss, rs, ls):
        self.u=units; self.ss,self.rs,self.ls=ss,rs,ls; self.pl=Plane()
    def refs(self,i):
        S,F,r0,rr=self.u[i]; r=pl.ds(r0,rr)
        return S.at[r], (lambda s: F.at[s,r])
    def a(self,i):
        S,F=self.refs(i); q=self.pl; own=q.lane[0]
        remote(S,F(own),self.ss.at[i,0],self.rs.at[i,0],q.toX).start()
        remote(S,F(own),self.ss.at[i,1],self.rs.at[i,1],q.toY).start()
        remote(S,F(own),self.ss.at[i,2],self.rs.at[i,3],q.toC).start()
        pltpu.make_async_copy(S,F(own),self.ls.at[i]).start()
    def b(self,i):
        S,F=self.refs(i); q=self.pl; X,Y=q.lane[1],q.lane[2]
        remote(S,F(X),self.ss.at[i,0],self.rs.at[i,0],q.toX).wait_recv()
        @pl.when(q.is1)
        def _(): remote(F(X),F(X),self.ss.at[i,3],self.rs.at[i,2],q.toY).start()
        remote(F(X),F(X),self.ss.at[i,4],self.rs.at[i,4],q.toC).start()
        remote(S,F(Y),self.ss.at[i,1],self.rs.at[i,1],q.toY).wait_recv()
        @pl.when(q.is0)
        def _(): remote(F(Y),F(Y),self.ss.at[i,3],self.rs.at[i,2],q.toX).start()
        remote(F(Y),F(Y),self.ss.at[i,5],self.rs.at[i,5],q.toC).start()
    def d(self,i):
        S,F=self.refs(i); q=self.pl; D=q.lane[3]
        c=remote(F(D),F(D),self.ss.at[i,6],self.rs.at[i,6],q.toC)
        remote(S,F(D),self.ss.at[i,3],self.rs.at[i,2],q.toX).wait_recv()
        c.start()
    def e(self,i):
        S,F=self.refs(i); q=self.pl
        for j in range(4):
            remote(S,F(q.other[j]),self.ss.at[i,0],self.rs.at[i,3+j],q.toC).wait_recv()
        pltpu.make_async_copy(S,F(q.lane[0]),self.ls.at[i]).wait()
        for j in range(7):
            remote(S,S,self.ss.at[i,j],self.rs.at[i,0],q.toC).wait_send()
    def tick(self,T):
        n=len(self.u)
        if 0<=T<n: self.a(T)
        if 0<=T-1<n: self.b(T-1)
        if 0<=T-2<n: self.d(T-2)
        if 0<=T-3<n: self.e(T-3)
    @property
    def ticks(self): return len(self.u)+3
def gather_sems(n):
    D=pltpu.SemaphoreType.DMA
    return [D((n,7)),D((n,7)),D((n,))]

F32=jnp.float32; BF=jnp.bfloat16
class GatherD(Gather):
    def __init__(self,src,dst,n,lags,ss,rs,ls,base=0):
        self.src,self.dst,self.n,self.lags,self.base=src,dst,n,lags,base
        self.ss,self.rs,self.ls=ss,rs,ls; self.pl=Plane()
    def refs(self,i):
        i=i-self.base
        return self.src(i),(lambda s: self.dst(i,s))
    def tick(self,T):
        lb,ld,le=self.lags
        for lag,f in ((0,self.a),(lb,self.b),(ld,self.d),(le,self.e)):
            i=T-lag
            @pl.when((i>=0)&(i<self.n))
            def _(): f(i+self.base)
def gelu_parts(g):
    k=0.7978845608028654; c=0.044715
    t=jnp.tanh(k*(g+c*g*g*g))
    act=0.5*g*(1.0+t)
    der=0.5*(1.0+t)+0.5*g*(1.0-t*t)*k*(1.0+3.0*c*g*g)
    return act,der
def nt_dot(a,b): return lax.dot_general(a,b,(((1,),(1,)),((),())),preferred_element_type=F32)
def rsq(v): return lax.rsqrt(jnp.mean(v*v,axis=-1,keepdims=True)+1e-6)

def f_kernel(gather,half,ch,lags,grr,qrr,glags,tn,nheads,*refs):
    (x_ref,dy_ref,cos,sin,segc,segr,wq_ref,ga_ref,s_ref,
     at_out,f_out,d_out,n2_out,hid_out,dg_out,du_out,df_out,n1_out,q_out,k_out,v_out,o_out,w_out,g_out,gm_out,
     Wt,BIG,XS,GV,P,RE,RM,O,sp,so,ve,vm,vo,gss,grs,gls,isem,osem)=refs
    C=Chain(half,ch,P,RE,RM,O,sp,so,ve,vm,vo,lags)
    L=lags[-1]; nt=C.nt; ff=Wt.shape[2]; nj=ff//tn; nd=W//tn; total=2*half; HS=256
    qw=nheads*HS; wq=qw+2*HS+qw
    def rows(h): return pl.ds(h*half,half)
    def cp(src,dst,sem): return pltpu.make_async_copy(src,dst,sem)
    n2r=pl.ds(4*half,half); hidr=pl.ds(5*half,half)
    N2=BIG.at[n2r]; HID=BIG.at[hidr]
    def gu(k,h): return pl.ds((k*2+h)*half,half)
    WQ=BIG.at[pl.ds(0,W),pl.ds(0,wq)]
    GA=BIG.at[pl.ds(0,W),pl.ds(wq,128)]
    c0,c1=wq+128,wq+128+HS
    def qpart(hd): return (pl.ds(hd*total,total),pl.ds(c0,HS))
    kpart=(pl.ds(0,total),pl.ds(c1,HS)); vpart=(pl.ds(total,total),pl.ds(c1,HS))
    def opart(h): return (pl.ds(2*total+h*half,half),pl.ds(c0,qw))
    xin=lambda ref,h: cp(ref.at[rows(h)],XS,isem.at[0])
    xin(x_ref,0).start()
    line_signal()
    oc={}
    def out(name,src,dst,i):
        c=cp(src,dst,osem.at[i]); c.start(); oc[name]=c
    def fin(name): oc.pop(name).wait()
    shard=W//8 if gather else 0
    nq=0; st={'q':0,'g':0}
    if gather:
        plane_signal()
        pl.semaphore_wait(pltpu.get_barrier_semaphore(),line_count()+3)
        def al(v): return pl.ds(pl.multiple_of(v,16),qrr)
        per=shard//grr; nq=shard//qrr; ng=s_ref.shape[0]*per
        Gg=GatherD(lambda i: ga_ref,lambda i,s: BIG.at[pl.ds(pl.multiple_of(s*shard,16),shard),pl.ds(wq,128)],1,(0,0,0),gss,grs,gls)
        Gq=GatherD(lambda i: wq_ref.at[al(i*qrr)],lambda i,s: BIG.at[al(s*shard+i*qrr),pl.ds(0,wq)],nq,(1,2,3),gss,grs,gls,1)
        Gt=GatherD(lambda i: s_ref.at[i//per,pl.ds(pl.multiple_of((i%per)*grr,16),grr)],
                   lambda i,s: Wt.at[i//per,pl.ds(pl.multiple_of(s*shard+(i%per)*grr,16),grr)],ng,glags,gss,grs,gls,1+nq)
        def done(k): return (k+1)*per-1+glags[2]+1
        Gg.a(0); Gq.tick(0); Gg.b(0); Gg.d(0); Gq.tick(1); Gg.e(0); st['q']=2
    else:
        pl.semaphore_wait(pltpu.get_barrier_semaphore(),line_count())
        wc=[cp(s_ref.at[k],Wt.at[k],gls.at[k]) for k in range(3)]+[cp(wq_ref,WQ,gls.at[3]),cp(ga_ref,GA,gls.at[4])]
        for c in wc: c.start()
        for c in wc: c.wait()
        def done(k): return 0
    def qg(upto):
        if gather:
            while st['q']<upto: Gq.tick(st['q']); st['q']+=1
    def ag(upto):
        if gather and upto>st['g']:
            lax.fori_loop(st['g'],upto,lambda T,_: (Gt.tick(T),0)[1],0); st['g']=upto
    S={'T':0,'base0':0,'hi0':0,'start':0,'base':0,'hi':0}
    def tick(T,s): C.tick(T,s['base0'],s['hi0'],s['start'],s['base'],s['hi'])
    def top(): return S['base']+S['hi']+L
    def ticks(until,every_g=0):
        s=dict(S); T0,g0=s['T'],st['g']; until=min(until,top())
        if until<=T0: return
        def body(T,_):
            tick(T,s)
            if every_g and gather:
                @pl.when((T-T0)%every_g==0)
                def _(): Gt.tick(g0+(T-T0)//every_g)
            return 0
        lax.fori_loop(T0,until,body,0)
        S['T']=until
        if every_g and gather: st['g']=g0+(until-T0+every_g-1)//every_g
    def finish(c,every_g=0):
        base=S['base'] if c>S['hi0'] else S['base0']
        ticks(base+c+L,every_g)
    def ready(c):
        if S['T']>S['base']+S['hi']:
            ticks(S['start']+L)
            S.update(base0=S['base'],hi0=S['hi'],start=S['T'],base=S['T']-S['hi'])
        S['hi']=c
    def units(n,fn,every=0,eg=0):
        s=dict(S); T0,g0=s['T'],st['g']
        def body(i,_):
            fn(i)
            if every:
                @pl.when((i+1)%every==0)
                def _(): tick(T0+i//every,s)
            if eg and gather:
                @pl.when((i+1)%eg==0)
                def _(): Gt.tick(g0+i//eg)
            return 0
        lax.fori_loop(0,n,body,0)
        if eg and gather: st['g']=g0+n//eg
        if every: S['T']=min(T0+n//every,max(top(),T0))
    def wait_w(k):
        while gather and st['g']<done(k):
            ag(st['g']+1); ticks(S['T']+2)
    nr=32; nn=half//nr
    def rch(i): return pl.ds(pl.multiple_of(i*nr,nr),nr)
    def gain(k): return GV[k:k+1,:]
    def norm0(h):
        def f(i):
            r=rch(i)
            v=XS[r,:].astype(F32)
            P[h,r,:]=(v*rsq(v)*gain(0)).astype(BF)
        return f
    def norm1(h):
        def f(i):
            r=rch(i)
            a=O[h,r,:].astype(F32)
            h1=XS[r,:].astype(F32)+a*rsq(a)*gain(1)
            BIG[pl.ds(pl.multiple_of(4*half+i*nr,nr),nr),:]=(h1*rsq(h1)*gain(2)).astype(BF)
        return f
    def normf(h):
        def f(i):
            r=rch(i)
            v=O[h,r,:].astype(F32); q=rsq(v); z=v*q
            s=XS[r,:].astype(F32)*gain(3)
            BIG[pl.ds(pl.multiple_of(4*half+i*nr,nr),nr),:]=(q*(s-z*jnp.mean(s*z,axis=-1,keepdims=True))).astype(BF)
        return f
    def qkv(h):
        def f(j):
            t=jnp.dot(P[h],BIG[pl.ds(0,W),pl.ds(pl.multiple_of(j*HS,HS),HS)],preferred_element_type=F32)
            return t
        cs=cos[rows(h),:]; sn=sin[rows(h),:]
        def rot(t):
            a,b=t[:,:HS//2],t[:,HS//2:]
            return jnp.concatenate([a*cs-b*sn,b*cs+a*sn],axis=1).astype(BF)
        for hd in range(nheads): BIG[pl.ds(hd*total+h*half,half),pl.ds(c0,HS)]=rot(f(hd))
        BIG[pl.ds(h*half,half),pl.ds(c1,HS)]=rot(f(nheads))
        BIG[pl.ds(total+h*half,half),pl.ds(c1,HS)]=f(nheads+1).astype(BF)
    qb=half//2
    def attend(h):
        nk=(h+1)*half; ks=pl.ds(0,nk)
        def f(i):
            hd=i%nheads; r0=h*half+(i//nheads)*qb
            rr=pl.ds(pl.multiple_of(r0,16),qb)
            q=BIG[pl.ds(pl.multiple_of(hd*total+r0,16),qb),pl.ds(c0,HS)]
            s=nt_dot(q,BIG[pl.ds(0,nk),pl.ds(c1,HS)])*(HS**-0.5)
            cc=50.0*jnp.tanh(s*(1.0/50.0))
            ri=r0+lax.broadcasted_iota(jnp.int32,(qb,nk),0); ci=lax.broadcasted_iota(jnp.int32,(qb,nk),1)
            vis=(ci<=ri)&(segc[rr,:]==segr[:,ks])
            cc=jnp.where(vis,cc,-jnp.inf)
            e=jnp.exp(cc-jnp.max(cc,axis=-1,keepdims=True))
            p=(e/jnp.sum(e,axis=-1,keepdims=True)).astype(BF)
            o=jnp.dot(p,BIG[pl.ds(total,nk),pl.ds(c1,HS)],preferred_element_type=F32).astype(BF)
            BIG[pl.ds(pl.multiple_of(2*total+r0,16),qb),pl.ds(pl.multiple_of(c0+hd*HS,128),HS)]=o
        return f
    def col(j): return pl.ds(pl.multiple_of(j*tn,tn),tn)
    def outp(h):
        def f(j): P[h,:,col(j)]=nt_dot(BIG[opart(h)],BIG[col(j),pl.ds(qw+2*HS,qw)]).astype(BF)
        return f
    def gate(h):
        def f(j): BIG[gu(0,h),col(j)]=jnp.dot(N2[...],Wt[0,:,col(j)],preferred_element_type=F32).astype(BF)
        return f
    def up(h):
        def f(j):
            u=jnp.dot(N2[...],Wt[1,:,col(j)],preferred_element_type=F32)
            g=BIG[gu(0,h),col(j)].astype(F32)
            act,_=gelu_parts(g)
            BIG[gu(1,h),col(j)]=u.astype(BF)
            BIG[hidr,col(j)]=(act*u).astype(BF)
        return f
    def down(h):
        def f(j): P[h,:,col(j)]=nt_dot(HID[...],Wt[2,col(j),:]).astype(BF)
        return f
    def bwd1(h):
        def f(j):
            d=jnp.dot(N2[...],Wt[2,:,col(j)],preferred_element_type=F32)
            g=BIG[gu(0,h),col(j)].astype(F32); u=BIG[gu(1,h),col(j)].astype(F32)
            act,der=gelu_parts(g)
            BIG[gu(0,h),col(j)]=(d*u*der).astype(BF)
            BIG[gu(1,h),col(j)]=(d*act).astype(BF)
        return f
    def bwd2(h):
        def f(j):
            P[h,:,col(j)]=(nt_dot(BIG[gu(0,h),:],Wt[0,col(j),:])+nt_dot(BIG[gu(1,h),:],Wt[1,col(j),:])).astype(BF)
        return f
    GV[...]=jnp.transpose(GA[...].astype(F32))[:8,:]
    xin(x_ref,0).wait()
    units(nn,norm0(0))
    xin(x_ref,1).start()
    out('g',GV,g_out,7)
    out('n1a',P.at[0],n1_out.at[rows(0)],4)
    qg(nq)
    ag(1)
    xin(x_ref,1).wait()
    units(nn,norm0(1))
    xin(x_ref,0).start()
    out('n1b',P.at[1],n1_out.at[rows(1)],5)
    qg(nq+3)
    ag(2)
    out('w',WQ,w_out,6)
    qkv(0)
    ag(3)
    qkv(1)
    out('q0',BIG.at[qpart(0)],q_out.at[0],0)
    if nheads>1: out('q1',BIG.at[qpart(1)],q_out.at[1],1)
    out('k',BIG.at[kpart],k_out,2)
    out('v',BIG.at[vpart],v_out,3)
    ag(4)
    fin('n1a'); fin('n1b')
    units(2*nheads,attend(0),eg=4)
    units(nd,outp(0))
    ready(nt)
    units(2*nheads,attend(1),1,eg=4)
    units(nd,outp(1),3)
    ready(2*nt)
    out('o0',BIG.at[opart(0)],o_out.at[rows(0)],8)
    out('o1',BIG.at[opart(1)],o_out.at[rows(1)],9)
    finish(nt,2)
    out('at0',O.at[0],at_out.at[rows(0)],10)
    xin(x_ref,0).wait()
    for k in ('q0','q1','k','v','o0','o1','w','g'):
        if k in oc: fin(k)
    units(nn,norm1(0),7)
    xin(x_ref,1).start()
    out('n2',N2,n2_out.at[rows(0)],0)
    wait_w(0)
    units(nj,gate(0),3)
    wait_w(1)
    units(nj,up(0),4)
    out('hid',HID,hid_out.at[rows(0)],1)
    wait_w(2)
    fin('at0')
    units(nd,down(0),3)
    ready(3*nt)
    finish(2*nt)
    out('at1',O.at[1],at_out.at[rows(1)],11)
    xin(x_ref,1).wait()
    fin('n2')
    units(nn,norm1(1),7)
    xin(dy_ref,0).start()
    out('n2',N2,n2_out.at[rows(1)],0)
    units(nj,gate(1),3)
    fin('hid')
    units(nj,up(1),4)
    out('hid',HID,hid_out.at[rows(1)],1)
    fin('at1')
    units(nd,down(1),3)
    ready(4*nt)
    finish(3*nt)
    out('f0',O.at[0],f_out.at[rows(0)],10)
    xin(dy_ref,0).wait()
    fin('n2')
    units(nn,normf(0),7)
    xin(dy_ref,1).start()
    out('df',N2,df_out.at[rows(0)],0)
    units(nj,bwd1(0),3)
    out('dg0',BIG.at[gu(0,0)],dg_out.at[rows(0)],2); out('du0',BIG.at[gu(1,0)],du_out.at[rows(0)],3)
    fin('f0')
    units(nd,bwd2(0),2)
    ready(5*nt)
    finish(4*nt)
    out('f1',O.at[1],f_out.at[rows(1)],11)
    xin(dy_ref,1).wait()
    fin('df')
    units(nn,normf(1),7)
    out('df',N2,df_out.at[rows(1)],0)
    units(nj,bwd1(1),3)
    out('dg1',BIG.at[gu(0,1)],dg_out.at[rows(1)],4); out('du1',BIG.at[gu(1,1)],du_out.at[rows(1)],5)
    fin('f1'); fin('df'); fin('hid')
    n2f=pl.ds(2*total,total); dff=pl.ds(0,total); hidf=pl.ds(total,total)
    back=[cp(n2_out,BIG.at[n2f],isem.at[1]),cp(df_out,Wt.at[2,dff],isem.at[2]),cp(hid_out,Wt.at[2,hidf],isem.at[3])]
    for c in back: c.start()
    units(nd,bwd2(1),2)
    ready(6*nt)
    for c in back: c.wait()
    def wgrad(lhs,rhs,k):
        def f(j):
            lt=lhs(col(j))
            for n in range(0,ff,768):
                t=lax.dot_general(lt,rhs(pl.ds(n,768)),(((0,),(0,)),((),())),preferred_element_type=F32)
                Wt[k,col(j),pl.ds(n,768)]=t.astype(BF)
        return f
    units(nd,wgrad(lambda c: Wt[2,dff,c],lambda c: Wt[2,hidf,c],0),1)
    out('gd',Wt.at[0],gm_out.at[2],6)
    units(nd,wgrad(lambda c: BIG[n2f,c],lambda c: BIG[pl.ds(0,total),c],1),1)
    out('gg',Wt.at[1],gm_out.at[0],7)
    finish(5*nt)
    out('d0',O.at[0],d_out.at[rows(0)],10)
    units(nd,wgrad(lambda c: BIG[n2f,c],lambda c: BIG[pl.ds(total,total),c],2),1)
    out('gu',Wt.at[2],gm_out.at[1],8)
    finish(6*nt)
    out('d1',O.at[1],d_out.at[rows(1)],11)
    for k in list(oc): fin(k)

def line_signal():
    te=lax.axis_index("tensor")
    bar=pltpu.get_barrier_semaphore()
    @pl.when(te<3)
    def _(): pl.semaphore_signal(bar, inc=1, device_id={"tensor":te+1}, device_id_type=MESH)
    @pl.when(te>0)
    def _(): pl.semaphore_signal(bar, inc=1, device_id={"tensor":te-1}, device_id_type=MESH)
def line_count():
    te=lax.axis_index("tensor")
    return (te<3).astype(jnp.int32)+(te>0).astype(jnp.int32)

def forward_both(x,dy,cos,sin,seg,qkvo,gains,shards,nheads,gather,cid=9,ch=16,lags=(2,3,4,5),grr=48,qrr=48,glags=(3,4,6),tn=256):
    total=x.shape[0]; half=total//2; D=pltpu.SemaphoreType.DMA; ff=shards.shape[2]; w3=qkvo.shape[1]
    ng=(1+qkvo.shape[0]//qrr+shards.shape[0]*shards.shape[1]//grr) if gather else 5
    sds=jax.ShapeDtypeStruct
    act=sds((total,W),BF); wide=sds((total,ff),BF); hd=sds((total,256),BF)
    A=pl.BlockSpec(memory_space=pl.ANY); V=pl.BlockSpec(memory_space=pltpu.VMEM)
    return pl.pallas_call(functools.partial(f_kernel,gather,half,ch,lags,grr,qrr,glags,tn,nheads),
        out_shape=[act,act,act,act,wide,wide,wide,act,act,sds((nheads,total,256),BF),hd,hd,sds((total,nheads*256),BF),sds((W,w3),BF),sds((8,W),F32)]+[sds((3,W,ff),BF)],
        in_specs=[A,A,V,V,V,V,A,A,A],out_specs=[A]*16,
        scratch_shapes=[pltpu.VMEM((3,W,ff),BF),pltpu.VMEM((6*half,W),BF),pltpu.VMEM((half,W),BF),pltpu.VMEM((8,W),F32)]
            +chain_scratch(half,ch)+gather_sems(ng)+[D((4,)),D((12,))],
        compiler_params=pltpu.CompilerParams(collective_id=cid,has_side_effects=True,vmem_limit_bytes=64*2**20))(
            x,dy,cos,sin,seg.reshape(-1,1),seg.reshape(1,-1),qkvo,gains,shards)
class Ring:
    def __init__(self,src,dst,base,n,rr,cols,bufs,ss,rs,ls):
        self.src,self.dst,self.base,self.n,self.rr,self.cols=src,dst,base,n,rr,cols
        self.lags=(1,3,5)
        self.LB,self.OB,self.CB,self.DB,self.XB,self.YB=bufs
        self.ss,self.rs,self.ls=ss,rs,ls; self.pl=Plane()
    def at(self,ref,*idx): return ref.at[(*idx,pl.ds(0,self.rr),pl.ds(0,self.cols))]
    def get(self,i):
        s=i%self.LB.shape[0]; c=i%self.CB.shape[0]; d=i%self.DB.shape[0]; o=i%2
        lb=lambda j: self.at(self.LB,s,j)
        cb=lambda j: self.at(self.CB,c,j)
        return (lambda k: self.src(i-self.base,k)),lb,cb,self.at(self.DB,d),self.at(self.XB,d),self.at(self.YB,d),self.at(self.OB,o)
    def p1(self,i):
        g,lb,cb,db,xb,yb,ob=self.get(i); q=self.pl
        for j in (3,1,2,0):
            remote(g(q.other[j]),cb(j),self.ss.at[i,j],self.rs.at[i,j],q.toC).start()
            pltpu.make_async_copy(g(q.lane[j]),lb(j),self.ls.at[i,j]).start()
    def p2(self,i):
        g,lb,cb,db,xb,yb,ob=self.get(i); q=self.pl
        for j in (3,1,2,0):
            pltpu.make_async_copy(g(q.lane[j]),lb(j),self.ls.at[i,j]).wait()
            remote(g(q.other[j]),cb(j),self.ss.at[i,j],self.rs.at[i,j],q.toC).wait_recv()
            lb(j)[...]=lb(j)[...]+cb(j)[...]
            if j==3:
                @pl.when(q.is0)
                def _(): remote(lb(3),db,self.ss.at[i,4],self.rs.at[i,4],q.toX).start()
                @pl.when(q.is1)
                def _(): remote(lb(3),db,self.ss.at[i,4],self.rs.at[i,4],q.toY).start()
            if j==1:
                @pl.when(q.is0)
                def _(): remote(lb(1),xb,self.ss.at[i,5],self.rs.at[i,5],q.toX).start()
            if j==2:
                @pl.when(q.is1)
                def _(): remote(lb(2),yb,self.ss.at[i,5],self.rs.at[i,6],q.toY).start()
    def p3(self,i):
        g,lb,cb,db,xb,yb,ob=self.get(i); q=self.pl
        remote(lb(3),db,self.ss.at[i,4],self.rs.at[i,4],q.toX).wait_recv()
        def relay(j,buf,sem,dev):
            lb(j)[...]=lb(j)[...]+db[...]
            remote(lb(j),buf,self.ss.at[i,6],self.rs.at[i,sem],dev).start()
        @pl.when(q.is0)
        def _(): relay(2,yb,6,q.toY)
        @pl.when(q.is1)
        def _(): relay(1,xb,5,q.toX)
    def p4(self,i):
        g,lb,cb,db,xb,yb,ob=self.get(i); q=self.pl
        remote(lb(0),xb,self.ss.at[i,5],self.rs.at[i,5],q.toX).wait_recv()
        remote(lb(0),yb,self.ss.at[i,5],self.rs.at[i,6],q.toY).wait_recv()
        ob[...]=(lb(0)[...].astype(F32)+xb[...].astype(F32)+yb[...].astype(F32)).astype(BF)
        pltpu.make_async_copy(ob,self.dst(i-self.base),self.ls.at[i,4]).start()
        for j in range(7):
            remote(lb(0),xb,self.ss.at[i,j],self.rs.at[i,0],q.toX).wait_send()
    def p5(self,i):
        g,lb,cb,db,xb,yb,ob=self.get(i)
        pltpu.make_async_copy(ob,self.dst(i-self.base),self.ls.at[i,4]).wait()
    def tick(self,T):
        l2,l3,l4=self.lags
        for lag,f in ((0,self.p1),(l2,self.p2),(l3,self.p3),(l4+1,self.p5),(l4,self.p4)):
            i=T-lag
            @pl.when((i>=self.base)&(i<self.base+self.n))
            def _(): f(i)

def b_kernel(scatter,half,ch,lags,rr,tn,nheads,*refs):
    (at_ref,x_ref,dy_ref,dn_ref,n1_ref,w_ref,q_ref,k_ref,v_ref,o_ref,gv,cos,sin,segc,segr,gm_ref,
     t_out,h_out,acc_out,rm_out,rq_out,
     WQ,N1,X2,X3,Q,K,V,OO,DO,DQ,DK,DV,ACC,LB,OB,CB,DB,XB,YB,ss,rs,ls,
     P,RE,RM,O,sp,so,ve,vm,vo,isem,osem)=refs
    C=Chain(half,ch,P,RE,RM,O,sp,so,ve,vm,vo,lags)
    L=lags[-1]; nt=C.nt; total=2*half; HS=256; qw=nheads*HS; wide=qw+2*HS; nd=W//tn
    def cp(src,dst,i): return pltpu.make_async_copy(src,dst,isem.at[i])
    def rows(h): return pl.ds(h*half,half)
    first=[cp(at_ref.at[rows(1)],P.at[0],0),cp(x_ref.at[rows(1)],N1.at[rows(1)],2),cp(dy_ref.at[rows(1)],X2.at[rows(1)],3),cp(dn_ref.at[rows(1)],X3.at[rows(1)],4)]
    second=[cp(at_ref.at[rows(0)],P.at[1],1),cp(x_ref.at[rows(0)],N1.at[rows(0)],10),cp(dy_ref.at[rows(0)],X2.at[rows(0)],11),cp(dn_ref.at[rows(0)],X3.at[rows(0)],12)]
    later=[cp(w_ref,WQ,5),cp(q_ref,Q,6),cp(k_ref,K,7),cp(v_ref,V,8),cp(o_ref,OO,9)]
    for c in first+later+second: c.start()
    line_signal(); st={'r':0}
    if scatter:
        plane_signal()
        pl.semaphore_wait(pltpu.get_barrier_semaphore(),line_count()+3)
        bufs=(LB,OB,CB,DB,XB,YB); shard=W//8; per=shard//rr; nm=3*per; nq=per
        def gi(k,r): return pl.ds(pl.multiple_of(k*shard+r*rr,16),rr)
        R1=Ring(lambda i,k: gm_ref.at[i//per,gi(k,i%per)],lambda i: rm_out.at[i//per,pl.ds(pl.multiple_of((i%per)*rr,16),rr)],0,nm,rr,W,bufs,ss,rs,ls)
        R2=Ring(lambda i,k: WQ.at[gi(k,i)],lambda i: rq_out.at[pl.ds(pl.multiple_of(i*rr,16),rr)],nm,nq,rr,wide+qw,bufs,ss,rs,ls)
    else:
        pl.semaphore_wait(pltpu.get_barrier_semaphore(),line_count())
    def rg(n):
        for _ in range(n):
            if scatter: R1.tick(st['r'])
            st['r']+=1
    S={'T':0,'base0':0,'hi0':0,'start':0,'base':0,'hi':0}
    def tick(T,s): C.tick(T,s['base0'],s['hi0'],s['start'],s['base'],s['hi'])
    def top(): return S['base']+S['hi']+L
    def ready(c):
        if S['T']>S['base']+S['hi']:
            loop(S['start']+L-S['T'],1)
            S.update(base0=S['base'],hi0=S['hi'],start=S['T'],base=S['T']-S['hi'])
        S['hi']=c
    def units(n,fn,every=0,er=0):
        s=dict(S); T0,r0=s['T'],st['r']
        def body(i,_):
            fn(i)
            if every:
                @pl.when((i+1)%every==0)
                def _(): tick(T0+i//every,s)
            if er and scatter:
                @pl.when((i+1)%er==0)
                def _(): R1.tick(r0+i//er)
            return 0
        lax.fori_loop(0,n,body,0)
        if er: st['r']=r0+n//er
        if every: S['T']=min(T0+n//every,max(top(),T0))
    def loop(n,every,er=0,both=False):
        if n>0: units(n,lambda i: None,every,er)
    rg(2)
    for c in first: c.wait()
    nr=16; nh=half//nr
    ACC[...]=jnp.zeros_like(ACC)
    def back(h):
        def f(i):
            r=pl.ds(pl.multiple_of(i*nr,nr),nr); rf=pl.ds(pl.multiple_of(h*half+i*nr,nr),nr)
            a=P[1-h,r,:].astype(F32); q1=rsq(a); z2=a*q1
            h1=N1[rf,:].astype(F32)+z2*gv[1:2,:]; q2=rsq(h1); z3=h1*q2
            d=X3[rf,:].astype(F32); s=d*gv[2:3,:]
            dh=X2[rf,:].astype(F32)+q2*(s-z3*jnp.mean(s*z3,axis=-1,keepdims=True))
            s2=dh*gv[1:2,:]
            X2[rf,:]=(q1*(s2-z2*jnp.mean(s2*z2,axis=-1,keepdims=True))).astype(BF)
            X3[rf,:]=dh.astype(BF)
            u=dh*z2; w=d*z3
            ACC[0]+=u[:8]+u[8:]; ACC[1]+=w[:8]+w[8:]
        return f
    def col(j): return pl.ds(pl.multiple_of(j*tn,tn),tn)
    def tn_dot(a,b): return lax.dot_general(a,b,(((0,),(0,)),((),())),preferred_element_type=F32)
    def dout(h):
        for c in range(nheads):
            DO[rows(h),pl.ds(c*HS,HS)]=jnp.dot(X2[rows(h),:],WQ[:,pl.ds(wide+c*HS,HS)],preferred_element_type=F32).astype(BF)
    def gout(j): WQ[col(j),pl.ds(wide,qw)]=tn_dot(X2[:,col(j)],OO[...]).astype(BF)
    qb=half//2; sc=HS**-0.5
    def unrot(t,rr_):
        a,b=t[:,:HS//2],t[:,HS//2:]; cs=cos[rr_,:]; sn=sin[rr_,:]
        return jnp.concatenate([a*cs+b*sn,b*cs-a*sn],axis=1)
    def attend(h):
        nk=(h+1)*half; ks=pl.ds(0,nk)
        def f(i):
            hd=i%nheads; r0=h*half+(i//nheads)*qb; rq=pl.ds(pl.multiple_of(r0,16),qb); hc_=pl.ds(pl.multiple_of(hd*HS,HS),HS)
            q=Q[hd,rq,:]; do=DO[rq,hc_]
            t=jnp.tanh(nt_dot(q,K[ks,:])*(sc/50.0))
            ri=r0+lax.broadcasted_iota(jnp.int32,(qb,nk),0); ci=lax.broadcasted_iota(jnp.int32,(qb,nk),1)
            vis=(ci<=ri)&(segc[rq,:]==segr[:,ks])
            cc=jnp.where(vis,50.0*t,-jnp.inf)
            e=jnp.exp(cc-jnp.max(cc,axis=-1,keepdims=True))
            p=e/jnp.sum(e,axis=-1,keepdims=True)
            dp=nt_dot(do,V[ks,:])
            inner=jnp.sum(p*dp,axis=-1,keepdims=True)
            ds=(p*(dp-inner)*(1.0-t*t)).astype(BF)
            DQ[rq,hc_]=unrot(jnp.dot(ds,K[ks,:],preferred_element_type=F32)*sc,rq).astype(BF)
            DK[ks,:]+=tn_dot(ds,q)
            DV[ks,:]+=tn_dot(p.astype(BF),do)
        return f
    def keys(h):
        DQ[rows(h),pl.ds(qw,HS)]=unrot(DK[rows(h),:]*sc,rows(h)).astype(BF)
        DQ[rows(h),pl.ds(qw+HS,HS)]=DV[rows(h),:].astype(BF)
    def dn1(h):
        def f(j): P[1-h,:,col(j)]=nt_dot(DQ[rows(h),:],WQ[col(j),pl.ds(0,wide)]).astype(BF)
        return f
    def gqkv(j): WQ[col(j),pl.ds(0,wide)]=tn_dot(N1[:,col(j)],DQ[...]).astype(BF)
    DK[...]=jnp.zeros_like(DK); DV[...]=jnp.zeros_like(DV)
    units(nh,back(1),0,28)
    for c in later: c.wait()
    dout(1)
    units(2*nheads,attend(1),0,2)
    keys(1)
    units(nd,dn1(1),0,9)
    for c in second: c.wait()
    ready(nt)
    units(nh,back(0),7,14)
    n1c=cp(n1_ref,N1,2); n1c.start()
    hc=cp(X3,h_out,3); hc.start()
    ac=cp(ACC,acc_out,4); ac.start()
    dout(0)
    units(nd,gout,3,9)
    units(2*nheads,attend(0),1,2)
    keys(0)
    units(nd,dn1(0),3)
    ready(2*nt)
    n1c.wait()
    units(nd,gqkv,1,2)
    outs=[pltpu.make_async_copy(O.at[h],t_out.at[rows(1-h)],osem.at[h]) for h in (0,1)]
    rest=top()-S['T']
    if scatter:
        k1=max(0,min(rest//2,nm-st['r']))
        loop(2*k1,1,2)
        rest-=2*k1; r0=st['r']; last=nm+nq+R1.lags[2]+1; s=dict(S); T0=S['T']
        k2=(rest+1)//2
        def body2(i,_):
            R1.tick(r0+i); R2.tick(r0+i); tick(T0+2*i,s); tick(T0+2*i+1,s)
            return 0
        if k2>0: lax.fori_loop(0,k2,body2,0)
        r0+=max(k2,0)
        for c in outs: c.start()
        def body3(i,_):
            R1.tick(i); R2.tick(i); return 0
        lax.fori_loop(r0,last,body3,0)
    else:
        loop(rest,1)
        for c in outs: c.start()
        wc=cp(WQ,rq_out,5); wc.start(); wc.wait()
    for c in outs+[hc,ac]: c.wait()

def backward_both(at,x,dy,dn,n1,w,q,k,v,o,gv,cos,sin,seg,gm,scatter,cid=10,ch=16,lags=(2,3,4,5),rr=48,tn=256,ring=(6,6,14)):
    total=x.shape[0]; half=total//2; D=pltpu.SemaphoreType.DMA; sds=jax.ShapeDtypeStruct; nheads=q.shape[0]
    A=pl.BlockSpec(memory_space=pl.ANY); V=pl.BlockSpec(memory_space=pltpu.VMEM); M=pltpu.VMEM
    qw=nheads*256; wide=qw+512; w3=w.shape[1]; act=sds((total,W),BF)
    if scatter: outs=[sds((3,W//8,W),BF),sds((W//8,w3),BF)]; nu=4*(W//8//rr)
    else: outs=[sds((8,128),BF),sds((W,w3),BF)]; nu=1; ring=(1,1,1); rr=16
    nl,nc,nx=ring
    return pl.pallas_call(functools.partial(b_kernel,scatter,half,ch,lags,rr,tn,nheads),
        out_shape=[act,act,sds((2,8,W),F32)]+outs,
        in_specs=[A]*10+[V]*5+[A],out_specs=[A]*5,
        scratch_shapes=[M((W,w3),BF),M((total,W),BF),M((total,W),BF),M((total,W),BF),M((nheads,total,256),BF),M((total,256),BF),M((total,256),BF),
            M((total,qw),BF),M((total,qw),BF),M((total,wide),BF),M((total,256),F32),M((total,256),F32),M((2,8,W),F32),
            M((nl,4,rr,W),BF),M((2,rr,W),BF),M((nc,4,rr,W),BF),M((nx,rr,W),BF),M((nx,rr,W),BF),M((nx,rr,W),BF),D((nu,7)),D((nu,7)),D((nu,5))]
            +chain_scratch(half,ch)+[D((13,)),D((2,))],
        compiler_params=pltpu.CompilerParams(collective_id=cid,has_side_effects=True,vmem_limit_bytes=64*2**20))(
            at,x,dy,dn,n1,w,q,k,v,o,gv,cos,sin,seg.reshape(-1,1),seg.reshape(1,-1),gm)

def small_plane():
    return (lax.axis_size("dp"), lax.axis_size("zero")) == (4, 2)


def per_device(
    inputs,
    cotangent,
    segment,
    query_weight,
    key_weight,
    value_weight,
    out_weight,
    gate_weight,
    up_weight,
    down_weight,
    norm_gains,
    query_mean,
    key_mean,
    value_mean,
    out_mean,
    gate_mean,
    up_mean,
    down_mean,
    gains_mean,
    query_square,
    key_square,
    value_square,
    out_square,
    gate_square,
    up_square,
    down_square,
    gains_square,
):
    qkvo_low = jnp.concatenate(
        [query_weight, key_weight, value_weight, out_weight.T], axis=1
    ).astype(jnp.bfloat16)
    mlp_shards = jnp.stack([gate_weight, up_weight, down_weight.T]).astype(jnp.bfloat16)
    gains_low = jnp.pad(norm_gains.T.astype(jnp.bfloat16), ((0, 0), (0, 124)))
    if not small_plane():
        both = ("dp", "zero")
        qkvo_low = lax.all_gather(qkvo_low, both, axis=0, tiled=True)
        gains_low = lax.all_gather(gains_low, both, axis=0, tiled=True)
        mlp_shards = lax.all_gather(mlp_shards, both, axis=1, tiled=True)
    heads_q = query_weight.shape[1]
    heads_k = key_weight.shape[1]
    wide = heads_q + 2 * heads_k
    token_rows = inputs.shape[0]
    cosine, sine = rope_tables(segment)
    (
        attn_total,
        mlp_total,
        normed_grad,
        unused_mlp_in,
        unused_hidden,
        unused_gate_dlow,
        unused_up_dlow,
        unused_mlp_low,
        attn_in,
        rotated_queries,
        rotated_keys,
        value_low,
        attention_output,
        qkvo_mat,
        gains_val,
        mlp_grads,
    ) = forward_both(
        inputs,
        cotangent,
        cosine[:, 0],
        sine[:, 0],
        segment,
        qkvo_low,
        gains_low,
        mlp_shards,
        heads_q // HEAD_SIZE,
        small_plane(),
    )
    first_grad, middle_grad, sums, mlp_red, qkvo_red = backward_both(
        attn_total,
        inputs,
        cotangent,
        normed_grad,
        attn_in,
        qkvo_mat,
        rotated_queries,
        rotated_keys,
        value_low,
        attention_output,
        gains_val,
        cosine[:, 0],
        sine[:, 0],
        segment,
        mlp_grads,
        small_plane(),
    )
    if not small_plane():
        mlp_red = lax.psum_scatter(mlp_grads, both, scatter_dimension=1, tiled=True)
        qkvo_red = lax.psum_scatter(qkvo_red, both, scatter_dimension=0, tiled=True)
    resid_in = inputs.astype(jnp.float32)
    out_grad = cotangent.astype(jnp.float32)
    unused, unit_one, factor_one = rms_forward(resid_in, gains_val[0])
    post_attn, unused, unused = rms_forward(attn_total.astype(jnp.float32), gains_val[1])
    post_mlp, unit_four, unused = rms_forward(mlp_total.astype(jnp.float32), gains_val[3])
    block_out = (resid_in + post_attn + post_mlp).astype(jnp.bfloat16)
    gain_four = jnp.sum(out_grad * unit_four, axis=0)
    gain_two, gain_three = jnp.sum(sums, axis=1)
    input_part, gain_one = rms_backward(
        first_grad.astype(jnp.float32), gains_val[0], unit_one, factor_one
    )
    input_grad = middle_grad.astype(jnp.float32) + input_part
    gains_grad = jnp.stack([gain_one, gain_two, gain_three, gain_four])
    gate_red, up_red, down_red = mlp_red.astype(jnp.float32)
    qkvo_red = qkvo_red.astype(jnp.float32)
    gains_red = lax.psum_scatter(
        gains_grad.astype(jnp.bfloat16), ("dp", "zero"), scatter_dimension=1, tiled=True
    ).astype(jnp.float32)
    reduced = (
        qkvo_red[:, :heads_q],
        qkvo_red[:, heads_q : heads_q + heads_k],
        qkvo_red[:, heads_q + heads_k : wide],
        qkvo_red[:, wide:].T,
        gate_red,
        up_red,
        down_red.T,
        gains_red,
    )
    masters = (
        query_weight,
        key_weight,
        value_weight,
        out_weight,
        gate_weight,
        up_weight,
        down_weight,
        norm_gains,
    )
    means = (query_mean, key_mean, value_mean, out_mean, gate_mean, up_mean, down_mean, gains_mean)
    squares = (
        query_square,
        key_square,
        value_square,
        out_square,
        gate_square,
        up_square,
        down_square,
        gains_square,
    )
    rates = (
        MODEL_WIDTH ** (-0.5),
        MODEL_WIDTH ** (-0.5),
        MODEL_WIDTH ** (-0.5),
        (QUERY_HEADS * HEAD_SIZE) ** (-0.5),
        MODEL_WIDTH ** (-0.5),
        MODEL_WIDTH ** (-0.5),
        FF ** (-0.5),
        gain_rate,
    )
    decays = (weight_decay,) * 7 + (0.0,)
    moments = []
    seconds = []
    updated = []
    for index in range(8):
        moment, second, master = adam_update(
            masters[index],
            means[index],
            squares[index],
            reduced[index],
            rates[index],
            decays[index],
        )
        moments.append(moment)
        seconds.append(second)
        updated.append(master)
    return (block_out, input_grad, *moments, *seconds, *updated)


def solution(mesh):
    in_specs = (
        P(("dp", "zero"), None),
        P(("dp", "zero"), None),
        P(("dp", "zero")),
        P(("dp", "zero"), "tensor"),
        P(("dp", "zero"), "tensor"),
        P(("dp", "zero"), "tensor"),
        P("tensor", ("dp", "zero")),
        P(("dp", "zero"), "tensor"),
        P(("dp", "zero"), "tensor"),
        P("tensor", ("dp", "zero")),
        P(None, ("dp", "zero")),
        P(("dp", "zero"), "tensor"),
        P(("dp", "zero"), "tensor"),
        P(("dp", "zero"), "tensor"),
        P("tensor", ("dp", "zero")),
        P(("dp", "zero"), "tensor"),
        P(("dp", "zero"), "tensor"),
        P("tensor", ("dp", "zero")),
        P(None, ("dp", "zero")),
        P(("dp", "zero"), "tensor"),
        P(("dp", "zero"), "tensor"),
        P(("dp", "zero"), "tensor"),
        P("tensor", ("dp", "zero")),
        P(("dp", "zero"), "tensor"),
        P(("dp", "zero"), "tensor"),
        P("tensor", ("dp", "zero")),
        P(None, ("dp", "zero")),
    )
    out_specs = (
        P(("dp", "zero"), None),
        P(("dp", "zero"), None),
        P(("dp", "zero"), "tensor"),
        P(("dp", "zero"), "tensor"),
        P(("dp", "zero"), "tensor"),
        P("tensor", ("dp", "zero")),
        P(("dp", "zero"), "tensor"),
        P(("dp", "zero"), "tensor"),
        P("tensor", ("dp", "zero")),
        P(None, ("dp", "zero")),
        P(("dp", "zero"), "tensor"),
        P(("dp", "zero"), "tensor"),
        P(("dp", "zero"), "tensor"),
        P("tensor", ("dp", "zero")),
        P(("dp", "zero"), "tensor"),
        P(("dp", "zero"), "tensor"),
        P("tensor", ("dp", "zero")),
        P(None, ("dp", "zero")),
        P(("dp", "zero"), "tensor"),
        P(("dp", "zero"), "tensor"),
        P(("dp", "zero"), "tensor"),
        P("tensor", ("dp", "zero")),
        P(("dp", "zero"), "tensor"),
        P(("dp", "zero"), "tensor"),
        P("tensor", ("dp", "zero")),
        P(None, ("dp", "zero")),
    )
    return jax.shard_map(
        per_device, mesh=mesh, in_specs=in_specs, out_specs=out_specs, check_vma=False
    )
```

```python
import functools

import jax
import jax.numpy as jnp
from jax import lax
from jax.experimental import pallas as pl
from jax.experimental.pallas import tpu as pltpu
from jax.sharding import PartitionSpec as P

MESH = pl.DeviceIdType.MESH

MODEL_WIDTH = 2304
QUERY_HEADS = 8
HEAD_SIZE = 256
FF = 9216
STEP = 10
W = MODEL_WIDTH


norm_eps = 1e-06
soft_cap = 50.0
rope_base = 10000.0
beta_one = 0.9
beta_two = 0.95
adam_eps = 1e-08
weight_decay = 0.1
gain_rate = 0.7


def rms_forward(value_rows, gain):
    factor = lax.rsqrt(jnp.mean(value_rows * value_rows, axis=-1, keepdims=True) + norm_eps)
    normed = value_rows * factor
    return (normed * gain, normed, factor)


def rms_backward(grad, gain, normed, factor):
    scaled = grad * gain
    inner = jnp.mean(scaled * normed, axis=-1, keepdims=True)
    return (factor * (scaled - normed * inner), jnp.sum(grad * normed, axis=0))


def rope_tables(segment):
    index = jnp.arange(segment.shape[0], dtype=jnp.int32)
    earlier = jnp.concatenate([jnp.full((1,), -1, jnp.int32), segment[:-1]])
    first = lax.cummax(jnp.where(segment != earlier, index, 0), axis=0)
    place = (index - first).astype(jnp.float32)
    inverse = rope_base ** (-jnp.arange(0, HEAD_SIZE, 2, dtype=jnp.float32) / HEAD_SIZE)
    angle = place[:, None] * inverse[None, :]
    return (jnp.cos(angle)[:, None, :], jnp.sin(angle)[:, None, :])


def adam_update(master, mean, square, grad, rate, decay):
    moment = beta_one * mean + (1.0 - beta_one) * grad
    second = beta_two * square + (1.0 - beta_two) * grad * grad
    direction = (
        moment / (1.0 - beta_one**STEP) / (jnp.sqrt(second / (1.0 - beta_two**STEP)) + adam_eps)
    )
    return (moment, second, master - rate * (direction + decay * master))


def remote(src,dst,ss,rs,dev):
    return pltpu.make_async_remote_copy(src_ref=src,dst_ref=dst,send_sem=ss,recv_sem=rs,device_id=dev,device_id_type=MESH)

class Chain:
    def __init__(self, half, ch, P, RE, RM, O, sp, so, ve, vm, vo, lags=(1,2,3,4)):
        self.p = lax.axis_index("tensor"); p=self.p
        self.reg=half//2; self.ch=ch; self.nt=self.reg//ch
        self.P,self.RE,self.RM,self.O=P,RE,RM,O
        self.sp,self.so,self.ve,self.vm,self.vo=sp,so,ve,vm,vo
        self.lags=lags
        self.end = (p==0)|(p==3)
        self.mid = (p==1)|(p==2)
        self.to_mid = {"tensor": jnp.where(p<2, 1, 2)}
        self.to_end = {"tensor": jnp.where(p<2, 0, 3)}
        self.to_oth = {"tensor": jnp.where(p<2, 2, 1)}
        self.own = jnp.where(p<2,0,1); self.oth=1-self.own
    def rows(self, part, t):
        return pl.ds(pl.multiple_of(part*self.reg+t*self.ch,16), self.ch)
    def trow(self,t): return pl.ds(pl.multiple_of(t*self.ch,16), self.ch)
    def r1(self,h,t):
        for part in (0,1):
            r=self.rows(part,t)
            remote(self.P.at[h,r],self.RE.at[h,r],self.sp.at[h,t,part],self.ve.at[h,t,part],self.to_mid).start()
    def r2(self,h,t):
        r=self.rows(self.oth,t)
        remote(self.P.at[h,r],self.RE.at[h,r],self.sp.at[h,t,0],self.ve.at[h,t,self.oth],self.to_end).wait_recv()
        self.P[h,r,:]=self.P[h,r,:]+self.RE[h,r,:]
        remote(self.P.at[h,r],self.RM.at[h,self.trow(t)],self.sp.at[h,t,0],self.vm.at[h,t],self.to_oth).start()
    def r3(self,h,t):
        r=self.rows(self.own,t); q=self.trow(t)
        remote(self.P.at[h,r],self.RE.at[h,r],self.sp.at[h,t,0],self.ve.at[h,t,self.own],self.to_end).wait_recv()
        remote(self.P.at[h,r],self.RM.at[h,q],self.sp.at[h,t,0],self.vm.at[h,t],self.to_oth).wait_recv()
        self.O[h,r,:]=(self.P[h,r,:].astype(jnp.float32)+self.RE[h,r,:].astype(jnp.float32)+self.RM[h,q,:].astype(jnp.float32)).astype(jnp.bfloat16)
        remote(self.O.at[h,r],self.O.at[h,r],self.so.at[h,t,0],self.vo.at[h,t,self.own],self.to_end).start()
        remote(self.O.at[h,r],self.O.at[h,r],self.so.at[h,t,1],self.vo.at[h,t,self.own],self.to_oth).start()
    def b4(self,h,t):
        r=self.rows(self.oth,t)
        c=remote(self.O.at[h,r],self.O.at[h,r],self.so.at[h,t,2],self.vo.at[h,t,self.oth],self.to_end)
        c.wait_recv(); c.start()
    def b5_end(self,h,t):
        for part in (0,1):
            r=self.rows(part,t)
            remote(self.O.at[h,r],self.O.at[h,r],self.so.at[h,t,0],self.vo.at[h,t,part],self.to_mid).wait_recv()
            remote(self.P.at[h,r],self.RE.at[h,r],self.sp.at[h,t,part],self.ve.at[h,t,part],self.to_mid).wait_send()
    def b5_mid(self,h,t):
        r=self.rows(self.own,t)
        remote(self.P.at[h,r],self.RE.at[h,r],self.sp.at[h,t,0],self.ve.at[h,t,0],self.to_oth).wait_send()
        for i in range(3):
            remote(self.O.at[h,r],self.O.at[h,r],self.so.at[h,t,i],self.vo.at[h,t,0],self.to_end).wait_send()
    def tick(self, T, base0, hi0, start, base, hi):
        nt=self.nt
        def at(t0, cond, fns):
            late=t0>=start
            c=jnp.where(late,t0-base,t0-base0)
            ok=(t0>=0)&(c<jnp.where(late,hi,hi0))
            j=c//nt; h=j%2; t=c%nt
            @pl.when(ok&cond)
            def _():
                for f in fns: f(h,t)
        l1,l2,l3,l4=self.lags
        at(T,self.end,[self.r1])
        at(T-l1,self.mid,[self.r2])
        at(T-l2,self.mid,[self.r3])
        at(T-l3,self.mid,[self.b4])
        at(T-l4,self.end,[self.b5_end])
        at(T-l4,self.mid,[self.b5_mid])

def chain_scratch(half,ch):
    nt=half//2//ch
    B=jnp.bfloat16; D=pltpu.SemaphoreType.DMA
    return [pltpu.VMEM((2,half,W),B),pltpu.VMEM((2,half,W),B),pltpu.VMEM((2,half//2,W),B),pltpu.VMEM((2,half,W),B),
            D((2,nt,2)),D((2,nt,3)),D((2,nt,2)),D((2,nt)),D((2,nt,2))]


def coords():
    dp,ze=lax.axis_index("dp"),lax.axis_index("zero")
    x=dp//2; c=dp%2
    return x,c,ze
def sid(x,c,y): return (x*2+c)*2+y
class Plane:
    def __init__(self):
        x,c,y=coords()
        self.x,self.c,self.y=x,c,y
        self.toX={"dp":(1-x)*2+c}; self.toY={"zero":1-y}; self.toC={"dp":x*2+1-c}
        self.lane=[sid(x,c,y),sid(1-x,c,y),sid(x,c,1-y),sid(1-x,c,1-y)]
        d=1-c
        self.other=[sid(x,d,y),sid(1-x,d,y),sid(x,d,1-y),sid(1-x,d,1-y)]
        self.is0=c==0; self.is1=c==1
def plane_signal():
    x,c,y=coords()
    bar=pltpu.get_barrier_semaphore()
    for dev in ({"dp":(1-x)*2+c},{"zero":1-y},{"dp":x*2+1-c}):
        pl.semaphore_signal(bar, inc=1, device_id=dev, device_id_type=MESH)
def plane_barrier():
    plane_signal(); pl.semaphore_wait(pltpu.get_barrier_semaphore(),3)

class Gather:
    def __init__(self, units, ss, rs, ls):
        self.u=units; self.ss,self.rs,self.ls=ss,rs,ls; self.pl=Plane()
    def refs(self,i):
        S,F,r0,rr=self.u[i]; r=pl.ds(r0,rr)
        return S.at[r], (lambda s: F.at[s,r])
    def a(self,i):
        S,F=self.refs(i); q=self.pl; own=q.lane[0]
        remote(S,F(own),self.ss.at[i,0],self.rs.at[i,0],q.toX).start()
        remote(S,F(own),self.ss.at[i,1],self.rs.at[i,1],q.toY).start()
        remote(S,F(own),self.ss.at[i,2],self.rs.at[i,3],q.toC).start()
        pltpu.make_async_copy(S,F(own),self.ls.at[i]).start()
    def b(self,i):
        S,F=self.refs(i); q=self.pl; X,Y=q.lane[1],q.lane[2]
        remote(S,F(X),self.ss.at[i,0],self.rs.at[i,0],q.toX).wait_recv()
        @pl.when(q.is1)
        def _(): remote(F(X),F(X),self.ss.at[i,3],self.rs.at[i,2],q.toY).start()
        remote(F(X),F(X),self.ss.at[i,4],self.rs.at[i,4],q.toC).start()
        remote(S,F(Y),self.ss.at[i,1],self.rs.at[i,1],q.toY).wait_recv()
        @pl.when(q.is0)
        def _(): remote(F(Y),F(Y),self.ss.at[i,3],self.rs.at[i,2],q.toX).start()
        remote(F(Y),F(Y),self.ss.at[i,5],self.rs.at[i,5],q.toC).start()
    def d(self,i):
        S,F=self.refs(i); q=self.pl; D=q.lane[3]
        c=remote(F(D),F(D),self.ss.at[i,6],self.rs.at[i,6],q.toC)
        remote(S,F(D),self.ss.at[i,3],self.rs.at[i,2],q.toX).wait_recv()
        c.start()
    def e(self,i):
        S,F=self.refs(i); q=self.pl
        for j in range(4):
            remote(S,F(q.other[j]),self.ss.at[i,0],self.rs.at[i,3+j],q.toC).wait_recv()
        pltpu.make_async_copy(S,F(q.lane[0]),self.ls.at[i]).wait()
        for j in range(7):
            remote(S,S,self.ss.at[i,j],self.rs.at[i,0],q.toC).wait_send()
    def tick(self,T):
        n=len(self.u)
        if 0<=T<n: self.a(T)
        if 0<=T-1<n: self.b(T-1)
        if 0<=T-2<n: self.d(T-2)
        if 0<=T-3<n: self.e(T-3)
    @property
    def ticks(self): return len(self.u)+3
def gather_sems(n):
    D=pltpu.SemaphoreType.DMA
    return [D((n,7)),D((n,7)),D((n,))]

F32=jnp.float32; BF=jnp.bfloat16
class GatherD(Gather):
    def __init__(self,src,dst,n,lags,ss,rs,ls,base=0):
        self.src,self.dst,self.n,self.lags,self.base=src,dst,n,lags,base
        self.ss,self.rs,self.ls=ss,rs,ls; self.pl=Plane()
    def refs(self,i):
        i=i-self.base
        return self.src(i),(lambda s: self.dst(i,s))
    def tick(self,T):
        lb,ld,le=self.lags
        for lag,f in ((0,self.a),(lb,self.b),(ld,self.d),(le,self.e)):
            i=T-lag
            @pl.when((i>=0)&(i<self.n))
            def _(): f(i+self.base)
def gelu_parts(g):
    k=0.7978845608028654; c=0.044715
    t=jnp.tanh(k*(g+c*g*g*g))
    act=0.5*g*(1.0+t)
    der=0.5*(1.0+t)+0.5*g*(1.0-t*t)*k*(1.0+3.0*c*g*g)
    return act,der
def nt_dot(a,b): return lax.dot_general(a,b,(((1,),(1,)),((),())),preferred_element_type=F32)
def rsq(v): return lax.rsqrt(jnp.mean(v*v,axis=-1,keepdims=True)+1e-6)

def f_kernel(gather,half,ch,lags,grr,qrr,glags,tn,nheads,*refs):
    (x_ref,dy_ref,cos,sin,segc,segr,wq_ref,ga_ref,s_ref,
     at_out,f_out,d_out,n2_out,hid_out,dg_out,du_out,df_out,n1_out,q_out,k_out,v_out,o_out,w_out,g_out,gm_out,
     Wt,BIG,XS,GV,P,RE,RM,O,sp,so,ve,vm,vo,gss,grs,gls,isem,osem)=refs
    C=Chain(half,ch,P,RE,RM,O,sp,so,ve,vm,vo,lags)
    L=lags[-1]; nt=C.nt; ff=Wt.shape[2]; nj=ff//tn; nd=W//tn; total=2*half; HS=256
    qw=nheads*HS; wq=qw+2*HS+qw
    def rows(h): return pl.ds(h*half,half)
    def cp(src,dst,sem): return pltpu.make_async_copy(src,dst,sem)
    n2r=pl.ds(4*half,half); hidr=pl.ds(5*half,half)
    N2=BIG.at[n2r]; HID=BIG.at[hidr]
    def gu(k,h): return pl.ds((k*2+h)*half,half)
    WQ=BIG.at[pl.ds(0,W),pl.ds(0,wq)]
    GA=BIG.at[pl.ds(0,W),pl.ds(wq,128)]
    c0,c1=wq+128,wq+128+HS
    def qpart(hd): return (pl.ds(hd*total,total),pl.ds(c0,HS))
    kpart=(pl.ds(0,total),pl.ds(c1,HS)); vpart=(pl.ds(total,total),pl.ds(c1,HS))
    def opart(h): return (pl.ds(2*total+h*half,half),pl.ds(c0,qw))
    xin=lambda ref,h: cp(ref.at[rows(h)],XS,isem.at[0])
    xin(x_ref,0).start()
    line_signal()
    oc={}
    def out(name,src,dst,i):
        c=cp(src,dst,osem.at[i]); c.start(); oc[name]=c
    def fin(name): oc.pop(name).wait()
    shard=W//8 if gather else 0
    nq=0; st={'q':0,'g':0}
    if gather:
        plane_signal()
        pl.semaphore_wait(pltpu.get_barrier_semaphore(),line_count()+3)
        def al(v): return pl.ds(pl.multiple_of(v,16),qrr)
        per=shard//grr; nq=shard//qrr; ng=s_ref.shape[0]*per
        Gg=GatherD(lambda i: ga_ref,lambda i,s: BIG.at[pl.ds(pl.multiple_of(s*shard,16),shard),pl.ds(wq,128)],1,(0,0,0),gss,grs,gls)
        Gq=GatherD(lambda i: wq_ref.at[al(i*qrr)],lambda i,s: BIG.at[al(s*shard+i*qrr),pl.ds(0,wq)],nq,(1,2,3),gss,grs,gls,1)
        Gt=GatherD(lambda i: s_ref.at[i//per,pl.ds(pl.multiple_of((i%per)*grr,16),grr)],
                   lambda i,s: Wt.at[i//per,pl.ds(pl.multiple_of(s*shard+(i%per)*grr,16),grr)],ng,glags,gss,grs,gls,1+nq)
        def done(k): return (k+1)*per-1+glags[2]+1
        Gg.a(0); Gq.tick(0); Gg.b(0); Gg.d(0); Gq.tick(1); Gg.e(0); st['q']=2
    else:
        pl.semaphore_wait(pltpu.get_barrier_semaphore(),line_count())
        wc=[cp(s_ref.at[k],Wt.at[k],gls.at[k]) for k in range(3)]+[cp(wq_ref,WQ,gls.at[3]),cp(ga_ref,GA,gls.at[4])]
        for c in wc: c.start()
        for c in wc: c.wait()
        def done(k): return 0
    def qg(upto):
        if gather:
            while st['q']<upto: Gq.tick(st['q']); st['q']+=1
    def ag(upto):
        if gather and upto>st['g']:
            lax.fori_loop(st['g'],upto,lambda T,_: (Gt.tick(T),0)[1],0); st['g']=upto
    S={'T':0,'base0':0,'hi0':0,'start':0,'base':0,'hi':0}
    def tick(T,s): C.tick(T,s['base0'],s['hi0'],s['start'],s['base'],s['hi'])
    def top(): return S['base']+S['hi']+L
    def ticks(until,every_g=0):
        s=dict(S); T0,g0=s['T'],st['g']; until=min(until,top())
        if until<=T0: return
        def body(T,_):
            tick(T,s)
            if every_g and gather:
                @pl.when((T-T0)%every_g==0)
                def _(): Gt.tick(g0+(T-T0)//every_g)
            return 0
        lax.fori_loop(T0,until,body,0)
        S['T']=until
        if every_g and gather: st['g']=g0+(until-T0+every_g-1)//every_g
    def finish(c,every_g=0):
        every_g=every_g*16//ch
        base=S['base'] if c>S['hi0'] else S['base0']
        ticks(base+c+L,every_g)
    def ready(c):
        if S['T']>S['base']+S['hi']:
            ticks(S['start']+L)
            S.update(base0=S['base'],hi0=S['hi'],start=S['T'],base=S['T']-S['hi'])
        S['hi']=c
    def units(n,fn,every=0,eg=0):
        s=dict(S); T0,g0=s['T'],st['g']; every=every*ch//16
        def body(i,_):
            fn(i)
            if every:
                @pl.when((i+1)%every==0)
                def _(): tick(T0+i//every,s)
            if eg and gather:
                @pl.when((i+1)%eg==0)
                def _(): Gt.tick(g0+i//eg)
            return 0
        lax.fori_loop(0,n,body,0)
        if eg and gather: st['g']=g0+n//eg
        if every: S['T']=min(T0+n//every,max(top(),T0))
    def wait_w(k):
        while gather and st['g']<done(k):
            ag(st['g']+1); ticks(S['T']+max(1,32//ch))
    nr=32; nn=half//nr
    def rch(i): return pl.ds(pl.multiple_of(i*nr,nr),nr)
    def gain(k): return GV[k:k+1,:]
    def norm0(h):
        def f(i):
            r=rch(i)
            v=XS[r,:].astype(F32)
            P[h,r,:]=(v*rsq(v)*gain(0)).astype(BF)
        return f
    def norm1(h):
        def f(i):
            r=rch(i)
            a=O[h,r,:].astype(F32)
            h1=XS[r,:].astype(F32)+a*rsq(a)*gain(1)
            BIG[pl.ds(pl.multiple_of(4*half+i*nr,nr),nr),:]=(h1*rsq(h1)*gain(2)).astype(BF)
        return f
    def normf(h):
        def f(i):
            r=rch(i)
            v=O[h,r,:].astype(F32); q=rsq(v); z=v*q
            s=XS[r,:].astype(F32)*gain(3)
            BIG[pl.ds(pl.multiple_of(4*half+i*nr,nr),nr),:]=(q*(s-z*jnp.mean(s*z,axis=-1,keepdims=True))).astype(BF)
        return f
    def qkv(h):
        def f(j):
            t=jnp.dot(P[h],BIG[pl.ds(0,W),pl.ds(pl.multiple_of(j*HS,HS),HS)],preferred_element_type=F32)
            return t
        cs=cos[rows(h),:]; sn=sin[rows(h),:]
        def rot(t):
            a,b=t[:,:HS//2],t[:,HS//2:]
            return jnp.concatenate([a*cs-b*sn,b*cs+a*sn],axis=1).astype(BF)
        for hd in range(nheads): BIG[pl.ds(hd*total+h*half,half),pl.ds(c0,HS)]=rot(f(hd))
        BIG[pl.ds(h*half,half),pl.ds(c1,HS)]=rot(f(nheads))
        BIG[pl.ds(total+h*half,half),pl.ds(c1,HS)]=f(nheads+1).astype(BF)
    qb=half//2
    def attend(h):
        nk=(h+1)*half; ks=pl.ds(0,nk)
        def f(i):
            hd=i%nheads; r0=h*half+(i//nheads)*qb
            rr=pl.ds(pl.multiple_of(r0,16),qb)
            q=BIG[pl.ds(pl.multiple_of(hd*total+r0,16),qb),pl.ds(c0,HS)]
            s=nt_dot(q,BIG[pl.ds(0,nk),pl.ds(c1,HS)])*(HS**-0.5)
            cc=50.0*jnp.tanh(s*(1.0/50.0))
            ri=r0+lax.broadcasted_iota(jnp.int32,(qb,nk),0); ci=lax.broadcasted_iota(jnp.int32,(qb,nk),1)
            vis=(ci<=ri)&(segc[rr,:]==segr[:,ks])
            cc=jnp.where(vis,cc,-jnp.inf)
            e=jnp.exp(cc-jnp.max(cc,axis=-1,keepdims=True))
            p=(e/jnp.sum(e,axis=-1,keepdims=True)).astype(BF)
            o=jnp.dot(p,BIG[pl.ds(total,nk),pl.ds(c1,HS)],preferred_element_type=F32).astype(BF)
            BIG[pl.ds(pl.multiple_of(2*total+r0,16),qb),pl.ds(pl.multiple_of(c0+hd*HS,128),HS)]=o
        return f
    def col(j): return pl.ds(pl.multiple_of(j*tn,tn),tn)
    def outp(h):
        def f(j): P[h,:,col(j)]=nt_dot(BIG[opart(h)],BIG[col(j),pl.ds(qw+2*HS,qw)]).astype(BF)
        return f
    def gate(h):
        def f(j): BIG[gu(0,h),col(j)]=jnp.dot(N2[...],Wt[0,:,col(j)],preferred_element_type=F32).astype(BF)
        return f
    def up(h):
        def f(j):
            u=jnp.dot(N2[...],Wt[1,:,col(j)],preferred_element_type=F32)
            g=BIG[gu(0,h),col(j)].astype(F32)
            act,_=gelu_parts(g)
            BIG[gu(1,h),col(j)]=u.astype(BF)
            BIG[hidr,col(j)]=(act*u).astype(BF)
        return f
    def down(h):
        def f(j): P[h,:,col(j)]=nt_dot(HID[...],Wt[2,col(j),:]).astype(BF)
        return f
    def bwd1(h):
        def f(j):
            d=jnp.dot(N2[...],Wt[2,:,col(j)],preferred_element_type=F32)
            g=BIG[gu(0,h),col(j)].astype(F32); u=BIG[gu(1,h),col(j)].astype(F32)
            act,der=gelu_parts(g)
            BIG[gu(0,h),col(j)]=(d*u*der).astype(BF)
            BIG[gu(1,h),col(j)]=(d*act).astype(BF)
        return f
    def bwd2(h):
        def f(j):
            P[h,:,col(j)]=(nt_dot(BIG[gu(0,h),:],Wt[0,col(j),:])+nt_dot(BIG[gu(1,h),:],Wt[1,col(j),:])).astype(BF)
        return f
    GV[...]=jnp.transpose(GA[...].astype(F32))[:8,:]
    xin(x_ref,0).wait()
    units(nn,norm0(0))
    xin(x_ref,1).start()
    out('g',GV,g_out,7)
    out('n1a',P.at[0],n1_out.at[rows(0)],4)
    qg(nq)
    ag(1)
    xin(x_ref,1).wait()
    units(nn,norm0(1))
    xin(x_ref,0).start()
    out('n1b',P.at[1],n1_out.at[rows(1)],5)
    qg(nq+3)
    ag(2)
    out('w',WQ,w_out,6)
    qkv(0)
    ag(3)
    qkv(1)
    out('q0',BIG.at[qpart(0)],q_out.at[0],0)
    if nheads>1: out('q1',BIG.at[qpart(1)],q_out.at[1],1)
    out('k',BIG.at[kpart],k_out,2)
    out('v',BIG.at[vpart],v_out,3)
    ag(4)
    fin('n1a'); fin('n1b')
    units(2*nheads,attend(0),eg=4)
    units(nd,outp(0))
    ready(nt)
    units(2*nheads,attend(1),1,eg=4)
    units(nd,outp(1),3)
    ready(2*nt)
    out('o0',BIG.at[opart(0)],o_out.at[rows(0)],8)
    out('o1',BIG.at[opart(1)],o_out.at[rows(1)],9)
    finish(nt,2)
    out('at0',O.at[0],at_out.at[rows(0)],10)
    xin(x_ref,0).wait()
    for k in ('q0','q1','k','v','o0','o1','w','g'):
        if k in oc: fin(k)
    units(nn,norm1(0),7)
    xin(x_ref,1).start()
    out('n2',N2,n2_out.at[rows(0)],0)
    wait_w(0)
    units(nj,gate(0),3)
    wait_w(1)
    units(nj,up(0),4)
    out('hid',HID,hid_out.at[rows(0)],1)
    wait_w(2)
    fin('at0')
    units(nd,down(0),3)
    ready(3*nt)
    finish(2*nt)
    out('at1',O.at[1],at_out.at[rows(1)],11)
    xin(x_ref,1).wait()
    fin('n2')
    units(nn,norm1(1),7)
    xin(dy_ref,0).start()
    out('n2',N2,n2_out.at[rows(1)],0)
    units(nj,gate(1),3)
    fin('hid')
    units(nj,up(1),4)
    out('hid',HID,hid_out.at[rows(1)],1)
    fin('at1')
    units(nd,down(1),3)
    ready(4*nt)
    finish(3*nt)
    out('f0',O.at[0],f_out.at[rows(0)],10)
    xin(dy_ref,0).wait()
    fin('n2')
    units(nn,normf(0),7)
    xin(dy_ref,1).start()
    out('df',N2,df_out.at[rows(0)],0)
    units(nj,bwd1(0),3)
    out('dg0',BIG.at[gu(0,0)],dg_out.at[rows(0)],2); out('du0',BIG.at[gu(1,0)],du_out.at[rows(0)],3)
    fin('f0')
    units(nd,bwd2(0),2)
    ready(5*nt)
    finish(4*nt)
    out('f1',O.at[1],f_out.at[rows(1)],11)
    xin(dy_ref,1).wait()
    fin('df')
    units(nn,normf(1),7)
    out('df',N2,df_out.at[rows(1)],0)
    units(nj,bwd1(1),3)
    out('dg1',BIG.at[gu(0,1)],dg_out.at[rows(1)],4); out('du1',BIG.at[gu(1,1)],du_out.at[rows(1)],5)
    fin('f1'); fin('df'); fin('hid')
    n2f=pl.ds(2*total,total); dff=pl.ds(0,total); hidf=pl.ds(total,total)
    back=[cp(n2_out,BIG.at[n2f],isem.at[1]),cp(df_out,Wt.at[2,dff],isem.at[2]),cp(hid_out,Wt.at[2,hidf],isem.at[3])]
    for c in back: c.start()
    units(nd,bwd2(1),2)
    ready(6*nt)
    for c in back: c.wait()
    def wgrad(lhs,rhs,k):
        def f(j):
            lt=lhs(col(j))
            for n in range(0,ff,768):
                t=lax.dot_general(lt,rhs(pl.ds(n,768)),(((0,),(0,)),((),())),preferred_element_type=F32)
                Wt[k,col(j),pl.ds(n,768)]=t.astype(BF)
        return f
    units(nd,wgrad(lambda c: Wt[2,dff,c],lambda c: Wt[2,hidf,c],0),1)
    out('gd',Wt.at[0],gm_out.at[2],6)
    units(nd,wgrad(lambda c: BIG[n2f,c],lambda c: BIG[pl.ds(0,total),c],1),1)
    out('gg',Wt.at[1],gm_out.at[0],7)
    finish(5*nt)
    out('d0',O.at[0],d_out.at[rows(0)],10)
    units(nd,wgrad(lambda c: BIG[n2f,c],lambda c: BIG[pl.ds(total,total),c],2),1)
    out('gu',Wt.at[2],gm_out.at[1],8)
    finish(6*nt)
    out('d1',O.at[1],d_out.at[rows(1)],11)
    for k in list(oc): fin(k)

def line_signal():
    te=lax.axis_index("tensor")
    bar=pltpu.get_barrier_semaphore()
    @pl.when(te<3)
    def _(): pl.semaphore_signal(bar, inc=1, device_id={"tensor":te+1}, device_id_type=MESH)
    @pl.when(te>0)
    def _(): pl.semaphore_signal(bar, inc=1, device_id={"tensor":te-1}, device_id_type=MESH)
def line_count():
    te=lax.axis_index("tensor")
    return (te<3).astype(jnp.int32)+(te>0).astype(jnp.int32)

def forward_both(x,dy,cos,sin,seg,qkvo,gains,shards,nheads,gather,cid=9,ch=32,lags=(2,3,4,5),grr=48,qrr=48,glags=(3,4,6),tn=256):
    total=x.shape[0]; half=total//2; D=pltpu.SemaphoreType.DMA; ff=shards.shape[2]; w3=qkvo.shape[1]
    ng=(1+qkvo.shape[0]//qrr+shards.shape[0]*shards.shape[1]//grr) if gather else 5
    sds=jax.ShapeDtypeStruct
    act=sds((total,W),BF); wide=sds((total,ff),BF); hd=sds((total,256),BF)
    A=pl.BlockSpec(memory_space=pl.ANY); V=pl.BlockSpec(memory_space=pltpu.VMEM)
    return pl.pallas_call(functools.partial(f_kernel,gather,half,ch,lags,grr,qrr,glags,tn,nheads),
        out_shape=[act,act,act,act,wide,wide,wide,act,act,sds((nheads,total,256),BF),hd,hd,sds((total,nheads*256),BF),sds((W,w3),BF),sds((8,W),F32)]+[sds((3,W,ff),BF)],
        in_specs=[A,A,V,V,V,V,A,A,A],out_specs=[A]*16,
        scratch_shapes=[pltpu.VMEM((3,W,ff),BF),pltpu.VMEM((6*half,W),BF),pltpu.VMEM((half,W),BF),pltpu.VMEM((8,W),F32)]
            +chain_scratch(half,ch)+gather_sems(ng)+[D((4,)),D((12,))],
        compiler_params=pltpu.CompilerParams(collective_id=cid,has_side_effects=True,vmem_limit_bytes=64*2**20))(
            x,dy,cos,sin,seg.reshape(-1,1),seg.reshape(1,-1),qkvo,gains,shards)
class Ring:
    def __init__(self,src,dst,base,n,rr,cols,bufs,ss,rs,ls,lags=(1,3,5)):
        self.src,self.dst,self.base,self.n,self.rr,self.cols=src,dst,base,n,rr,cols
        self.lags=lags
        self.LB,self.OB,self.CB,self.DB,self.XB,self.YB=bufs
        self.ss,self.rs,self.ls=ss,rs,ls; self.pl=Plane()
    def at(self,ref,*idx): return ref.at[(*idx,pl.ds(0,self.rr),pl.ds(0,self.cols))]
    def get(self,i):
        s=i%self.LB.shape[0]; c=i%self.CB.shape[0]; d=i%self.DB.shape[0]; o=i%2
        lb=lambda j: self.at(self.LB,s,j)
        cb=lambda j: self.at(self.CB,c,j)
        return (lambda k: self.src(i-self.base,k)),lb,cb,self.at(self.DB,d),self.at(self.XB,d),self.at(self.YB,d),self.at(self.OB,o)
    def p1(self,i):
        g,lb,cb,db,xb,yb,ob=self.get(i); q=self.pl
        for j in (3,1,2,0):
            remote(g(q.other[j]),cb(j),self.ss.at[i,j],self.rs.at[i,j],q.toC).start()
            pltpu.make_async_copy(g(q.lane[j]),lb(j),self.ls.at[i,j]).start()
    def p2(self,i):
        g,lb,cb,db,xb,yb,ob=self.get(i); q=self.pl
        for j in (3,1,2,0):
            pltpu.make_async_copy(g(q.lane[j]),lb(j),self.ls.at[i,j]).wait()
            remote(g(q.other[j]),cb(j),self.ss.at[i,j],self.rs.at[i,j],q.toC).wait_recv()
            lb(j)[...]=lb(j)[...]+cb(j)[...]
            if j==3:
                @pl.when(q.is0)
                def _(): remote(lb(3),db,self.ss.at[i,4],self.rs.at[i,4],q.toX).start()
                @pl.when(q.is1)
                def _(): remote(lb(3),db,self.ss.at[i,4],self.rs.at[i,4],q.toY).start()
            if j==1:
                @pl.when(q.is0)
                def _(): remote(lb(1),xb,self.ss.at[i,5],self.rs.at[i,5],q.toX).start()
            if j==2:
                @pl.when(q.is1)
                def _(): remote(lb(2),yb,self.ss.at[i,5],self.rs.at[i,6],q.toY).start()
    def p3(self,i):
        g,lb,cb,db,xb,yb,ob=self.get(i); q=self.pl
        remote(lb(3),db,self.ss.at[i,4],self.rs.at[i,4],q.toX).wait_recv()
        def relay(j,buf,sem,dev):
            lb(j)[...]=lb(j)[...]+db[...]
            remote(lb(j),buf,self.ss.at[i,6],self.rs.at[i,sem],dev).start()
        @pl.when(q.is0)
        def _(): relay(2,yb,6,q.toY)
        @pl.when(q.is1)
        def _(): relay(1,xb,5,q.toX)
    def p4(self,i):
        g,lb,cb,db,xb,yb,ob=self.get(i); q=self.pl
        remote(lb(0),xb,self.ss.at[i,5],self.rs.at[i,5],q.toX).wait_recv()
        remote(lb(0),yb,self.ss.at[i,5],self.rs.at[i,6],q.toY).wait_recv()
        ob[...]=(lb(0)[...].astype(F32)+xb[...].astype(F32)+yb[...].astype(F32)).astype(BF)
        pltpu.make_async_copy(ob,self.dst(i-self.base),self.ls.at[i,4]).start()
        for j in range(7):
            remote(lb(0),xb,self.ss.at[i,j],self.rs.at[i,0],q.toX).wait_send()
    def p5(self,i):
        g,lb,cb,db,xb,yb,ob=self.get(i)
        pltpu.make_async_copy(ob,self.dst(i-self.base),self.ls.at[i,4]).wait()
    def tick(self,T):
        l2,l3,l4=self.lags
        for lag,f in ((0,self.p1),(l2,self.p2),(l3,self.p3),(l4+1,self.p5),(l4,self.p4)):
            i=T-lag
            @pl.when((i>=self.base)&(i<self.base+self.n))
            def _(): f(i)

def b_kernel(scatter,half,ch,lags,rr,tn,nheads,rlags,*refs):
    (at_ref,x_ref,dy_ref,dn_ref,n1_ref,w_ref,q_ref,k_ref,v_ref,o_ref,gv,cos,sin,segc,segr,gm_ref,
     t_out,h_out,acc_out,rm_out,rq_out,
     WQ,N1,X2,X3,Q,K,V,OO,DO,DQ,DK,DV,ACC,LB,OB,CB,DB,XB,YB,ss,rs,ls,
     P,RE,RM,O,sp,so,ve,vm,vo,isem,osem)=refs
    C=Chain(half,ch,P,RE,RM,O,sp,so,ve,vm,vo,lags)
    L=lags[-1]; nt=C.nt; total=2*half; HS=256; qw=nheads*HS; wide=qw+2*HS; nd=W//tn
    def cp(src,dst,i): return pltpu.make_async_copy(src,dst,isem.at[i])
    def rows(h): return pl.ds(h*half,half)
    first=[cp(at_ref.at[rows(1)],P.at[0],0),cp(x_ref.at[rows(1)],N1.at[rows(1)],2),cp(dy_ref.at[rows(1)],X2.at[rows(1)],3),cp(dn_ref.at[rows(1)],X3.at[rows(1)],4)]
    second=[cp(at_ref.at[rows(0)],P.at[1],1),cp(x_ref.at[rows(0)],N1.at[rows(0)],10),cp(dy_ref.at[rows(0)],X2.at[rows(0)],11),cp(dn_ref.at[rows(0)],X3.at[rows(0)],12)]
    later=[cp(w_ref,WQ,5),cp(q_ref,Q,6),cp(k_ref,K,7),cp(v_ref,V,8),cp(o_ref,OO,9)]
    for c in first+later+second: c.start()
    line_signal(); st={'r':0}
    if scatter:
        plane_signal()
        pl.semaphore_wait(pltpu.get_barrier_semaphore(),line_count()+3)
        bufs=(LB,OB,CB,DB,XB,YB); shard=W//8; per=shard//rr; nm=3*per; nq=per
        def gi(k,r): return pl.ds(pl.multiple_of(k*shard+r*rr,16),rr)
        R1=Ring(lambda i,k: gm_ref.at[i//per,gi(k,i%per)],lambda i: rm_out.at[i//per,pl.ds(pl.multiple_of((i%per)*rr,16),rr)],0,nm,rr,W,bufs,ss,rs,ls,rlags)
        R2=Ring(lambda i,k: WQ.at[gi(k,i)],lambda i: rq_out.at[pl.ds(pl.multiple_of(i*rr,16),rr)],nm,nq,rr,wide+qw,bufs,ss,rs,ls,rlags)
    else:
        pl.semaphore_wait(pltpu.get_barrier_semaphore(),line_count())
    def rg(n):
        for _ in range(n):
            if scatter: R1.tick(st['r'])
            st['r']+=1
    S={'T':0,'base0':0,'hi0':0,'start':0,'base':0,'hi':0}
    def tick(T,s): C.tick(T,s['base0'],s['hi0'],s['start'],s['base'],s['hi'])
    def top(): return S['base']+S['hi']+L
    def ready(c):
        if S['T']>S['base']+S['hi']:
            loop(S['start']+L-S['T'],1)
            S.update(base0=S['base'],hi0=S['hi'],start=S['T'],base=S['T']-S['hi'])
        S['hi']=c
    def units(n,fn,every=0,er=0):
        s=dict(S); T0,r0=s['T'],st['r']; every=every*ch//16; er=er*rr//48
        def body(i,_):
            fn(i)
            if every:
                @pl.when((i+1)%every==0)
                def _(): tick(T0+i//every,s)
            if er and scatter:
                @pl.when((i+1)%er==0)
                def _(): R1.tick(r0+i//er)
            return 0
        lax.fori_loop(0,n,body,0)
        if er: st['r']=r0+n//er
        if every: S['T']=min(T0+n//every,max(top(),T0))
    def loop(n,every,er=0,both=False):
        s=dict(S); T0=s['T']
        if n>0: lax.fori_loop(T0,T0+n,lambda t,_: (tick(t,s),0)[1],0); S['T']=T0+n
    rg(2 if rr==48 else 1)
    for c in first: c.wait()
    nr=16; nh=half//nr
    ACC[...]=jnp.zeros_like(ACC)
    def back(h):
        def f(i):
            r=pl.ds(pl.multiple_of(i*nr,nr),nr); rf=pl.ds(pl.multiple_of(h*half+i*nr,nr),nr)
            a=P[1-h,r,:].astype(F32); q1=rsq(a); z2=a*q1
            h1=N1[rf,:].astype(F32)+z2*gv[1:2,:]; q2=rsq(h1); z3=h1*q2
            d=X3[rf,:].astype(F32); s=d*gv[2:3,:]
            dh=X2[rf,:].astype(F32)+q2*(s-z3*jnp.mean(s*z3,axis=-1,keepdims=True))
            s2=dh*gv[1:2,:]
            X2[rf,:]=(q1*(s2-z2*jnp.mean(s2*z2,axis=-1,keepdims=True))).astype(BF)
            X3[rf,:]=dh.astype(BF)
            u=dh*z2; w=d*z3
            ACC[0]+=u[:8]+u[8:]; ACC[1]+=w[:8]+w[8:]
        return f
    def col(j): return pl.ds(pl.multiple_of(j*tn,tn),tn)
    def tn_dot(a,b): return lax.dot_general(a,b,(((0,),(0,)),((),())),preferred_element_type=F32)
    def dout(h):
        for c in range(nheads):
            DO[rows(h),pl.ds(c*HS,HS)]=jnp.dot(X2[rows(h),:],WQ[:,pl.ds(wide+c*HS,HS)],preferred_element_type=F32).astype(BF)
    def gout(j): WQ[col(j),pl.ds(wide,qw)]=tn_dot(X2[:,col(j)],OO[...]).astype(BF)
    qb=half//2; sc=HS**-0.5
    def unrot(t,rr_):
        a,b=t[:,:HS//2],t[:,HS//2:]; cs=cos[rr_,:]; sn=sin[rr_,:]
        return jnp.concatenate([a*cs+b*sn,b*cs-a*sn],axis=1)
    def attend(h):
        nk=(h+1)*half; ks=pl.ds(0,nk)
        def f(i):
            hd=i%nheads; r0=h*half+(i//nheads)*qb; rq=pl.ds(pl.multiple_of(r0,16),qb); hc_=pl.ds(pl.multiple_of(hd*HS,HS),HS)
            q=Q[hd,rq,:]; do=DO[rq,hc_]
            t=jnp.tanh(nt_dot(q,K[ks,:])*(sc/50.0))
            ri=r0+lax.broadcasted_iota(jnp.int32,(qb,nk),0); ci=lax.broadcasted_iota(jnp.int32,(qb,nk),1)
            vis=(ci<=ri)&(segc[rq,:]==segr[:,ks])
            cc=jnp.where(vis,50.0*t,-jnp.inf)
            e=jnp.exp(cc-jnp.max(cc,axis=-1,keepdims=True))
            p=e/jnp.sum(e,axis=-1,keepdims=True)
            dp=nt_dot(do,V[ks,:])
            inner=jnp.sum(p*dp,axis=-1,keepdims=True)
            ds=(p*(dp-inner)*(1.0-t*t)).astype(BF)
            DQ[rq,hc_]=unrot(jnp.dot(ds,K[ks,:],preferred_element_type=F32)*sc,rq).astype(BF)
            DK[ks,:]+=tn_dot(ds,q)
            DV[ks,:]+=tn_dot(p.astype(BF),do)
        return f
    def keys(h):
        DQ[rows(h),pl.ds(qw,HS)]=unrot(DK[rows(h),:]*sc,rows(h)).astype(BF)
        DQ[rows(h),pl.ds(qw+HS,HS)]=DV[rows(h),:].astype(BF)
    def dn1(h):
        def f(j): P[1-h,:,col(j)]=nt_dot(DQ[rows(h),:],WQ[col(j),pl.ds(0,wide)]).astype(BF)
        return f
    def gqkv(j): WQ[col(j),pl.ds(0,wide)]=tn_dot(N1[:,col(j)],DQ[...]).astype(BF)
    DK[...]=jnp.zeros_like(DK); DV[...]=jnp.zeros_like(DV)
    units(nh,back(1),0,28)
    for c in later: c.wait()
    dout(1)
    units(2*nheads,attend(1),0,2)
    keys(1)
    units(nd,dn1(1),0,9)
    for c in second: c.wait()
    ready(nt)
    units(nh,back(0),7,14)
    n1c=cp(n1_ref,N1,2); n1c.start()
    hc=cp(X3,h_out,3); hc.start()
    ac=cp(ACC,acc_out,4); ac.start()
    dout(0)
    units(nd,gout,3,9)
    units(2*nheads,attend(0),1,2)
    keys(0)
    units(nd,dn1(0),3)
    ready(2*nt)
    n1c.wait()
    units(nd,gqkv,1,2)
    outs=[pltpu.make_async_copy(O.at[h],t_out.at[rows(1-h)],osem.at[h]) for h in (0,1)]
    rest=top()-S['T']
    if scatter:
        q=max(1,2*16*rr//(48*ch)); s=dict(S); T0=S['T']; r0=st['r']
        R2.base=max(nm,r0); last=R2.base+nq+R1.lags[2]+1
        k1=max(0,min(-(-rest//q),R2.base-r0)); k2=max(0,-(-(rest-q*k1)//q))
        def both(two):
            def body(i,_):
                R1.tick(r0+i)
                if two: R2.tick(r0+i)
                for z in range(q): tick(T0+q*i+z,s)
                return 0
            return body
        if k1: lax.fori_loop(0,k1,both(False),0)
        if k2: lax.fori_loop(k1,k1+k2,both(True),0)
        r0+=k1+k2
        for c in outs: c.start()
        def body3(i,_):
            R1.tick(i); R2.tick(i); return 0
        lax.fori_loop(r0,last,body3,0)
    else:
        loop(rest,1)
        for c in outs: c.start()
        wc=cp(WQ,rq_out,5); wc.start(); wc.wait()
    for c in outs+[hc,ac]: c.wait()

def backward_both(at,x,dy,dn,n1,w,q,k,v,o,gv,cos,sin,seg,gm,scatter,cid=10,ch=32,lags=(2,3,4,5),rr=48,tn=256,ring=(6,6,14),rlags=(1,3,5)):
    total=x.shape[0]; half=total//2; D=pltpu.SemaphoreType.DMA; sds=jax.ShapeDtypeStruct; nheads=q.shape[0]
    A=pl.BlockSpec(memory_space=pl.ANY); V=pl.BlockSpec(memory_space=pltpu.VMEM); M=pltpu.VMEM
    qw=nheads*256; wide=qw+512; w3=w.shape[1]; act=sds((total,W),BF)
    if scatter: outs=[sds((3,W//8,W),BF),sds((W//8,w3),BF)]; nu=4*(W//8//rr)+8
    else: outs=[sds((8,128),BF),sds((W,w3),BF)]; nu=1; ring=(1,1,1); rr=16
    nl,nc,nx=ring
    return pl.pallas_call(functools.partial(b_kernel,scatter,half,ch,lags,rr,tn,nheads,rlags),
        out_shape=[act,act,sds((2,8,W),F32)]+outs,
        in_specs=[A]*10+[V]*5+[A],out_specs=[A]*5,
        scratch_shapes=[M((W,w3),BF),M((total,W),BF),M((total,W),BF),M((total,W),BF),M((nheads,total,256),BF),M((total,256),BF),M((total,256),BF),
            M((total,qw),BF),M((total,qw),BF),M((total,wide),BF),M((total,256),F32),M((total,256),F32),M((2,8,W),F32),
            M((nl,4,rr,W),BF),M((2,rr,W),BF),M((nc,4,rr,W),BF),M((nx,rr,W),BF),M((nx,rr,W),BF),M((nx,rr,W),BF),D((nu,7)),D((nu,7)),D((nu,5))]
            +chain_scratch(half,ch)+[D((13,)),D((2,))],
        compiler_params=pltpu.CompilerParams(collective_id=cid,has_side_effects=True,vmem_limit_bytes=64*2**20))(
            at,x,dy,dn,n1,w,q,k,v,o,gv,cos,sin,seg.reshape(-1,1),seg.reshape(1,-1),gm)

def small_plane():
    return (lax.axis_size("dp"), lax.axis_size("zero")) == (4, 2)


def sum_own_columns(part):
    if not small_plane():
        low = part.astype(jnp.bfloat16)
        return lax.psum_scatter(low, ("dp", "zero"), scatter_dimension=1, tiled=True)
    for axis, pairs in (
        ("dp", [(0, 1), (1, 0), (2, 3), (3, 2)]),
        ("dp", [(0, 2), (2, 0), (1, 3), (3, 1)]),
        ("zero", [(0, 1), (1, 0)]),
    ):
        part = part + lax.ppermute(part, axis, pairs)
    own = lax.axis_index("dp") * 2 + lax.axis_index("zero")
    width = part.shape[1] // 8
    return lax.dynamic_slice_in_dim(part, own * width, width, axis=1)


def per_device(
    inputs,
    cotangent,
    segment,
    query_weight,
    key_weight,
    value_weight,
    out_weight,
    gate_weight,
    up_weight,
    down_weight,
    norm_gains,
    query_mean,
    key_mean,
    value_mean,
    out_mean,
    gate_mean,
    up_mean,
    down_mean,
    gains_mean,
    query_square,
    key_square,
    value_square,
    out_square,
    gate_square,
    up_square,
    down_square,
    gains_square,
):
    qkvo_low = jnp.concatenate(
        [query_weight, key_weight, value_weight, out_weight.T], axis=1
    ).astype(jnp.bfloat16)
    mlp_shards = jnp.stack([gate_weight, up_weight, down_weight.T]).astype(jnp.bfloat16)
    gains_low = jnp.pad(norm_gains.T.astype(jnp.bfloat16), ((0, 0), (0, 124)))
    if not small_plane():
        both = ("dp", "zero")
        qkvo_low = lax.all_gather(qkvo_low, both, axis=0, tiled=True)
        gains_low = lax.all_gather(gains_low, both, axis=0, tiled=True)
        mlp_shards = lax.all_gather(mlp_shards, both, axis=1, tiled=True)
    heads_q = query_weight.shape[1]
    heads_k = key_weight.shape[1]
    wide = heads_q + 2 * heads_k
    token_rows = inputs.shape[0]
    cosine, sine = rope_tables(segment)
    (
        attn_total,
        mlp_total,
        normed_grad,
        unused_mlp_in,
        unused_hidden,
        unused_gate_dlow,
        unused_up_dlow,
        unused_mlp_low,
        attn_in,
        rotated_queries,
        rotated_keys,
        value_low,
        attention_output,
        qkvo_mat,
        gains_val,
        mlp_grads,
    ) = forward_both(
        inputs,
        cotangent,
        cosine[:, 0],
        sine[:, 0],
        segment,
        qkvo_low,
        gains_low,
        mlp_shards,
        heads_q // HEAD_SIZE,
        small_plane(),
    )
    first_grad, middle_grad, sums, mlp_red, qkvo_red = backward_both(
        attn_total,
        inputs,
        cotangent,
        normed_grad,
        attn_in,
        qkvo_mat,
        rotated_queries,
        rotated_keys,
        value_low,
        attention_output,
        gains_val,
        cosine[:, 0],
        sine[:, 0],
        segment,
        mlp_grads,
        small_plane(),
    )
    if not small_plane():
        mlp_red = lax.psum_scatter(mlp_grads, both, scatter_dimension=1, tiled=True)
        qkvo_red = lax.psum_scatter(qkvo_red, both, scatter_dimension=0, tiled=True)
    resid_in = inputs.astype(jnp.float32)
    out_grad = cotangent.astype(jnp.float32)
    unused, unit_one, factor_one = rms_forward(resid_in, gains_val[0])
    post_attn, unused, unused = rms_forward(attn_total.astype(jnp.float32), gains_val[1])
    post_mlp, unit_four, unused = rms_forward(mlp_total.astype(jnp.float32), gains_val[3])
    block_out = (resid_in + post_attn + post_mlp).astype(jnp.bfloat16)
    gain_four = jnp.sum(out_grad * unit_four, axis=0)
    gain_two, gain_three = jnp.sum(sums, axis=1)
    input_part, gain_one = rms_backward(
        first_grad.astype(jnp.float32), gains_val[0], unit_one, factor_one
    )
    input_grad = middle_grad.astype(jnp.float32) + input_part
    gains_grad = jnp.stack([gain_one, gain_two, gain_three, gain_four])
    gains_red = sum_own_columns(gains_grad)
    down_red, out_red = lax.optimization_barrier((mlp_red[2].T, qkvo_red[:, wide:].T))
    reduced = [
        part.astype(jnp.float32)
        for part in (
            qkvo_red[:, :heads_q],
            qkvo_red[:, heads_q : heads_q + heads_k],
            qkvo_red[:, heads_q + heads_k : wide],
            out_red,
            mlp_red[0],
            mlp_red[1],
            down_red,
            gains_red,
        )
    ]
    masters = (
        query_weight,
        key_weight,
        value_weight,
        out_weight,
        gate_weight,
        up_weight,
        down_weight,
        norm_gains,
    )
    means = (query_mean, key_mean, value_mean, out_mean, gate_mean, up_mean, down_mean, gains_mean)
    squares = (
        query_square,
        key_square,
        value_square,
        out_square,
        gate_square,
        up_square,
        down_square,
        gains_square,
    )
    rates = (
        MODEL_WIDTH ** (-0.5),
        MODEL_WIDTH ** (-0.5),
        MODEL_WIDTH ** (-0.5),
        (QUERY_HEADS * HEAD_SIZE) ** (-0.5),
        MODEL_WIDTH ** (-0.5),
        MODEL_WIDTH ** (-0.5),
        FF ** (-0.5),
        gain_rate,
    )
    decays = (weight_decay,) * 7 + (0.0,)
    moments = []
    seconds = []
    updated = []
    for index in range(8):
        moment, second, master = adam_update(
            masters[index],
            means[index],
            squares[index],
            reduced[index],
            rates[index],
            decays[index],
        )
        moments.append(moment)
        seconds.append(second)
        updated.append(master)
    return (block_out, input_grad, *moments, *seconds, *updated)


def solution(mesh):
    in_specs = (
        P(("dp", "zero"), None),
        P(("dp", "zero"), None),
        P(("dp", "zero")),
        P(("dp", "zero"), "tensor"),
        P(("dp", "zero"), "tensor"),
        P(("dp", "zero"), "tensor"),
        P("tensor", ("dp", "zero")),
        P(("dp", "zero"), "tensor"),
        P(("dp", "zero"), "tensor"),
        P("tensor", ("dp", "zero")),
        P(None, ("dp", "zero")),
        P(("dp", "zero"), "tensor"),
        P(("dp", "zero"), "tensor"),
        P(("dp", "zero"), "tensor"),
        P("tensor", ("dp", "zero")),
        P(("dp", "zero"), "tensor"),
        P(("dp", "zero"), "tensor"),
        P("tensor", ("dp", "zero")),
        P(None, ("dp", "zero")),
        P(("dp", "zero"), "tensor"),
        P(("dp", "zero"), "tensor"),
        P(("dp", "zero"), "tensor"),
        P("tensor", ("dp", "zero")),
        P(("dp", "zero"), "tensor"),
        P(("dp", "zero"), "tensor"),
        P("tensor", ("dp", "zero")),
        P(None, ("dp", "zero")),
    )
    out_specs = (
        P(("dp", "zero"), None),
        P(("dp", "zero"), None),
        P(("dp", "zero"), "tensor"),
        P(("dp", "zero"), "tensor"),
        P(("dp", "zero"), "tensor"),
        P("tensor", ("dp", "zero")),
        P(("dp", "zero"), "tensor"),
        P(("dp", "zero"), "tensor"),
        P("tensor", ("dp", "zero")),
        P(None, ("dp", "zero")),
        P(("dp", "zero"), "tensor"),
        P(("dp", "zero"), "tensor"),
        P(("dp", "zero"), "tensor"),
        P("tensor", ("dp", "zero")),
        P(("dp", "zero"), "tensor"),
        P(("dp", "zero"), "tensor"),
        P("tensor", ("dp", "zero")),
        P(None, ("dp", "zero")),
        P(("dp", "zero"), "tensor"),
        P(("dp", "zero"), "tensor"),
        P(("dp", "zero"), "tensor"),
        P("tensor", ("dp", "zero")),
        P(("dp", "zero"), "tensor"),
        P(("dp", "zero"), "tensor"),
        P("tensor", ("dp", "zero")),
        P(None, ("dp", "zero")),
    )
    return jax.shard_map(
        per_device, mesh=mesh, in_specs=in_specs, out_specs=out_specs, check_vma=False
    )
```

```python
import functools

import jax
import jax.numpy as jnp
from jax import lax
from jax.experimental import pallas as pl
from jax.experimental.pallas import tpu as pltpu
from jax.sharding import PartitionSpec as P

MESH = pl.DeviceIdType.MESH

MODEL_WIDTH = 2304
QUERY_HEADS = 8
HEAD_SIZE = 256
FF = 9216
STEP = 10
W = MODEL_WIDTH


norm_eps = 1e-06
soft_cap = 50.0
rope_base = 10000.0
beta_one = 0.9
beta_two = 0.95
adam_eps = 1e-08
weight_decay = 0.1
gain_rate = 0.7


def rms_forward(value_rows, gain):
    factor = lax.rsqrt(jnp.mean(value_rows * value_rows, axis=-1, keepdims=True) + norm_eps)
    normed = value_rows * factor
    return (normed * gain, normed, factor)


def rope_tables(segment):
    index = jnp.arange(segment.shape[0], dtype=jnp.int32)
    first = jnp.sum((segment[None, :] < segment[:, None]).astype(jnp.int32), axis=1)
    place = (index - first).astype(jnp.float32)
    inverse = rope_base ** (-jnp.arange(0, HEAD_SIZE, 2, dtype=jnp.float32) / HEAD_SIZE)
    angle = place[:, None] * inverse[None, :]
    return (jnp.cos(angle)[:, None, :], jnp.sin(angle)[:, None, :])


def adam_update(master, mean, square, grad, rate, decay):
    moment = beta_one * mean + (1.0 - beta_one) * grad
    second = beta_two * square + (1.0 - beta_two) * grad * grad
    direction = (
        moment / (1.0 - beta_one**STEP) / (jnp.sqrt(second / (1.0 - beta_two**STEP)) + adam_eps)
    )
    return (moment, second, master - rate * (direction + decay * master))


def remote(src,dst,ss,rs,dev):
    return pltpu.make_async_remote_copy(src_ref=src,dst_ref=dst,send_sem=ss,recv_sem=rs,device_id=dev,device_id_type=MESH)

class Chain:
    def __init__(self, half, ch, P, RE, RM, O, sp, so, ve, vm, vo, lags=(1,2,3,4)):
        self.p = lax.axis_index("tensor"); p=self.p
        self.reg=half//2; self.ch=ch; self.nt=self.reg//ch
        self.P,self.RE,self.RM,self.O=P,RE,RM,O
        self.sp,self.so,self.ve,self.vm,self.vo=sp,so,ve,vm,vo
        self.lags=lags
        self.end = (p==0)|(p==3)
        self.mid = (p==1)|(p==2)
        self.to_mid = {"tensor": jnp.where(p<2, 1, 2)}
        self.to_end = {"tensor": jnp.where(p<2, 0, 3)}
        self.to_oth = {"tensor": jnp.where(p<2, 2, 1)}
        self.own = jnp.where(p<2,0,1); self.oth=1-self.own
    def rows(self, part, t):
        return pl.ds(pl.multiple_of(part*self.reg+t*self.ch,16), self.ch)
    def trow(self,t): return pl.ds(pl.multiple_of(t*self.ch,16), self.ch)
    def r1(self,h,t):
        for part in (0,1):
            r=self.rows(part,t)
            remote(self.P.at[h,r],self.RE.at[h,r],self.sp.at[h,t,part],self.ve.at[h,t,part],self.to_mid).start()
    def r2(self,h,t):
        r=self.rows(self.oth,t)
        remote(self.P.at[h,r],self.RE.at[h,r],self.sp.at[h,t,0],self.ve.at[h,t,self.oth],self.to_end).wait_recv()
        self.P[h,r,:]=self.P[h,r,:]+self.RE[h,r,:]
        remote(self.P.at[h,r],self.RM.at[h,self.trow(t)],self.sp.at[h,t,0],self.vm.at[h,t],self.to_oth).start()
    def r3(self,h,t):
        r=self.rows(self.own,t); q=self.trow(t)
        remote(self.P.at[h,r],self.RE.at[h,r],self.sp.at[h,t,0],self.ve.at[h,t,self.own],self.to_end).wait_recv()
        remote(self.P.at[h,r],self.RM.at[h,q],self.sp.at[h,t,0],self.vm.at[h,t],self.to_oth).wait_recv()
        self.O[h,r,:]=(self.P[h,r,:].astype(jnp.float32)+self.RE[h,r,:].astype(jnp.float32)+self.RM[h,q,:].astype(jnp.float32)).astype(jnp.bfloat16)
        remote(self.O.at[h,r],self.O.at[h,r],self.so.at[h,t,0],self.vo.at[h,t,self.own],self.to_end).start()
        remote(self.O.at[h,r],self.O.at[h,r],self.so.at[h,t,1],self.vo.at[h,t,self.own],self.to_oth).start()
    def b4(self,h,t):
        r=self.rows(self.oth,t)
        c=remote(self.O.at[h,r],self.O.at[h,r],self.so.at[h,t,2],self.vo.at[h,t,self.oth],self.to_end)
        c.wait_recv(); c.start()
    def b5_end(self,h,t):
        for part in (0,1):
            r=self.rows(part,t)
            remote(self.O.at[h,r],self.O.at[h,r],self.so.at[h,t,0],self.vo.at[h,t,part],self.to_mid).wait_recv()
            remote(self.P.at[h,r],self.RE.at[h,r],self.sp.at[h,t,part],self.ve.at[h,t,part],self.to_mid).wait_send()
    def b5_mid(self,h,t):
        r=self.rows(self.own,t)
        remote(self.P.at[h,r],self.RE.at[h,r],self.sp.at[h,t,0],self.ve.at[h,t,0],self.to_oth).wait_send()
        for i in range(3):
            remote(self.O.at[h,r],self.O.at[h,r],self.so.at[h,t,i],self.vo.at[h,t,0],self.to_end).wait_send()
    def tick(self, T, base0, hi0, start, base, hi):
        nt=self.nt
        def at(t0, cond, fns):
            late=t0>=start
            c=jnp.where(late,t0-base,t0-base0)
            ok=(t0>=0)&(c<jnp.where(late,hi,hi0))
            j=c//nt; h=j%2; t=c%nt
            @pl.when(ok&cond)
            def _():
                for f in fns: f(h,t)
        l1,l2,l3,l4=self.lags
        at(T,self.end,[self.r1])
        at(T-l1,self.mid,[self.r2])
        at(T-l2,self.mid,[self.r3])
        at(T-l3,self.mid,[self.b4])
        at(T-l4,self.end,[self.b5_end])
        at(T-l4,self.mid,[self.b5_mid])

def chain_scratch(half,ch):
    nt=half//2//ch
    B=jnp.bfloat16; D=pltpu.SemaphoreType.DMA
    return [pltpu.VMEM((2,half,W),B),pltpu.VMEM((2,half,W),B),pltpu.VMEM((2,half//2,W),B),pltpu.VMEM((2,half,W),B),
            D((2,nt,2)),D((2,nt,3)),D((2,nt,2)),D((2,nt)),D((2,nt,2))]


def coords():
    dp,ze=lax.axis_index("dp"),lax.axis_index("zero")
    x=dp//2; c=dp%2
    return x,c,ze
def sid(x,c,y): return (x*2+c)*2+y
class Plane:
    def __init__(self):
        x,c,y=coords()
        self.x,self.c,self.y=x,c,y
        self.toX={"dp":(1-x)*2+c}; self.toY={"zero":1-y}; self.toC={"dp":x*2+1-c}
        self.lane=[sid(x,c,y),sid(1-x,c,y),sid(x,c,1-y),sid(1-x,c,1-y)]
        d=1-c
        self.other=[sid(x,d,y),sid(1-x,d,y),sid(x,d,1-y),sid(1-x,d,1-y)]
        self.is0=c==0; self.is1=c==1
def plane_signal():
    x,c,y=coords()
    bar=pltpu.get_barrier_semaphore()
    for dev in ({"dp":(1-x)*2+c},{"zero":1-y},{"dp":x*2+1-c}):
        pl.semaphore_signal(bar, inc=1, device_id=dev, device_id_type=MESH)
def plane_barrier():
    plane_signal(); pl.semaphore_wait(pltpu.get_barrier_semaphore(),3)

class Gather:
    def __init__(self, units, ss, rs, ls):
        self.u=units; self.ss,self.rs,self.ls=ss,rs,ls; self.pl=Plane()
    def refs(self,i):
        S,F,r0,rr=self.u[i]; r=pl.ds(r0,rr)
        return S.at[r], (lambda s: F.at[s,r])
    def a(self,i):
        S,F=self.refs(i); q=self.pl; own=q.lane[0]
        remote(S,F(own),self.ss.at[i,0],self.rs.at[i,0],q.toX).start()
        remote(S,F(own),self.ss.at[i,1],self.rs.at[i,1],q.toY).start()
        remote(S,F(own),self.ss.at[i,2],self.rs.at[i,3],q.toC).start()
        pltpu.make_async_copy(S,F(own),self.ls.at[i]).start()
    def b(self,i):
        S,F=self.refs(i); q=self.pl; X,Y=q.lane[1],q.lane[2]
        remote(S,F(X),self.ss.at[i,0],self.rs.at[i,0],q.toX).wait_recv()
        @pl.when(q.is1)
        def _(): remote(F(X),F(X),self.ss.at[i,3],self.rs.at[i,2],q.toY).start()
        remote(F(X),F(X),self.ss.at[i,4],self.rs.at[i,4],q.toC).start()
        remote(S,F(Y),self.ss.at[i,1],self.rs.at[i,1],q.toY).wait_recv()
        @pl.when(q.is0)
        def _(): remote(F(Y),F(Y),self.ss.at[i,3],self.rs.at[i,2],q.toX).start()
        remote(F(Y),F(Y),self.ss.at[i,5],self.rs.at[i,5],q.toC).start()
    def d(self,i):
        S,F=self.refs(i); q=self.pl; D=q.lane[3]
        c=remote(F(D),F(D),self.ss.at[i,6],self.rs.at[i,6],q.toC)
        remote(S,F(D),self.ss.at[i,3],self.rs.at[i,2],q.toX).wait_recv()
        c.start()
    def e(self,i):
        S,F=self.refs(i); q=self.pl
        for j in range(4):
            remote(S,F(q.other[j]),self.ss.at[i,0],self.rs.at[i,3+j],q.toC).wait_recv()
        pltpu.make_async_copy(S,F(q.lane[0]),self.ls.at[i]).wait()
        for j in range(7):
            remote(S,S,self.ss.at[i,j],self.rs.at[i,0],q.toC).wait_send()
    def tick(self,T):
        n=len(self.u)
        if 0<=T<n: self.a(T)
        if 0<=T-1<n: self.b(T-1)
        if 0<=T-2<n: self.d(T-2)
        if 0<=T-3<n: self.e(T-3)
    @property
    def ticks(self): return len(self.u)+3
def gather_sems(n):
    D=pltpu.SemaphoreType.DMA
    return [D((n,7)),D((n,7)),D((n,))]

F32=jnp.float32; BF=jnp.bfloat16
class GatherD(Gather):
    def __init__(self,src,dst,n,lags,ss,rs,ls,base=0):
        self.src,self.dst,self.n,self.lags,self.base=src,dst,n,lags,base
        self.ss,self.rs,self.ls=ss,rs,ls; self.pl=Plane()
    def refs(self,i):
        i=i-self.base
        return self.src(i),(lambda s: self.dst(i,s))
    def tick(self,T):
        lb,ld,le=self.lags
        for lag,f in ((0,self.a),(lb,self.b),(ld,self.d),(le,self.e)):
            i=T-lag
            @pl.when((i>=0)&(i<self.n))
            def _(): f(i+self.base)
def gelu_parts(g):
    k=0.7978845608028654; c=0.044715
    t=jnp.tanh(k*(g+c*g*g*g))
    act=0.5*g*(1.0+t)
    der=0.5*(1.0+t)+0.5*g*(1.0-t*t)*k*(1.0+3.0*c*g*g)
    return act,der
def nt_dot(a,b): return lax.dot_general(a,b,(((1,),(1,)),((),())),preferred_element_type=F32)
def rsq(v): return lax.rsqrt(jnp.mean(v*v,axis=-1,keepdims=True)+1e-6)

def f_kernel(gather,half,ch,lags,grr,qrr,glags,tn,nheads,*refs):
    (x_ref,dy_ref,cos,sin,segc,segr,wq_ref,ga_ref,s_ref,
     at_out,f_out,d_out,n2_out,hid_out,dg_out,du_out,df_out,n1_out,q_out,k_out,v_out,o_out,w_out,g_out,gm_out,
     Wt,BIG,XS,GV,P,RE,RM,O,sp,so,ve,vm,vo,gss,grs,gls,isem,osem)=refs
    C=Chain(half,ch,P,RE,RM,O,sp,so,ve,vm,vo,lags)
    L=lags[-1]; nt=C.nt; ff=Wt.shape[2]; nj=ff//tn; nd=W//tn; total=2*half; HS=256
    qw=nheads*HS; wq=qw+2*HS+qw
    def rows(h): return pl.ds(h*half,half)
    def cp(src,dst,sem): return pltpu.make_async_copy(src,dst,sem)
    n2r=pl.ds(4*half,half); hidr=pl.ds(5*half,half)
    N2=BIG.at[n2r]; HID=BIG.at[hidr]
    def gu(k,h): return pl.ds((k*2+h)*half,half)
    WQ=BIG.at[pl.ds(0,W),pl.ds(0,wq)]
    GA=BIG.at[pl.ds(0,W),pl.ds(wq,128)]
    c0,c1=wq+128,wq+128+HS
    def qpart(hd): return (pl.ds(hd*total,total),pl.ds(c0,HS))
    kpart=(pl.ds(0,total),pl.ds(c1,HS)); vpart=(pl.ds(total,total),pl.ds(c1,HS))
    def opart(h): return (pl.ds(2*total+h*half,half),pl.ds(c0,qw))
    xin=lambda ref,h: cp(ref.at[rows(h)],XS,isem.at[0])
    xin(x_ref,0).start()
    line_signal()
    oc={}
    def out(name,src,dst,i):
        c=cp(src,dst,osem.at[i]); c.start(); oc[name]=c
    def fin(name): oc.pop(name).wait()
    shard=W//8 if gather else 0
    nq=0; st={'q':0,'g':0}
    if gather:
        plane_signal()
        pl.semaphore_wait(pltpu.get_barrier_semaphore(),line_count()+3)
        def al(v): return pl.ds(pl.multiple_of(v,16),qrr)
        per=shard//grr; nq=shard//qrr; ng=s_ref.shape[0]*per
        Gg=GatherD(lambda i: ga_ref,lambda i,s: BIG.at[pl.ds(pl.multiple_of(s*shard,16),shard),pl.ds(wq,128)],1,(0,0,0),gss,grs,gls)
        Gq=GatherD(lambda i: wq_ref.at[al(i*qrr)],lambda i,s: BIG.at[al(s*shard+i*qrr),pl.ds(0,wq)],nq,(1,2,3),gss,grs,gls,1)
        Gt=GatherD(lambda i: s_ref.at[i//per,pl.ds(pl.multiple_of((i%per)*grr,16),grr)],
                   lambda i,s: Wt.at[i//per,pl.ds(pl.multiple_of(s*shard+(i%per)*grr,16),grr)],ng,glags,gss,grs,gls,1+nq)
        def done(k): return (k+1)*per-1+glags[2]+1
        Gg.a(0); Gq.tick(0); Gg.b(0); Gg.d(0); Gq.tick(1); Gg.e(0); st['q']=2
    else:
        pl.semaphore_wait(pltpu.get_barrier_semaphore(),line_count())
        wc=[cp(s_ref.at[k],Wt.at[k],gls.at[k]) for k in range(3)]+[cp(wq_ref,WQ,gls.at[3]),cp(ga_ref,GA,gls.at[4])]
        for c in wc: c.start()
        for c in wc: c.wait()
        def done(k): return 0
    def qg(upto):
        if gather:
            while st['q']<upto: Gq.tick(st['q']); st['q']+=1
    def ag(upto):
        if gather and upto>st['g']:
            lax.fori_loop(st['g'],upto,lambda T,_: (Gt.tick(T),0)[1],0); st['g']=upto
    S={'T':0,'base0':0,'hi0':0,'start':0,'base':0,'hi':0}
    def tick(T,s): C.tick(T,s['base0'],s['hi0'],s['start'],s['base'],s['hi'])
    def top(): return S['base']+S['hi']+L
    def ticks(until,every_g=0):
        s=dict(S); T0,g0=s['T'],st['g']; until=min(until,top())
        if until<=T0: return
        def body(T,_):
            tick(T,s)
            if every_g and gather:
                @pl.when((T-T0)%every_g==0)
                def _(): Gt.tick(g0+(T-T0)//every_g)
            return 0
        lax.fori_loop(T0,until,body,0)
        S['T']=until
        if every_g and gather: st['g']=g0+(until-T0+every_g-1)//every_g
    def finish(c,every_g=0):
        every_g=every_g*16//ch
        base=S['base'] if c>S['hi0'] else S['base0']
        ticks(base+c+L,every_g)
    def ready(c):
        if S['T']>S['base']+S['hi']:
            ticks(S['start']+L)
            S.update(base0=S['base'],hi0=S['hi'],start=S['T'],base=S['T']-S['hi'])
        S['hi']=c
    def units(n,fn,every=0,eg=0):
        s=dict(S); T0,g0=s['T'],st['g']; every=every*ch//16
        def body(i,_):
            fn(i)
            if every:
                @pl.when((i+1)%every==0)
                def _(): tick(T0+i//every,s)
            if eg and gather:
                @pl.when((i+1)%eg==0)
                def _(): Gt.tick(g0+i//eg)
            return 0
        lax.fori_loop(0,n,body,0)
        if eg and gather: st['g']=g0+n//eg
        if every: S['T']=min(T0+n//every,max(top(),T0))
    def wait_w(k):
        while gather and st['g']<done(k):
            ag(st['g']+1); ticks(S['T']+max(1,32//ch))
    nr=32; nn=half//nr
    def rch(i): return pl.ds(pl.multiple_of(i*nr,nr),nr)
    def gain(k): return GV[k:k+1,:]
    def norm0(h):
        def f(i):
            r=rch(i)
            v=XS[r,:].astype(F32)
            P[h,r,:]=(v*rsq(v)*gain(0)).astype(BF)
        return f
    def norm1(h):
        def f(i):
            r=rch(i)
            a=O[h,r,:].astype(F32)
            h1=XS[r,:].astype(F32)+a*rsq(a)*gain(1)
            BIG[pl.ds(pl.multiple_of(4*half+i*nr,nr),nr),:]=(h1*rsq(h1)*gain(2)).astype(BF)
        return f
    def normf(h):
        def f(i):
            r=rch(i)
            v=O[h,r,:].astype(F32); q=rsq(v); z=v*q
            s=XS[r,:].astype(F32)*gain(3)
            BIG[pl.ds(pl.multiple_of(4*half+i*nr,nr),nr),:]=(q*(s-z*jnp.mean(s*z,axis=-1,keepdims=True))).astype(BF)
        return f
    def qkv(h):
        def f(j):
            t=jnp.dot(P[h],BIG[pl.ds(0,W),pl.ds(pl.multiple_of(j*HS,HS),HS)],preferred_element_type=F32)
            return t
        cs=cos[rows(h),:]; sn=sin[rows(h),:]
        def rot(t):
            a,b=t[:,:HS//2],t[:,HS//2:]
            return jnp.concatenate([a*cs-b*sn,b*cs+a*sn],axis=1).astype(BF)
        for hd in range(nheads): BIG[pl.ds(hd*total+h*half,half),pl.ds(c0,HS)]=rot(f(hd))
        BIG[pl.ds(h*half,half),pl.ds(c1,HS)]=rot(f(nheads))
        BIG[pl.ds(total+h*half,half),pl.ds(c1,HS)]=f(nheads+1).astype(BF)
    qb=half//2
    def attend(h):
        nk=(h+1)*half; ks=pl.ds(0,nk)
        def f(i):
            hd=i%nheads; r0=h*half+(i//nheads)*qb
            rr=pl.ds(pl.multiple_of(r0,16),qb)
            q=BIG[pl.ds(pl.multiple_of(hd*total+r0,16),qb),pl.ds(c0,HS)]
            s=nt_dot(q,BIG[pl.ds(0,nk),pl.ds(c1,HS)])*(HS**-0.5)
            cc=50.0*jnp.tanh(s*(1.0/50.0))
            ri=r0+lax.broadcasted_iota(jnp.int32,(qb,nk),0); ci=lax.broadcasted_iota(jnp.int32,(qb,nk),1)
            vis=(ci<=ri)&(segc[rr,:]==segr[:,ks])
            cc=jnp.where(vis,cc,-jnp.inf)
            e=jnp.exp(cc-jnp.max(cc,axis=-1,keepdims=True))
            p=(e/jnp.sum(e,axis=-1,keepdims=True)).astype(BF)
            o=jnp.dot(p,BIG[pl.ds(total,nk),pl.ds(c1,HS)],preferred_element_type=F32).astype(BF)
            BIG[pl.ds(pl.multiple_of(2*total+r0,16),qb),pl.ds(pl.multiple_of(c0+hd*HS,128),HS)]=o
        return f
    def col(j): return pl.ds(pl.multiple_of(j*tn,tn),tn)
    def outp(h):
        def f(j): P[h,:,col(j)]=nt_dot(BIG[opart(h)],BIG[col(j),pl.ds(qw+2*HS,qw)]).astype(BF)
        return f
    def gate(h):
        def f(j): BIG[gu(0,h),col(j)]=jnp.dot(N2[...],Wt[0,:,col(j)],preferred_element_type=F32).astype(BF)
        return f
    def up(h):
        def f(j):
            u=jnp.dot(N2[...],Wt[1,:,col(j)],preferred_element_type=F32)
            g=BIG[gu(0,h),col(j)].astype(F32)
            act,_=gelu_parts(g)
            BIG[gu(1,h),col(j)]=u.astype(BF)
            BIG[hidr,col(j)]=(act*u).astype(BF)
        return f
    def down(h):
        def f(j): P[h,:,col(j)]=nt_dot(HID[...],Wt[2,col(j),:]).astype(BF)
        return f
    def bwd1(h):
        def f(j):
            d=jnp.dot(N2[...],Wt[2,:,col(j)],preferred_element_type=F32)
            g=BIG[gu(0,h),col(j)].astype(F32); u=BIG[gu(1,h),col(j)].astype(F32)
            act,der=gelu_parts(g)
            BIG[gu(0,h),col(j)]=(d*u*der).astype(BF)
            BIG[gu(1,h),col(j)]=(d*act).astype(BF)
        return f
    def bwd2(h):
        def f(j):
            P[h,:,col(j)]=(nt_dot(BIG[gu(0,h),:],Wt[0,col(j),:])+nt_dot(BIG[gu(1,h),:],Wt[1,col(j),:])).astype(BF)
        return f
    GV[...]=jnp.transpose(GA[...].astype(F32))[:8,:]
    xin(x_ref,0).wait()
    units(nn,norm0(0))
    xin(x_ref,1).start()
    out('g',GV,g_out,7)
    out('n1a',P.at[0],n1_out.at[rows(0)],4)
    qg(nq)
    ag(1)
    xin(x_ref,1).wait()
    units(nn,norm0(1))
    xin(x_ref,0).start()
    out('n1b',P.at[1],n1_out.at[rows(1)],5)
    qg(nq+3)
    ag(2)
    out('w',WQ,w_out,6)
    qkv(0)
    ag(3)
    qkv(1)
    out('q0',BIG.at[qpart(0)],q_out.at[0],0)
    if nheads>1: out('q1',BIG.at[qpart(1)],q_out.at[1],1)
    out('k',BIG.at[kpart],k_out,2)
    out('v',BIG.at[vpart],v_out,3)
    ag(4)
    fin('n1a'); fin('n1b')
    units(2*nheads,attend(0),eg=4)
    units(nd,outp(0))
    ready(nt)
    units(2*nheads,attend(1),1,eg=4)
    units(nd,outp(1),3)
    ready(2*nt)
    out('o0',BIG.at[opart(0)],o_out.at[rows(0)],8)
    out('o1',BIG.at[opart(1)],o_out.at[rows(1)],9)
    finish(nt,2)
    out('at0',O.at[0],at_out.at[rows(0)],10)
    xin(x_ref,0).wait()
    for k in ('q0','q1','k','v','o0','o1','w','g'):
        if k in oc: fin(k)
    units(nn,norm1(0),7)
    xin(x_ref,1).start()
    out('n2',N2,n2_out.at[rows(0)],0)
    wait_w(0)
    units(nj,gate(0),3)
    wait_w(1)
    units(nj,up(0),4)
    out('hid',HID,hid_out.at[rows(0)],1)
    wait_w(2)
    fin('at0')
    units(nd,down(0),3)
    ready(3*nt)
    finish(2*nt)
    out('at1',O.at[1],at_out.at[rows(1)],11)
    xin(x_ref,1).wait()
    fin('n2')
    units(nn,norm1(1),7)
    xin(dy_ref,0).start()
    out('n2',N2,n2_out.at[rows(1)],0)
    units(nj,gate(1),3)
    fin('hid')
    units(nj,up(1),4)
    out('hid',HID,hid_out.at[rows(1)],1)
    fin('at1')
    units(nd,down(1),3)
    ready(4*nt)
    finish(3*nt)
    out('f0',O.at[0],f_out.at[rows(0)],10)
    xin(dy_ref,0).wait()
    fin('n2')
    units(nn,normf(0),7)
    xin(dy_ref,1).start()
    out('df',N2,df_out.at[rows(0)],0)
    units(nj,bwd1(0),3)
    out('dg0',BIG.at[gu(0,0)],dg_out.at[rows(0)],2); out('du0',BIG.at[gu(1,0)],du_out.at[rows(0)],3)
    fin('f0')
    units(nd,bwd2(0),2)
    ready(5*nt)
    finish(4*nt)
    out('f1',O.at[1],f_out.at[rows(1)],11)
    xin(dy_ref,1).wait()
    fin('df')
    units(nn,normf(1),7)
    out('df',N2,df_out.at[rows(1)],0)
    units(nj,bwd1(1),3)
    out('dg1',BIG.at[gu(0,1)],dg_out.at[rows(1)],4); out('du1',BIG.at[gu(1,1)],du_out.at[rows(1)],5)
    fin('f1'); fin('df'); fin('hid')
    n2f=pl.ds(2*total,total); dff=pl.ds(0,total); hidf=pl.ds(total,total)
    back=[cp(n2_out,BIG.at[n2f],isem.at[1]),cp(df_out,Wt.at[2,dff],isem.at[2]),cp(hid_out,Wt.at[2,hidf],isem.at[3])]
    for c in back: c.start()
    units(nd,bwd2(1),2)
    ready(6*nt)
    for c in back: c.wait()
    def wgrad(lhs,rhs,k):
        def f(j):
            lt=lhs(col(j))
            for n in range(0,ff,768):
                t=lax.dot_general(lt,rhs(pl.ds(n,768)),(((0,),(0,)),((),())),preferred_element_type=F32)
                Wt[k,col(j),pl.ds(n,768)]=t.astype(BF)
        return f
    units(nd,wgrad(lambda c: Wt[2,dff,c],lambda c: Wt[2,hidf,c],0),1)
    out('gd',Wt.at[0],gm_out.at[2],6)
    units(nd,wgrad(lambda c: BIG[n2f,c],lambda c: BIG[pl.ds(0,total),c],1),1)
    out('gg',Wt.at[1],gm_out.at[0],7)
    finish(5*nt)
    out('d0',O.at[0],d_out.at[rows(0)],10)
    units(nd,wgrad(lambda c: BIG[n2f,c],lambda c: BIG[pl.ds(total,total),c],2),1)
    out('gu',Wt.at[2],gm_out.at[1],8)
    finish(6*nt)
    out('d1',O.at[1],d_out.at[rows(1)],11)
    for k in list(oc): fin(k)

def line_signal():
    te=lax.axis_index("tensor")
    bar=pltpu.get_barrier_semaphore()
    @pl.when(te<3)
    def _(): pl.semaphore_signal(bar, inc=1, device_id={"tensor":te+1}, device_id_type=MESH)
    @pl.when(te>0)
    def _(): pl.semaphore_signal(bar, inc=1, device_id={"tensor":te-1}, device_id_type=MESH)
def line_count():
    te=lax.axis_index("tensor")
    return (te<3).astype(jnp.int32)+(te>0).astype(jnp.int32)

def forward_both(x,dy,cos,sin,seg,qkvo,gains,shards,nheads,gather,cid=9,ch=32,lags=(2,3,4,5),grr=48,qrr=48,glags=(3,4,6),tn=256):
    total=x.shape[0]; half=total//2; D=pltpu.SemaphoreType.DMA; ff=shards.shape[2]; w3=qkvo.shape[1]
    ng=(1+qkvo.shape[0]//qrr+shards.shape[0]*shards.shape[1]//grr) if gather else 5
    sds=jax.ShapeDtypeStruct
    act=sds((total,W),BF); wide=sds((total,ff),BF); hd=sds((total,256),BF)
    A=pl.BlockSpec(memory_space=pl.ANY); V=pl.BlockSpec(memory_space=pltpu.VMEM)
    return pl.pallas_call(functools.partial(f_kernel,gather,half,ch,lags,grr,qrr,glags,tn,nheads),
        out_shape=[act,act,act,act,wide,wide,wide,act,act,sds((nheads,total,256),BF),hd,hd,sds((total,nheads*256),BF),sds((W,w3),BF),sds((8,W),F32)]+[sds((3,W,ff),BF)],
        in_specs=[A,A,V,V,V,V,A,A,A],out_specs=[A]*16,
        scratch_shapes=[pltpu.VMEM((3,W,ff),BF),pltpu.VMEM((6*half,W),BF),pltpu.VMEM((half,W),BF),pltpu.VMEM((8,W),F32)]
            +chain_scratch(half,ch)+gather_sems(ng)+[D((4,)),D((12,))],
        compiler_params=pltpu.CompilerParams(collective_id=cid,has_side_effects=True,vmem_limit_bytes=64*2**20))(
            x,dy,cos,sin,seg.reshape(-1,1),seg.reshape(1,-1),qkvo,gains,shards)
class Ring:
    def __init__(self,src,dst,base,n,rr,cols,bufs,ss,rs,ls,lags=(1,3,5)):
        self.src,self.dst,self.base,self.n,self.rr,self.cols=src,dst,base,n,rr,cols
        self.lags=lags
        self.LB,self.OB,self.CB,self.DB,self.XB,self.YB=bufs
        self.ss,self.rs,self.ls=ss,rs,ls; self.pl=Plane()
    def at(self,ref,*idx): return ref.at[(*idx,pl.ds(0,self.rr),pl.ds(0,self.cols))]
    def get(self,i):
        s=i%self.LB.shape[0]; c=i%self.CB.shape[0]; d=i%self.DB.shape[0]; o=i%2
        lb=lambda j: self.at(self.LB,s,j)
        cb=lambda j: self.at(self.CB,c,j)
        return (lambda k: self.src(i-self.base,k)),lb,cb,self.at(self.DB,d),self.at(self.XB,d),self.at(self.YB,d),self.at(self.OB,o)
    def p1(self,i):
        g,lb,cb,db,xb,yb,ob=self.get(i); q=self.pl
        for j in (3,1,2,0):
            remote(g(q.other[j]),cb(j),self.ss.at[i,j],self.rs.at[i,j],q.toC).start()
            pltpu.make_async_copy(g(q.lane[j]),lb(j),self.ls.at[i,j]).start()
    def p2(self,i):
        g,lb,cb,db,xb,yb,ob=self.get(i); q=self.pl
        for j in (3,1,2,0):
            pltpu.make_async_copy(g(q.lane[j]),lb(j),self.ls.at[i,j]).wait()
            remote(g(q.other[j]),cb(j),self.ss.at[i,j],self.rs.at[i,j],q.toC).wait_recv()
            lb(j)[...]=lb(j)[...]+cb(j)[...]
            if j==3:
                @pl.when(q.is0)
                def _(): remote(lb(3),db,self.ss.at[i,4],self.rs.at[i,4],q.toX).start()
                @pl.when(q.is1)
                def _(): remote(lb(3),db,self.ss.at[i,4],self.rs.at[i,4],q.toY).start()
            if j==1:
                @pl.when(q.is0)
                def _(): remote(lb(1),xb,self.ss.at[i,5],self.rs.at[i,5],q.toX).start()
            if j==2:
                @pl.when(q.is1)
                def _(): remote(lb(2),yb,self.ss.at[i,5],self.rs.at[i,6],q.toY).start()
    def p3(self,i):
        g,lb,cb,db,xb,yb,ob=self.get(i); q=self.pl
        remote(lb(3),db,self.ss.at[i,4],self.rs.at[i,4],q.toX).wait_recv()
        def relay(j,buf,sem,dev):
            lb(j)[...]=lb(j)[...]+db[...]
            remote(lb(j),buf,self.ss.at[i,6],self.rs.at[i,sem],dev).start()
        @pl.when(q.is0)
        def _(): relay(2,yb,6,q.toY)
        @pl.when(q.is1)
        def _(): relay(1,xb,5,q.toX)
    def p4(self,i):
        g,lb,cb,db,xb,yb,ob=self.get(i); q=self.pl
        remote(lb(0),xb,self.ss.at[i,5],self.rs.at[i,5],q.toX).wait_recv()
        remote(lb(0),yb,self.ss.at[i,5],self.rs.at[i,6],q.toY).wait_recv()
        ob[...]=(lb(0)[...].astype(F32)+xb[...].astype(F32)+yb[...].astype(F32)).astype(BF)
        pltpu.make_async_copy(ob,self.dst(i-self.base),self.ls.at[i,4]).start()
        for j in range(7):
            remote(lb(0),xb,self.ss.at[i,j],self.rs.at[i,0],q.toX).wait_send()
    def p5(self,i):
        g,lb,cb,db,xb,yb,ob=self.get(i)
        pltpu.make_async_copy(ob,self.dst(i-self.base),self.ls.at[i,4]).wait()
    def tick(self,T):
        l2,l3,l4=self.lags
        for lag,f in ((0,self.p1),(l2,self.p2),(l3,self.p3),(l4+1,self.p5),(l4,self.p4)):
            i=T-lag
            @pl.when((i>=self.base)&(i<self.base+self.n))
            def _(): f(i)

def b_kernel(scatter,half,ch,lags,rr,tn,nheads,rlags,*refs):
    (at_ref,x_ref,dy_ref,dn_ref,n1_ref,w_ref,q_ref,k_ref,v_ref,o_ref,gv,cos,sin,segc,segr,gm_ref,
     g_out,acc_out,rm_out,rq_out,
     WQ,N1,X2,X3,Q,K,V,OO,DO,DQ,DK,DV,ACC,LB,OB,CB,DB,XB,YB,ss,rs,ls,
     P,RE,RM,O,sp,so,ve,vm,vo,isem,osem)=refs
    C=Chain(half,ch,P,RE,RM,O,sp,so,ve,vm,vo,lags)
    L=lags[-1]; nt=C.nt; total=2*half; HS=256; qw=nheads*HS; wide=qw+2*HS; nd=W//tn
    def cp(src,dst,i): return pltpu.make_async_copy(src,dst,isem.at[i])
    def rows(h): return pl.ds(h*half,half)
    first=[cp(at_ref.at[rows(1)],P.at[0],0),cp(x_ref.at[rows(1)],N1.at[rows(1)],2),cp(dy_ref.at[rows(1)],X2.at[rows(1)],3),cp(dn_ref.at[rows(1)],X3.at[rows(1)],4)]
    second=[cp(at_ref.at[rows(0)],P.at[1],1),cp(x_ref.at[rows(0)],N1.at[rows(0)],10),cp(dy_ref.at[rows(0)],X2.at[rows(0)],11),cp(dn_ref.at[rows(0)],X3.at[rows(0)],12)]
    later=[cp(w_ref,WQ,5),cp(q_ref,Q,6),cp(k_ref,K,7),cp(v_ref,V,8),cp(o_ref,OO,9)]
    for c in first+later+second: c.start()
    line_signal(); st={'r':0}
    if scatter:
        plane_signal()
        pl.semaphore_wait(pltpu.get_barrier_semaphore(),line_count()+3)
        bufs=(LB,OB,CB,DB,XB,YB); shard=W//8; per=shard//rr; nm=3*per; nq=per
        def gi(k,r): return pl.ds(pl.multiple_of(k*shard+r*rr,16),rr)
        R1=Ring(lambda i,k: gm_ref.at[i//per,gi(k,i%per)],lambda i: rm_out.at[i//per,pl.ds(pl.multiple_of((i%per)*rr,16),rr)],0,nm,rr,W,bufs,ss,rs,ls,rlags)
        R2=Ring(lambda i,k: WQ.at[gi(k,i)],lambda i: rq_out.at[pl.ds(pl.multiple_of(i*rr,16),rr)],nm,nq,rr,wide+qw,bufs,ss,rs,ls,rlags)
    else:
        pl.semaphore_wait(pltpu.get_barrier_semaphore(),line_count())
    def rg(n):
        for _ in range(n):
            if scatter: R1.tick(st['r'])
            st['r']+=1
    S={'T':0,'base0':0,'hi0':0,'start':0,'base':0,'hi':0}
    def tick(T,s): C.tick(T,s['base0'],s['hi0'],s['start'],s['base'],s['hi'])
    def top(): return S['base']+S['hi']+L
    def ready(c):
        if S['T']>S['base']+S['hi']:
            loop(S['start']+L-S['T'],1)
            S.update(base0=S['base'],hi0=S['hi'],start=S['T'],base=S['T']-S['hi'])
        S['hi']=c
    def units(n,fn,every=0,er=0):
        s=dict(S); T0,r0=s['T'],st['r']; every=every*ch//16; er=er*rr//48
        def body(i,_):
            fn(i)
            if every:
                @pl.when((i+1)%every==0)
                def _(): tick(T0+i//every,s)
            if er and scatter:
                @pl.when((i+1)%er==0)
                def _(): R1.tick(r0+i//er)
            return 0
        lax.fori_loop(0,n,body,0)
        if er: st['r']=r0+n//er
        if every: S['T']=min(T0+n//every,max(top(),T0))
    def loop(n,every,er=0,both=False):
        s=dict(S); T0=s['T']
        if n>0: lax.fori_loop(T0,T0+n,lambda t,_: (tick(t,s),0)[1],0); S['T']=T0+n
    rg(2 if rr==48 else 1)
    for c in first: c.wait()
    nr=16; nh=half//nr
    ACC[...]=jnp.zeros_like(ACC)
    def back(h):
        def f(i):
            r=pl.ds(pl.multiple_of(i*nr,nr),nr); rf=pl.ds(pl.multiple_of(h*half+i*nr,nr),nr)
            a=P[1-h,r,:].astype(F32); q1=rsq(a); z2=a*q1
            h1=N1[rf,:].astype(F32)+z2*gv[1:2,:]; q2=rsq(h1); z3=h1*q2
            d=X3[rf,:].astype(F32); s=d*gv[2:3,:]
            dh=X2[rf,:].astype(F32)+q2*(s-z3*jnp.mean(s*z3,axis=-1,keepdims=True))
            s2=dh*gv[1:2,:]
            X2[rf,:]=(q1*(s2-z2*jnp.mean(s2*z2,axis=-1,keepdims=True))).astype(BF)
            X3[rf,:]=dh.astype(BF)
            u=dh*z2; w=d*z3
            ACC[0]+=u[:8]+u[8:]; ACC[1]+=w[:8]+w[8:]
        return f
    def col(j): return pl.ds(pl.multiple_of(j*tn,tn),tn)
    def tn_dot(a,b): return lax.dot_general(a,b,(((0,),(0,)),((),())),preferred_element_type=F32)
    def dout(h):
        for c in range(nheads):
            DO[rows(h),pl.ds(c*HS,HS)]=jnp.dot(X2[rows(h),:],WQ[:,pl.ds(wide+c*HS,HS)],preferred_element_type=F32).astype(BF)
    def gout(j): WQ[col(j),pl.ds(wide,qw)]=tn_dot(X2[:,col(j)],OO[...]).astype(BF)
    qb=half//2; sc=HS**-0.5
    def unrot(t,rr_):
        a,b=t[:,:HS//2],t[:,HS//2:]; cs=cos[rr_,:]; sn=sin[rr_,:]
        return jnp.concatenate([a*cs+b*sn,b*cs-a*sn],axis=1)
    def attend(h):
        nk=(h+1)*half; ks=pl.ds(0,nk)
        def f(i):
            hd=i%nheads; r0=h*half+(i//nheads)*qb; rq=pl.ds(pl.multiple_of(r0,16),qb); hc_=pl.ds(pl.multiple_of(hd*HS,HS),HS)
            q=Q[hd,rq,:]; do=DO[rq,hc_]
            t=jnp.tanh(nt_dot(q,K[ks,:])*(sc/50.0))
            ri=r0+lax.broadcasted_iota(jnp.int32,(qb,nk),0); ci=lax.broadcasted_iota(jnp.int32,(qb,nk),1)
            vis=(ci<=ri)&(segc[rq,:]==segr[:,ks])
            cc=jnp.where(vis,50.0*t,-jnp.inf)
            e=jnp.exp(cc-jnp.max(cc,axis=-1,keepdims=True))
            p=e/jnp.sum(e,axis=-1,keepdims=True)
            dp=nt_dot(do,V[ks,:])
            inner=jnp.sum(p*dp,axis=-1,keepdims=True)
            ds=(p*(dp-inner)*(1.0-t*t)).astype(BF)
            DQ[rq,hc_]=unrot(jnp.dot(ds,K[ks,:],preferred_element_type=F32)*sc,rq).astype(BF)
            DK[ks,:]+=tn_dot(ds,q)
            DV[ks,:]+=tn_dot(p.astype(BF),do)
        return f
    def keys(h):
        DQ[rows(h),pl.ds(qw,HS)]=unrot(DK[rows(h),:]*sc,rows(h)).astype(BF)
        DQ[rows(h),pl.ds(qw+HS,HS)]=DV[rows(h),:].astype(BF)
    def dn1(h):
        def f(j): P[1-h,:,col(j)]=nt_dot(DQ[rows(h),:],WQ[col(j),pl.ds(0,wide)]).astype(BF)
        return f
    def gqkv(j): WQ[col(j),pl.ds(0,wide)]=tn_dot(N1[:,col(j)],DQ[...]).astype(BF)
    DK[...]=jnp.zeros_like(DK); DV[...]=jnp.zeros_like(DV)
    units(nh,back(1),0,28)
    for c in later: c.wait()
    dout(1)
    units(2*nheads,attend(1),0,2)
    keys(1)
    units(nd,dn1(1),0,9)
    for c in second: c.wait()
    ready(nt)
    units(nh,back(0),7,14)
    n1c=cp(n1_ref,N1,2); n1c.start()
    dout(0)
    units(nd,gout,3,9)
    units(2*nheads,attend(0),1,2)
    keys(0)
    units(nd,dn1(0),3)
    ready(2*nt)
    n1c.wait()
    units(nd,gqkv,1,2)
    xc=cp(x_ref,N1,2); xc.start()
    nz=total//nr
    def last_norm(c):
        h=c//nh; r=pl.ds(pl.multiple_of((c%nh)*nr,nr),nr); rf=pl.ds(pl.multiple_of(c*nr,nr),nr)
        v=N1[rf,:].astype(F32); q0=rsq(v); z=v*q0
        d=O[1-h,r,:].astype(F32); e=d*gv[0:1,:]
        X3[rf,:]=(X3[rf,:].astype(F32)+q0*(e-z*jnp.mean(e*z,axis=-1,keepdims=True))).astype(BF)
        u=d*z
        ACC[2]+=u[:8]+u[8:]
    rest=top()-S['T']
    if scatter:
        q=max(1,2*16*rr//(48*ch)); s=dict(S); T0=S['T']; r0=st['r']
        R2.base=max(nm,r0); last=R2.base+nq+R1.lags[2]+1
        k1=max(0,min(-(-rest//q),R2.base-r0)); k2=max(0,-(-(rest-q*k1)//q))
        def both(two):
            def body(i,_):
                R1.tick(r0+i)
                if two: R2.tick(r0+i)
                for z in range(q): tick(T0+q*i+z,s)
                return 0
            return body
        if k1: lax.fori_loop(0,k1,both(False),0)
        if k2: lax.fori_loop(k1,k1+k2,both(True),0)
        r0+=k1+k2
        xc.wait()
        n3=last-r0; each=-(-nz//max(n3,1))
        def body3(i,_):
            R1.tick(r0+i); R2.tick(r0+i)
            lax.fori_loop(jnp.minimum(i*each,nz),jnp.minimum((i+1)*each,nz),lambda c,_: (last_norm(c),0)[1],0)
            return 0
        lax.fori_loop(0,n3,body3,0)
        if n3<=0: lax.fori_loop(0,nz,lambda c,_: (last_norm(c),0)[1],0)
    else:
        loop(rest,1)
        xc.wait()
        lax.fori_loop(0,nz,lambda c,_: (last_norm(c),0)[1],0)
        wc=cp(WQ,rq_out,5); wc.start(); wc.wait()
    outs=[cp(X3,g_out,3),cp(ACC,acc_out,4)]
    for c in outs: c.start()
    for c in outs: c.wait()

def backward_both(at,x,dy,dn,n1,w,q,k,v,o,gv,cos,sin,seg,gm,scatter,cid=10,ch=32,lags=(2,3,4,5),rr=48,tn=256,ring=(6,6,14),rlags=(1,3,5)):
    total=x.shape[0]; half=total//2; D=pltpu.SemaphoreType.DMA; sds=jax.ShapeDtypeStruct; nheads=q.shape[0]
    A=pl.BlockSpec(memory_space=pl.ANY); V=pl.BlockSpec(memory_space=pltpu.VMEM); M=pltpu.VMEM
    qw=nheads*256; wide=qw+512; w3=w.shape[1]; act=sds((total,W),BF)
    if scatter: outs=[sds((3,W//8,W),BF),sds((W//8,w3),BF)]; nu=4*(W//8//rr)+8
    else: outs=[sds((8,128),BF),sds((W,w3),BF)]; nu=1; ring=(1,1,1); rr=16
    nl,nc,nx=ring
    return pl.pallas_call(functools.partial(b_kernel,scatter,half,ch,lags,rr,tn,nheads,rlags),
        out_shape=[act,sds((3,8,W),F32)]+outs,
        in_specs=[A]*10+[V]*5+[A],out_specs=[A]*4,
        scratch_shapes=[M((W,w3),BF),M((total,W),BF),M((total,W),BF),M((total,W),BF),M((nheads,total,256),BF),M((total,256),BF),M((total,256),BF),
            M((total,qw),BF),M((total,qw),BF),M((total,wide),BF),M((total,256),F32),M((total,256),F32),M((3,8,W),F32),
            M((nl,4,rr,W),BF),M((2,rr,W),BF),M((nc,4,rr,W),BF),M((nx,rr,W),BF),M((nx,rr,W),BF),M((nx,rr,W),BF),D((nu,7)),D((nu,7)),D((nu,5))]
            +chain_scratch(half,ch)+[D((13,)),D((2,))],
        compiler_params=pltpu.CompilerParams(collective_id=cid,has_side_effects=True,vmem_limit_bytes=64*2**20))(
            at,x,dy,dn,n1,w,q,k,v,o,gv,cos,sin,seg.reshape(-1,1),seg.reshape(1,-1),gm)

def small_plane():
    return (lax.axis_size("dp"), lax.axis_size("zero")) == (4, 2)


def sum_own_columns(part):
    if not small_plane():
        low = part.astype(jnp.bfloat16)
        return lax.psum_scatter(low, ("dp", "zero"), scatter_dimension=1, tiled=True)
    for axis, pairs in (
        ("dp", [(0, 1), (1, 0), (2, 3), (3, 2)]),
        ("dp", [(0, 2), (2, 0), (1, 3), (3, 1)]),
        ("zero", [(0, 1), (1, 0)]),
    ):
        part = part + lax.ppermute(part, axis, pairs)
    own = lax.axis_index("dp") * 2 + lax.axis_index("zero")
    width = part.shape[1] // 8
    return lax.dynamic_slice_in_dim(part, own * width, width, axis=1)


def per_device(
    inputs,
    cotangent,
    segment,
    query_weight,
    key_weight,
    value_weight,
    out_weight,
    gate_weight,
    up_weight,
    down_weight,
    norm_gains,
    query_mean,
    key_mean,
    value_mean,
    out_mean,
    gate_mean,
    up_mean,
    down_mean,
    gains_mean,
    query_square,
    key_square,
    value_square,
    out_square,
    gate_square,
    up_square,
    down_square,
    gains_square,
):
    qkvo_low = jnp.concatenate(
        [query_weight, key_weight, value_weight, out_weight.T], axis=1
    ).astype(jnp.bfloat16)
    mlp_shards = jnp.stack([gate_weight, up_weight, down_weight.T]).astype(jnp.bfloat16)
    gains_low = jnp.pad(norm_gains.T.astype(jnp.bfloat16), ((0, 0), (0, 124)))
    if not small_plane():
        both = ("dp", "zero")
        qkvo_low = lax.all_gather(qkvo_low, both, axis=0, tiled=True)
        gains_low = lax.all_gather(gains_low, both, axis=0, tiled=True)
        mlp_shards = lax.all_gather(mlp_shards, both, axis=1, tiled=True)
    heads_q = query_weight.shape[1]
    heads_k = key_weight.shape[1]
    wide = heads_q + 2 * heads_k
    token_rows = inputs.shape[0]
    cosine, sine = rope_tables(segment)
    (
        attn_total,
        mlp_total,
        normed_grad,
        unused_mlp_in,
        unused_hidden,
        unused_gate_dlow,
        unused_up_dlow,
        unused_mlp_low,
        attn_in,
        rotated_queries,
        rotated_keys,
        value_low,
        attention_output,
        qkvo_mat,
        gains_val,
        mlp_grads,
    ) = forward_both(
        inputs,
        cotangent,
        cosine[:, 0],
        sine[:, 0],
        segment,
        qkvo_low,
        gains_low,
        mlp_shards,
        heads_q // HEAD_SIZE,
        small_plane(),
    )
    input_grad, sums, mlp_red, qkvo_red = backward_both(
        attn_total,
        inputs,
        cotangent,
        normed_grad,
        attn_in,
        qkvo_mat,
        rotated_queries,
        rotated_keys,
        value_low,
        attention_output,
        gains_val,
        cosine[:, 0],
        sine[:, 0],
        segment,
        mlp_grads,
        small_plane(),
    )
    if not small_plane():
        mlp_red = lax.psum_scatter(mlp_grads, both, scatter_dimension=1, tiled=True)
        qkvo_red = lax.psum_scatter(qkvo_red, both, scatter_dimension=0, tiled=True)
    resid_in = inputs.astype(jnp.float32)
    out_grad = cotangent.astype(jnp.float32)
    post_attn, unused, unused = rms_forward(attn_total.astype(jnp.float32), gains_val[1])
    post_mlp, unit_four, unused = rms_forward(mlp_total.astype(jnp.float32), gains_val[3])
    block_out = (resid_in + post_attn + post_mlp).astype(jnp.bfloat16)
    gain_four = jnp.sum(out_grad * unit_four, axis=0)
    gain_two, gain_three, gain_one = jnp.sum(sums, axis=1)
    input_grad = input_grad.astype(jnp.float32)
    gains_grad = jnp.stack([gain_one, gain_two, gain_three, gain_four])
    gains_red = sum_own_columns(gains_grad)
    down_red, out_red = lax.optimization_barrier((mlp_red[2].T, qkvo_red[:, wide:].T))
    reduced = [
        part.astype(jnp.float32)
        for part in (
            qkvo_red[:, :heads_q],
            qkvo_red[:, heads_q : heads_q + heads_k],
            qkvo_red[:, heads_q + heads_k : wide],
            out_red,
            mlp_red[0],
            mlp_red[1],
            down_red,
            gains_red,
        )
    ]
    masters = (
        query_weight,
        key_weight,
        value_weight,
        out_weight,
        gate_weight,
        up_weight,
        down_weight,
        norm_gains,
    )
    means = (query_mean, key_mean, value_mean, out_mean, gate_mean, up_mean, down_mean, gains_mean)
    squares = (
        query_square,
        key_square,
        value_square,
        out_square,
        gate_square,
        up_square,
        down_square,
        gains_square,
    )
    rates = (
        MODEL_WIDTH ** (-0.5),
        MODEL_WIDTH ** (-0.5),
        MODEL_WIDTH ** (-0.5),
        (QUERY_HEADS * HEAD_SIZE) ** (-0.5),
        MODEL_WIDTH ** (-0.5),
        MODEL_WIDTH ** (-0.5),
        FF ** (-0.5),
        gain_rate,
    )
    decays = (weight_decay,) * 7 + (0.0,)
    moments = []
    seconds = []
    updated = []
    for index in range(8):
        moment, second, master = adam_update(
            masters[index],
            means[index],
            squares[index],
            reduced[index],
            rates[index],
            decays[index],
        )
        moments.append(moment)
        seconds.append(second)
        updated.append(master)
    return (block_out, input_grad, *moments, *seconds, *updated)


def solution(mesh):
    in_specs = (
        P(("dp", "zero"), None),
        P(("dp", "zero"), None),
        P(("dp", "zero")),
        P(("dp", "zero"), "tensor"),
        P(("dp", "zero"), "tensor"),
        P(("dp", "zero"), "tensor"),
        P("tensor", ("dp", "zero")),
        P(("dp", "zero"), "tensor"),
        P(("dp", "zero"), "tensor"),
        P("tensor", ("dp", "zero")),
        P(None, ("dp", "zero")),
        P(("dp", "zero"), "tensor"),
        P(("dp", "zero"), "tensor"),
        P(("dp", "zero"), "tensor"),
        P("tensor", ("dp", "zero")),
        P(("dp", "zero"), "tensor"),
        P(("dp", "zero"), "tensor"),
        P("tensor", ("dp", "zero")),
        P(None, ("dp", "zero")),
        P(("dp", "zero"), "tensor"),
        P(("dp", "zero"), "tensor"),
        P(("dp", "zero"), "tensor"),
        P("tensor", ("dp", "zero")),
        P(("dp", "zero"), "tensor"),
        P(("dp", "zero"), "tensor"),
        P("tensor", ("dp", "zero")),
        P(None, ("dp", "zero")),
    )
    out_specs = (
        P(("dp", "zero"), None),
        P(("dp", "zero"), None),
        P(("dp", "zero"), "tensor"),
        P(("dp", "zero"), "tensor"),
        P(("dp", "zero"), "tensor"),
        P("tensor", ("dp", "zero")),
        P(("dp", "zero"), "tensor"),
        P(("dp", "zero"), "tensor"),
        P("tensor", ("dp", "zero")),
        P(None, ("dp", "zero")),
        P(("dp", "zero"), "tensor"),
        P(("dp", "zero"), "tensor"),
        P(("dp", "zero"), "tensor"),
        P("tensor", ("dp", "zero")),
        P(("dp", "zero"), "tensor"),
        P(("dp", "zero"), "tensor"),
        P("tensor", ("dp", "zero")),
        P(None, ("dp", "zero")),
        P(("dp", "zero"), "tensor"),
        P(("dp", "zero"), "tensor"),
        P(("dp", "zero"), "tensor"),
        P("tensor", ("dp", "zero")),
        P(("dp", "zero"), "tensor"),
        P(("dp", "zero"), "tensor"),
        P("tensor", ("dp", "zero")),
        P(None, ("dp", "zero")),
    )
    return jax.shard_map(
        per_device, mesh=mesh, in_specs=in_specs, out_specs=out_specs, check_vma=False
    )
```
